128 devices in a mesh: dp: 64 (over x, y_hi, z, core), tensor: 2 (over y_lo).
Axes of the slice: x: 4, y: 4 (y_hi: 2, y_lo: 2; y = y_hi * 2 + y_lo), z: 4, core: 2. Of those that a mesh axis runs over, the one named last changes fastest.
Arguments:
- tokens: bfloat16 [16384, 1024], P('dp'), may hold values from -16 to 16
- segments: int32 [64, 256], P('dp'), may hold values from 0 to 3, never falling along the last dimension, each value on 1 to 128 neighbouring positions
- routes: int32 [2, 16384, 2], P(None, 'dp'), may hold values from 0 to 3, all different within a row
- norm_attention: bfloat16 [2, 1024], replicated, may hold values from 0.099609375 to 1.8984375
- query_weight: bfloat16 [2, 1024, 1024], P(None, None, 'tensor'), may hold values from -0.1875 to 0.1875
- key_matrix: bfloat16 [2, 1024, 512], P(None, None, 'tensor'), may hold values from -0.1875 to 0.1875
- value_matrix: bfloat16 [2, 1024, 512], P(None, None, 'tensor'), may hold values from -0.1875 to 0.1875
- output_weight: bfloat16 [2, 1024, 1024], P(None, 'tensor'), may hold values from -0.75 to 0.75
- norm_experts: bfloat16 [2, 1024], replicated, may hold values from 0.099609375 to 1.8984375
- router_weight: bfloat16 [2, 1024, 4], replicated, may hold values from -0.109375 to 0.109375
- gate_weight: bfloat16 [2, 4, 1024, 512], P(None, None, None, 'tensor'), may hold values from -0.1875 to 0.1875
- up_weight: bfloat16 [2, 4, 1024, 512], P(None, None, None, 'tensor'), may hold values from -0.1875 to 0.1875
- down_weight: bfloat16 [2, 4, 512, 1024], P(None, None, 'tensor'), may hold values from -0.375 to 0.375
- cotangent: bfloat16 [16384, 1024], P('dp'), may hold values from -16 to 16
Outputs:
- output: bfloat16 [16384, 1024], P('dp')
- input_gradient: float32 [16384, 1024], P('dp')
- attention_gain_gradient: float32 [2, 1024], P(None, 'dp')
- query_gradient: float32 [2, 1024, 1024], P(None, 'dp', 'tensor')
- key_gradient: float32 [2, 1024, 512], P(None, 'dp', 'tensor')
- value_gradient: float32 [2, 1024, 512], P(None, 'dp', 'tensor')
- projection_gradient: float32 [2, 1024, 1024], P(None, 'tensor', 'dp')
- expert_gain_gradient: float32 [2, 1024], P(None, 'dp')
- router_gradient: float32 [2, 1024, 4], P(None, 'dp')
- gate_gradient: float32 [2, 4, 1024, 512], P(None, None, 'dp', 'tensor')
- up_gradient: float32 [2, 4, 1024, 512], P(None, None, 'dp', 'tensor')
- down_gradient: float32 [2, 4, 512, 1024], P(None, None, 'tensor', 'dp')
The draws below stay inside these ranges and needn't reach their ends.
Inputs may be any that keep to these rules, and one draw needn't show every extreme that they name: `routes`: in each layer every token names 2 different experts. `segments`: numbers never fall along a sequence; a document has at most half of 256 tokens.
All inputs are finite; a program needn't handle non-finite values.
Results may differ from the reference program's by a relative error of at most 0.022.
The reference program's roundings to bfloat16 on the way count: a program that leaves them out, or rounds other values in their place, can miss the bound.
Values sent between devices are 32-bit elements; how exact they have to be, the bound alone decides.
No kernel may reach another device: no remote copies, remote signals or barrier semaphores. Data moves between devices by JAX's collectives and lax.ppermute only.
A program may use at most 256 MiB of HBM per device.

```python
import math
import jax
import jax.numpy as jnp
import numpy as np
from jax import lax

MODEL_WIDTH = 1024
QUERY_HEADS = 16
KV_HEAD_COUNT = 8
HEAD_SIZE = 64
FF_EXP = 512
EXPERTS = 4
TOPK = 2
LAYER_COUNT = 2
TOK_DEV = 256
SEQS = 64
TOKENS = 16384


def spiked(values, key, source, target, parts, factor):
    def block_of(dim):
        return (jnp.arange(values.shape[dim]) // (values.shape[dim] // parts)).reshape((-1,) + (1,) * (values.ndim - 1 - dim))

    one_side = jax.random.permutation(key, parts)[block_of(target)]
    other_side = (block_of(target) + parts // 2) % parts
    return jnp.where((block_of(source) == one_side) | (block_of(source) == other_side), factor * values, values)


def shard_levels(key, dims, cuts, smallest, largest):
    level, own = 1.0, jax.random.fold_in(key, 6)
    for axis_at, blocks in cuts:
        steps = jnp.exp(jax.random.uniform(jax.random.fold_in(own, axis_at), (blocks,), jnp.float32, smallest / len(cuts), largest / len(cuts)))
        level = level * jnp.repeat(steps, dims[axis_at] // blocks).reshape([-1 if axis == axis_at else 1 for axis in range(len(dims))])
    return level


def choose_distinct(own_key, rows, count, top, lift):
    order = jax.random.permutation(jax.random.fold_in(own_key, 1), count)
    pull = order
    for power in range(3):
        pull = pull * pull // count
    pull = pull * lift // count
    chance = jax.random.randint(jax.random.fold_in(own_key, 2), (rows, count), 0, 4096) + pull
    fixed_rows = jax.random.permutation(jax.random.fold_in(own_key, 3), rows)[jnp.arange(count) % rows]
    chance = jnp.where(jnp.arange(rows)[:, None] == fixed_rows[None, :], 1 << 14, chance)
    priority = chance * count + jnp.arange(count)
    return lax.top_k(priority.astype(jnp.int32), top)[1].astype(jnp.int32)


def length_profile(number_of, total, reach, lean):
    weights = [(1 << 20) // math.isqrt(rank ** lean) + 1 for rank in range(2, number_of + 1)]
    surplus, counts = total - reach - (number_of - 1), [1] * (number_of - 1)
    while surplus > 0:
        movable = [i for i in range(number_of - 1) if counts[i] < reach]
        whole, remaining = sum([weights[i] for i in movable]), surplus
        for i in movable:
            addition = min(reach - counts[i], max(1, remaining * weights[i] // whole), surplus)
            counts[i] = counts[i] + addition
            surplus = surplus - addition
    return np.array([reach] + counts)


def ragged(stream_key, amount, total, reach, lean):
    if amount == 2:
        one = jax.random.randint(stream_key, (), max(1, total - reach), min(reach, total - 1) + 1)
        return jnp.stack([one, total - one])
    lengths = jnp.asarray(length_profile(amount, total, reach, lean), jnp.int32)
    twos = (amount - 1) // 2
    source_of, sink = lengths[1:1 + 2 * twos:2], lengths[2:2 + 2 * twos:2]
    margin = jnp.minimum(source_of - 1, reach - sink)
    moved = jax.random.randint(jax.random.fold_in(stream_key, 1), (twos,), 0, 1 << 20) % (margin + 1)
    lengths = lengths.at[1:1 + 2 * twos:2].set(source_of - moved).at[2:2 + 2 * twos:2].set(sink + moved)
    return lengths[jax.random.permutation(jax.random.fold_in(stream_key, 2), amount)]


def bell_draw(own_key, shape, width, bound, cuts=(), held_as=jnp.bfloat16):
    drawn = width * jax.random.normal(own_key, shape, jnp.float32)
    if cuts:
        drawn = drawn * shard_levels(own_key, shape, cuts, -0.22, 0.18)
    return jnp.clip(drawn, -bound, bound).astype(held_as)


def gaussian_with(key, shape, spread, limit, split, heavy, kind=jnp.bfloat16):
    values = spread * jax.random.normal(key, shape, jnp.float32)
    if split:
        values = values * shard_levels(key, shape, split, -0.22, 0.18)
    return jnp.clip(spiked(values, jax.random.fold_in(key, 3), *heavy), -limit, limit).astype(kind)


def setup_inputs(seed: int = 0) -> dict:
    seeds = jax.random.split(jax.random.key(seed), 15)
    return {
        "tokens": gaussian_with(seeds[0], (TOKENS, MODEL_WIDTH), 1.0, 16.0, ((0, 64),), (0, 1, 64, 4.0)),
        "segments": jax.vmap(lambda own: jnp.searchsorted(jnp.cumsum(ragged(own, 4, TOK_DEV, TOK_DEV // 2, 0)), jnp.arange(TOK_DEV), side="right"))(jax.random.split(seeds[1], SEQS)).reshape((SEQS, TOK_DEV)).astype(jnp.int32),
        "routes": choose_distinct(seeds[2], LAYER_COUNT * TOKENS, EXPERTS, TOPK, 4096).reshape((LAYER_COUNT, TOKENS, TOPK)),
        "norm_attention": jnp.clip(1.0 + 0.18 * jax.random.normal(seeds[3], (LAYER_COUNT, MODEL_WIDTH), jnp.float32), 0.099609375, 1.8984375).astype(jnp.bfloat16),
        "query_weight": bell_draw(seeds[4], (LAYER_COUNT, MODEL_WIDTH, QUERY_HEADS * HEAD_SIZE), MODEL_WIDTH ** -0.5, 0.1875, ((2, 2),)),
        "key_matrix": bell_draw(seeds[5], (LAYER_COUNT, MODEL_WIDTH, KV_HEAD_COUNT * HEAD_SIZE), MODEL_WIDTH ** -0.5, 0.1875, ((2, 2),)),
        "value_matrix": bell_draw(seeds[6], (LAYER_COUNT, MODEL_WIDTH, KV_HEAD_COUNT * HEAD_SIZE), MODEL_WIDTH ** -0.5, 0.1875, ((2, 2),)),
        "output_weight": bell_draw(seeds[7], (LAYER_COUNT, QUERY_HEADS * HEAD_SIZE, MODEL_WIDTH), (QUERY_HEADS * HEAD_SIZE // 16) ** -0.5, 0.75, ((1, 2),)),
        "norm_experts": jnp.clip(1.0 + 0.18 * jax.random.normal(seeds[8], (LAYER_COUNT, MODEL_WIDTH), jnp.float32), 0.099609375, 1.8984375).astype(jnp.bfloat16),
        "router_weight": bell_draw(seeds[9], (LAYER_COUNT, MODEL_WIDTH, EXPERTS), (3 * MODEL_WIDTH) ** -0.5, 0.109375),
        "gate_weight": bell_draw(seeds[10], (LAYER_COUNT, EXPERTS, MODEL_WIDTH, FF_EXP), MODEL_WIDTH ** -0.5, 0.1875, ((3, 2),)),
        "up_weight": bell_draw(seeds[11], (LAYER_COUNT, EXPERTS, MODEL_WIDTH, FF_EXP), MODEL_WIDTH ** -0.5, 0.1875, ((3, 2),)),
        "down_weight": bell_draw(seeds[12], (LAYER_COUNT, EXPERTS, FF_EXP, MODEL_WIDTH), (FF_EXP // 2) ** -0.5, 0.375, ((2, 2),)),
        "cotangent": gaussian_with(seeds[13], (TOKENS, MODEL_WIDTH), 1.0, 16.0, ((0, 64),), (0, 1, 64, 4.0)),
    }


EPSILON = 1e-06
THETA = 10000.0
EXCLUDED = -1e+30
HIGHEST = lax.Precision.HIGHEST

@jax.custom_vjp
def lower_precision(v):
    return lax.optimization_barrier(v.astype(jnp.bfloat16)).astype(jnp.float32)

@jax.custom_vjp
def lower_precision_back(v):
    return v

def low_keep(v):
    return (lower_precision(v), None)

def low_pass(kept, grad):
    return (grad,)

def back_keep(v):
    return (v, None)

def back_low(kept, grad):
    return (lower_precision(grad),)
lower_precision.defvjp(low_keep, low_pass)
lower_precision_back.defvjp(back_keep, back_low)

def matrix_product(left, right):
    return jnp.dot(left, right, precision=HIGHEST)

def rope_tables(token_length, head_width):
    half_width = head_width // 2
    frequency = THETA ** (-2.0 * jnp.arange(half_width, dtype=jnp.float32) / head_width)
    angles = jnp.arange(token_length, dtype=jnp.float32)[:, None] * frequency[None, :]
    cosine_table = jnp.concatenate([jnp.cos(angles), jnp.cos(angles)], axis=1)[:, None, :]
    sine_table = jnp.concatenate([jnp.sin(angles), jnp.sin(angles)], axis=1)[:, None, :]
    return (cosine_table, sine_table)

def rotate(field, cosine_table, sine_table):
    half_width = field.shape[-1] // 2
    turned = jnp.concatenate([-field[..., half_width:], field[..., :half_width]], axis=-1)
    return field * cosine_table + turned * sine_table

def normalize(stream, gain):
    factor = lax.rsqrt(lax.optimization_barrier(jnp.mean(stream * stream, axis=-1, keepdims=True)) + EPSILON)
    return stream * factor * gain

def attention(query_rows, key_matrix_rows, value_matrix_rows, segment):
    head_groups, token_length = segment.shape
    rows_per_block = min(512, token_length)
    block_number = token_length // rows_per_block
    group_width = QUERY_HEADS // KV_HEAD_COUNT
    score_scale = HEAD_SIZE ** (-0.5)
    query_block_grid = query_rows.reshape(head_groups, block_number, rows_per_block, KV_HEAD_COUNT, group_width, HEAD_SIZE).transpose(1, 0, 2, 3, 4, 5)
    starts = jnp.arange(block_number, dtype=jnp.int32) * rows_per_block

    def one_block(inputs):
        query_block, offset = inputs
        scores = lower_precision_back(jnp.einsum('bqkgd,bskd->bkgqs', query_block, key_matrix_rows, precision=HIGHEST) * score_scale)
        rows_at = offset + jnp.arange(rows_per_block, dtype=jnp.int32)
        columns_at = jnp.arange(token_length, dtype=jnp.int32)
        query_segment = lax.dynamic_slice_in_dim(segment, offset, rows_per_block, axis=1)
        allowed = (columns_at[None, None, :] <= rows_at[None, :, None]) & (query_segment[:, :, None] == segment[:, None, :])
        masked = jnp.where(allowed[:, None, None, :, :], scores, EXCLUDED)
        probable = lower_precision(jax.nn.softmax(masked, axis=-1))
        return jnp.einsum('bkgqs,bskd->bqkgd', probable, value_matrix_rows, precision=HIGHEST)
    mixture = lax.map(jax.checkpoint(one_block), (query_block_grid, starts))
    return mixture.transpose(1, 0, 2, 3, 4, 5).reshape(head_groups * token_length, QUERY_HEADS * HEAD_SIZE)

def layer(stream, segment, route_rows, layer_weights):
    norm_attention, query_weight, key_matrix, value_matrix, output_weight, norm_experts, router_weight, gate_weight, up_weight, down_weight = layer_weights
    head_groups, token_length, features = stream.shape
    cosine_table, sine_table = rope_tables(token_length, HEAD_SIZE)
    flat_stream = stream.reshape(head_groups * token_length, features)
    attention_inputs = lower_precision(normalize(flat_stream, norm_attention))
    query_rows = lower_precision_back(matrix_product(attention_inputs, query_weight)).reshape(head_groups, token_length, QUERY_HEADS, HEAD_SIZE)
    key_matrix_rows = lower_precision_back(matrix_product(attention_inputs, key_matrix)).reshape(head_groups, token_length, KV_HEAD_COUNT, HEAD_SIZE)
    value_matrix_rows = lower_precision(lower_precision_back(matrix_product(attention_inputs, value_matrix))).reshape(head_groups, token_length, KV_HEAD_COUNT, HEAD_SIZE)
    query_rows = lower_precision(rotate(query_rows, cosine_table, sine_table))
    key_matrix_rows = lower_precision(rotate(key_matrix_rows, cosine_table, sine_table))
    mixture = lower_precision(lower_precision_back(attention(query_rows, key_matrix_rows, value_matrix_rows, segment)))
    middle = flat_stream + lower_precision_back(matrix_product(mixture, output_weight))
    expert_input = lower_precision(normalize(middle, norm_experts))
    logits = matrix_product(expert_input, router_weight)
    chosen = (route_rows[:, :, None] == jnp.arange(EXPERTS, dtype=jnp.int32)[None, None, :]).astype(middle.dtype)
    gates = jax.nn.softmax(lax.optimization_barrier(jnp.sum(chosen * logits[:, None, :], axis=-1)), axis=-1)
    shares = lax.optimization_barrier(jnp.sum(chosen * gates[:, :, None], axis=1))
    combined = jnp.zeros_like(middle)
    for expert_index in range(EXPERTS):
        gate_in = lower_precision_back(matrix_product(expert_input, gate_weight[expert_index]))
        linear = lower_precision_back(matrix_product(expert_input, up_weight[expert_index]))
        activation = lower_precision(jax.nn.silu(gate_in) * linear)
        expert_out = lower_precision_back(matrix_product(activation, down_weight[expert_index]))
        combined = combined + shares[:, expert_index:expert_index + 1] * expert_out
    return (middle + combined).reshape(head_groups, token_length, features)

def reference(tokens, segments, routes, norm_attention, query_weight, key_matrix, value_matrix, output_weight, norm_experts, router_weight, gate_weight, up_weight, down_weight, cotangent):
    group_count = math.gcd(SEQS, max(1, 4096 // TOK_DEV))
    step_count = SEQS // group_count
    weights = tuple((member.astype(jnp.float32) for member in (norm_attention, query_weight, key_matrix, value_matrix, output_weight, norm_experts, router_weight, gate_weight, up_weight, down_weight)))
    streams = tokens.astype(jnp.float32).reshape(step_count, group_count, TOK_DEV, MODEL_WIDTH)
    segment_steps = segments.reshape(step_count, group_count, TOK_DEV)
    route_steps = routes.reshape(LAYER_COUNT, step_count, group_count * TOK_DEV, TOPK).transpose(1, 0, 2, 3)
    cotangent_steps = cotangent.astype(jnp.float32).reshape(step_count, group_count, TOK_DEV, MODEL_WIDTH)

    def one_step(totals, inputs):
        stream, segment, route_rows, incoming = inputs

        def forward(start_stream, layer_weights):
            current = start_stream
            for layer_index in range(LAYER_COUNT):
                current = layer(current, segment, route_rows[layer_index], tuple((member[layer_index] for member in layer_weights)))
            return current
        result, pullback = jax.vjp(forward, stream, weights)
        stream_gradient, weight_gradients = pullback(incoming)
        totals = jax.tree.map(jnp.add, totals, weight_gradients)
        return (totals, (result, stream_gradient))
    totals, (results, gradients) = lax.scan(one_step, jax.tree.map(jnp.zeros_like, weights), (streams, segment_steps, route_steps, cotangent_steps))
    return (results.reshape(TOKENS, MODEL_WIDTH).astype(jnp.bfloat16), gradients.reshape(TOKENS, MODEL_WIDTH), totals[0], totals[1], totals[2], totals[3], totals[4], totals[5], totals[6], totals[7], totals[8], totals[9])
```

```python
import functools

import jax
import jax.numpy as jnp
import numpy as np
from jax import lax
from jax.experimental import pallas as pl
from jax.experimental.pallas import tpu as pltpu
from jax.sharding import Mesh
from jax.sharding import PartitionSpec as P

HEAD_SIZE = 64
LANES = 128
STREAMS = 4
SMALL = 128
DP = ("dp_0", "dp_1", "dp_2", "dp_3")
DP_SIZES = (4, 2, 4, 2)
EPSILON = 1e-06
THETA = 10000.0
EXCLUDED = -1e30
F32 = jnp.float32
BF16 = jnp.bfloat16
MIB = 1024 * 1024

ORDERS = (
    (("x", "u"), ("z", "u"), ("x", "v"), ("z", "v")),
    (("z", "u"), ("x", "v"), ("z", "v"), ("x", "u")),
    (("x", "v"), ("z", "v"), ("x", "u"), ("z", "u")),
    (("z", "v"), ("x", "u"), ("z", "u"), ("x", "v")),
)


def pair_bit(index, kind):
    high = index // 2
    if kind == "v":
        return high
    return high ^ (index % 2)


def place(stream, x, yh, z):
    at = 0
    for ring, kind in ORDERS[stream]:
        at = at * 2 + pair_bit(x if ring == "x" else z, kind)
    return at * 2 + yh


def mm(a, b):
    return lax.dot_general(a, b, (((1,), (0,)), ((), ())), preferred_element_type=F32)


def mm_nt(a, b):
    return lax.dot_general(a, b, (((1,), (1,)), ((), ())), preferred_element_type=F32)


def mm_tn(a, b):
    return lax.dot_general(a, b, (((0,), (0,)), ((), ())), preferred_element_type=F32)


def row_factor(stream):
    return lax.rsqrt(jnp.mean(stream * stream, axis=-1, keepdims=True) + EPSILON)


def norm_back(stream, factor, gain, gradient):
    weighted = gradient * gain
    inner = jnp.sum(weighted * stream, axis=-1, keepdims=True) * (1.0 / stream.shape[-1])
    change = factor * weighted - stream * (factor * factor * factor) * inner
    return change, jnp.sum(gradient * stream * factor, axis=0, keepdims=True)


def lane_of(rows):
    return lax.broadcasted_iota(jnp.int32, (rows, LANES), 1)


def partner(block, lane):
    back = pltpu.roll(block, LANES - HEAD_SIZE // 2, 1)
    ahead = pltpu.roll(block, HEAD_SIZE // 2, 1)
    return jnp.where(lane % HEAD_SIZE < HEAD_SIZE // 2, back, ahead)


def both_heads(block, lane):
    rolled = pltpu.roll(block, HEAD_SIZE, 1)
    low = lane < HEAD_SIZE
    return jnp.where(low, block, rolled), jnp.where(low, rolled, block)


def stacked_pair(block, lane):
    zero = jnp.zeros_like(block)
    low = lane < HEAD_SIZE
    return jnp.concatenate(
        [jnp.where(low, block, zero), jnp.where(low, zero, block)], axis=0
    )


def allowed_pairs(seg_row, seg_column):
    length = seg_column.shape[0]
    rows = lax.broadcasted_iota(jnp.int32, (length, length), 0)
    columns = lax.broadcasted_iota(jnp.int32, (length, length), 1)
    allowed = (columns <= rows) & (seg_column == seg_row)
    bias = jnp.where(allowed, 0.0, 1.0)
    return jnp.concatenate([bias, bias], axis=0) < 0.5


def store_blocks(keep_ref, send_ref, value, column, width, stream, my_core, my_place):
    rows = value.shape[0] // 64
    for block in range(32):
        x, yh, z = block // 8, (block // 4) % 2, block % 4
        at = place(stream, x, yh, z)
        to = pl.multiple_of((my_place ^ at) * rows, rows)
        first = value[2 * block * rows : (2 * block + 1) * rows]
        second = value[(2 * block + 1) * rows : (2 * block + 2) * rows]
        keep_ref[pl.ds(to, rows), column : column + width] = jnp.where(
            my_core == 0, first, second
        )
        send_ref[pl.ds(to, rows), column : column + width] = jnp.where(
            my_core == 0, second, first
        )


def store_natural(keep_ref, send_ref, value, column, width, my_core):
    rows = value.shape[0] // 64
    for block in range(32):
        first = value[2 * block * rows : (2 * block + 1) * rows]
        second = value[(2 * block + 1) * rows : (2 * block + 2) * rows]
        at = slice(block * rows, (block + 1) * rows)
        keep_ref[at, column : column + width] = jnp.where(my_core == 0, first, second)
        send_ref[at, column : column + width] = jnp.where(my_core == 0, second, first)


def attention_forward_kernel(count, *refs):
    parts = refs[:count]
    (gain, wq, wk, wv, wo, cos, sin, seg_row, seg_column) = refs[count : count + 9]
    (x_out, a_out, q_out, kk_out, vv_out, mix_out, part_out) = refs[count + 9 :]
    x = parts[0][...].astype(F32)
    if count == 3:
        x = x + (parts[1][...] + parts[2][...])
    x_out[...] = x
    length = x.shape[0]
    a = (x * row_factor(x) * gain[...].astype(F32)).astype(BF16)
    a_out[...] = a
    lane = lane_of(length)
    cosine, sine = cos[...], sin[...]
    q = mm(a, wq[...])
    k = mm(a, wk[...])
    v = mm(a, wv[...])
    allowed = allowed_pairs(seg_row[...], seg_column[...])
    scale = HEAD_SIZE**-0.5
    pairs = k.shape[1] // LANES
    for pair in range(pairs):
        at = slice(pair * LANES, (pair + 1) * LANES)
        k_block = k[:, at] * cosine + partner(k[:, at], lane) * sine
        k_twice = both_heads(k_block, lane)
        v_twice = both_heads(v[:, at], lane)
        for side in range(2):
            head = 2 * pair + side
            columns = slice(head * LANES, (head + 1) * LANES)
            kk = k_twice[side].astype(BF16)
            vv = v_twice[side].astype(BF16)
            kk_out[head] = kk
            vv_out[head] = vv
            q_block = q[:, columns]
            q_block = (q_block * cosine + partner(q_block, lane) * sine).astype(BF16)
            q_out[:, columns] = q_block
            scores = mm_nt(stacked_pair(q_block, lane), kk) * scale
            scores = jnp.where(allowed, scores, EXCLUDED)
            shifted = jnp.exp(scores - jnp.max(scores, axis=-1, keepdims=True))
            probs = (shifted / jnp.sum(shifted, axis=-1, keepdims=True)).astype(BF16)
            mixed = mm(probs, vv)
            mix_out[:, columns] = jnp.where(
                lane < HEAD_SIZE, mixed[:length], mixed[length:]
            ).astype(BF16)
    part_out[...] = mm(mix_out[...], wo[...])


def whole(shape):
    return pl.BlockSpec(shape, lambda i: (0,) * len(shape))


def of_layer(layer, shape):
    return pl.BlockSpec((None, *shape), lambda i: (layer,) + (0,) * len(shape))


def params(mib):
    return pltpu.CompilerParams(
        vmem_limit_bytes=mib * MIB, dimension_semantics=("arbitrary",)
    )


def cost(flops, nbytes):
    return pl.CostEstimate(flops=flops, bytes_accessed=nbytes, transcendentals=0)


def attention_forward(layer, parts, weights, tables, segment):
    gain, wq, wk, wv, wo = weights
    length, features = parts[0].shape
    q_width, k_width = wq.shape[2], wk.shape[2]
    heads = 2 * k_width // LANES
    ins = [*parts, gain, wq, wk, wv, wo, *tables, *segment]
    in_specs = [whole(part.shape) for part in parts]
    in_specs += [of_layer(layer, w.shape[1:]) for w in (gain, wq, wk, wv, wo)]
    in_specs += [whole(t.shape) for t in (*tables, *segment)]
    outs = [
        ((length, features), F32),
        ((length, features), BF16),
        ((length, q_width), BF16),
        ((heads, length, LANES), BF16),
        ((heads, length, LANES), BF16),
        ((length, q_width), BF16),
        ((length, features), F32),
    ]
    return pl.pallas_call(
        functools.partial(attention_forward_kernel, len(parts)),
        grid=(1,),
        in_specs=in_specs,
        out_specs=[whole(shape) for shape, _ in outs],
        out_shape=[jax.ShapeDtypeStruct(*out) for out in outs],
        compiler_params=params(48),
        cost_estimate=cost(1 << 30, 8 * MIB),
        name="attention_forward",
    )(*ins)


def column_of(table, lane, index):
    return jnp.sum(jnp.where(lane == index, table, 0.0), axis=1, keepdims=True)


def expert_prologue(x, own, other, gain, router, mask, middle_out, xi_out, share_out):
    middle = x[...] + (own[...] + other[...])
    middle_out[...] = middle
    xi = (middle * row_factor(middle) * gain[...].astype(F32)).astype(BF16)
    xi_out[...] = xi
    logits = mm(xi, router[...])
    chosen = mask[...] > 0.5
    logits = jnp.where(chosen, logits, EXCLUDED)
    shifted = jnp.exp(logits - jnp.max(logits, axis=-1, keepdims=True))
    shifted = jnp.where(chosen, shifted, 0.0)
    share_out[...] = shifted / jnp.sum(shifted, axis=-1, keepdims=True)


def expert_step(gate_in, linear, wd, share):
    squashed = 1.0 / (1.0 + jnp.exp(-gate_in))
    silu = gate_in * squashed
    activation = (silu * linear).astype(BF16)
    return squashed, silu, activation, mm(activation, wd)


def expert_backward_step(
    stream, places, g, xi, share, gate_in, linear, wg, wu, wd, keep, send, natural
):
    my_core, my_place = places
    squashed, silu, activation, expert_out = expert_step(gate_in, linear, wd, share)
    gate_grad = jnp.sum(g * expert_out, axis=1, keepdims=True)
    expert_grad = (share * g).astype(BF16)
    activation_grad = mm_nt(expert_grad, wd)
    gate_in_grad = (
        activation_grad * linear * squashed * (1.0 + gate_in * (1.0 - squashed))
    ).astype(BF16)
    linear_grad = (activation_grad * silu).astype(BF16)
    width = activation.shape[1]

    def store(value, column):
        if natural:
            store_natural(keep, send, value, column, width, my_core)
        else:
            store_blocks(keep, send, value, column, width, stream, my_core, my_place)

    store(mm_tn(xi, gate_in_grad), 0)
    store(mm_tn(xi, linear_grad), width)
    store(mm_tn(expert_grad, activation), 2 * width)
    return gate_grad, mm_nt(gate_in_grad, wg) + mm_nt(linear_grad, wu), expert_out


def expert_forward_kernel(
    x, own, other, gain, router, mask, wg, wu, wd,
    middle_out, xi_out, share_out, gate_out, linear_out, part_out,
):
    expert = pl.program_id(0)

    @pl.when(expert == 0)
    def _():
        expert_prologue(x, own, other, gain, router, mask, middle_out, xi_out, share_out)
        part_out[...] = jnp.zeros_like(part_out)

    share = column_of(share_out[...], lane_of(share_out.shape[0]), expert)
    xi = xi_out[...]
    gate_in = mm(xi, wg[...])
    linear = mm(xi, wu[...])
    gate_out[...] = gate_in
    linear_out[...] = linear
    part_out[...] += share * expert_step(gate_in, linear, wd[...], share)[3]


def expert_both_kernel(
    places, x, own, other, gain, router, mask, wg, wu, wd, cotangent,
    middle_out, xi_out, share_out, part_out, back_out, gate_grad_out, keep, send,
):
    expert = pl.program_id(0)
    lane = lane_of(share_out.shape[0])

    @pl.when(expert == 0)
    def _():
        expert_prologue(x, own, other, gain, router, mask, middle_out, xi_out, share_out)
        part_out[...] = jnp.zeros_like(part_out)
        back_out[...] = jnp.zeros_like(back_out)
        gate_grad_out[...] = jnp.zeros_like(gate_grad_out)

    share = column_of(share_out[...], lane, expert)
    xi = xi_out[...]
    gate_in = mm(xi, wg[...])
    linear = mm(xi, wu[...])
    gate_grad, back, expert_out = expert_backward_step(
        0, (places[STREAMS], 0), cotangent[...].astype(F32), xi, share,
        gate_in, linear, wg[...], wu[...], wd[...], keep, send, True,
    )
    part_out[...] += share * expert_out
    back_out[...] += back
    gate_grad_out[...] += jnp.where(lane == expert, gate_grad, 0.0)


def expert_backward_kernel(
    places, g_in, x, gain, own, other, xi_ref, share_ref, gate_ref, linear_ref, wg, wu, wd,
    g_out, gain_out, back_out, gate_grad_out, keep, send,
):
    expert = pl.program_id(0)
    lane = lane_of(share_ref.shape[0])

    @pl.when(expert == 0)
    def _():
        stream = x[...]
        change, gain_row = norm_back(
            stream, row_factor(stream), gain[...].astype(F32), own[...] + other[...]
        )
        g_out[...] = g_in[...] + change
        gain_out[...] = jnp.broadcast_to(gain_row, gain_out.shape)
        back_out[...] = jnp.zeros_like(back_out)
        gate_grad_out[...] = jnp.zeros_like(gate_grad_out)

    def stored_for(stream):
        @pl.when(expert == stream)
        def _():
            share = column_of(share_ref[...], lane, stream)
            gate_grad, back, _ = expert_backward_step(
                stream, (places[STREAMS], places[stream]), g_out[...], xi_ref[...], share,
                gate_ref[...], linear_ref[...], wg[...], wu[...], wd[...], keep, send, False,
            )
            back_out[...] += back
            gate_grad_out[...] += jnp.where(lane == stream, gate_grad, 0.0)

    for stream in range(STREAMS):
        stored_for(stream)


def of_expert(layer, shape):
    return pl.BlockSpec((None, None, *shape), lambda e: (layer, e, 0, 0))


def each_expert(shape):
    return pl.BlockSpec((None, *shape), lambda e: (e, 0, 0))


def gradient_outs(rows, width):
    spec = pl.BlockSpec((rows, 3 * width), lambda e: (0, e))
    shape = ((rows, 3 * width * STREAMS), F32)
    return [(spec, shape)] * 2


SMEM = pl.BlockSpec(memory_space=pltpu.SMEM)


def run_experts(kernel, name, ins, in_specs, outs, flops, nbytes, mib):
    return pl.pallas_call(
        kernel,
        grid=(STREAMS,),
        in_specs=in_specs,
        out_specs=[spec for spec, _ in outs],
        out_shape=[jax.ShapeDtypeStruct(*out) for _, out in outs],
        compiler_params=params(mib),
        cost_estimate=cost(flops, nbytes),
        name=name,
    )(*ins)


def expert_forward(layer, x, own, other, gain, router, mask, wg, wu, wd):
    length, features = x.shape
    width = wg.shape[3]
    big, low = ((length, features), F32), ((length, features), BF16)
    hidden = (each_expert((length, width)), ((STREAMS, length, width), F32))
    ins = [x, own, other, gain, router, mask, wg, wu, wd]
    in_specs = [whole(x.shape)] * 3 + [
        of_layer(layer, gain.shape[1:]),
        of_layer(layer, router.shape[1:]),
        of_layer(layer, mask.shape[1:]),
        *(of_expert(layer, w.shape[2:]) for w in (wg, wu, wd)),
    ]
    outs = [
        (whole(big[0]), big),
        (whole(low[0]), low),
        (whole((length, LANES)), ((length, LANES), F32)),
        hidden,
        hidden,
        (whole(big[0]), big),
    ]
    return run_experts(
        expert_forward_kernel, "experts_forward", ins, in_specs, outs, 8 << 28, 12 * MIB, 48
    )


def expert_both(layer, places, x, own, other, gain, router, mask, wg, wu, wd, cotangent):
    length, features = x.shape
    width = wg.shape[3]
    big, low = ((length, features), F32), ((length, features), BF16)
    table = (whole((length, LANES)), ((length, LANES), F32))
    ins = [places, x, own, other, gain, router, mask, wg, wu, wd, cotangent]
    in_specs = [SMEM] + [whole(x.shape)] * 3 + [
        of_layer(layer, gain.shape[1:]),
        of_layer(layer, router.shape[1:]),
        of_layer(layer, mask.shape[1:]),
        *(of_expert(layer, w.shape[2:]) for w in (wg, wu, wd)),
        whole(cotangent.shape),
    ]
    outs = [
        (whole(big[0]), big),
        (whole(low[0]), low),
        table,
        (whole(big[0]), big),
        (whole(big[0]), big),
        table,
        *gradient_outs(features // 2, width),
    ]
    return run_experts(
        expert_both_kernel, "experts_both", ins, in_specs, outs, 5 << 30, 30 * MIB, 56
    )


def expert_backward(layer, places, g, x, gain, own, other, xi, share, gate_in, linear, wg, wu, wd):
    length, features = x.shape
    width = wg.shape[3]
    big = ((length, features), F32)
    table = (whole((length, LANES)), ((length, LANES), F32))
    hidden = each_expert((length, width))
    ins = [places, g, x, gain, own, other, xi, share, gate_in, linear, wg, wu, wd]
    in_specs = [SMEM, whole(x.shape), whole(x.shape)] + [
        of_layer(layer + 1, gain.shape[1:]),
        whole(x.shape),
        whole(x.shape),
        whole(x.shape),
        whole(share.shape),
        hidden,
        hidden,
        *(of_expert(layer, w.shape[2:]) for w in (wg, wu, wd)),
    ]
    outs = [
        (whole(big[0]), big),
        (whole((8, features)), ((8, features), F32)),
        (whole(big[0]), big),
        table,
        *gradient_outs(features // 2, width),
    ]
    return run_experts(
        expert_backward_kernel, "experts_backward", ins, in_specs, outs, 4 << 30, 30 * MIB, 56
    )


def stream_columns(stream, width):
    return SMALL + width * stream if stream else 0


def attention_backward_kernel(
    places, g, own, other, gate_own, gate_other, middle, xi, share, gain, router_rows,
    wo, mix, q, kk, vv, a, wq, wk, wv, cos, sin, seg_row, seg_column, x, late_gain,
    g_out, part_out, keep, send, rows_scratch,
):
    my_core = places[STREAMS]
    length = middle.shape[0]
    lane = lane_of(length)
    shares = share[...]
    gate_grad = gate_own[...] + gate_other[...]
    pick = shares * (gate_grad - jnp.sum(shares * gate_grad, axis=1, keepdims=True))
    input_grad = own[...] + other[...]
    xi_full = xi[...].astype(F32)
    rows_scratch[...] = jnp.zeros_like(rows_scratch)
    for expert in range(STREAMS):
        logit_grad = column_of(pick, lane, expert)
        input_grad = input_grad + logit_grad * router_rows[expert : expert + 1, :]
        rows_scratch[expert : expert + 1, :] = jnp.sum(
            xi_full * logit_grad, axis=0, keepdims=True
        )
    mid = middle[...]
    change, gain_row = norm_back(mid, row_factor(mid), gain[...].astype(F32), input_grad)
    rows_scratch[4:5, :] = gain_row
    rows_scratch[6:7, :] = late_gain[0:1, :]
    gradient = g[...].astype(F32) + change
    g_out[...] = gradient
    output_grad = gradient.astype(BF16)
    mixture_grad = mm_nt(output_grad, wo[...]).astype(BF16)

    part = q.shape[1] // LANES
    gradients = [None] * (3 * part)
    projection = mm_tn(output_grad, mix[...])
    cosine, sine = cos[...], sin[...]
    allowed = allowed_pairs(seg_row[...], seg_column[...])
    scale = HEAD_SIZE**-0.5
    low = lane < HEAD_SIZE
    a_full = a[...]
    query_grads, key_grads, value_grads = [], [], []
    for pair in range(part // 2):
        key_sides, value_sides = [], []
        for side in range(2):
            head = 2 * pair + side
            columns = slice(head * LANES, (head + 1) * LANES)
            stacked = stacked_pair(q[:, columns], lane)
            scores = jnp.where(allowed, mm_nt(stacked, kk[head]) * scale, EXCLUDED)
            shifted = jnp.exp(scores - jnp.max(scores, axis=-1, keepdims=True))
            probs = shifted / jnp.sum(shifted, axis=-1, keepdims=True)
            mix_grad = stacked_pair(mixture_grad[:, columns], lane)
            prob_grad = mm_nt(mix_grad, vv[head])
            inner = jnp.sum(probs * prob_grad, axis=-1, keepdims=True)
            score_grad = (probs * (prob_grad - inner)).astype(BF16)
            query = mm(score_grad, kk[head])
            query = jnp.where(low, query[:length], query[length:]) * scale
            query = query * cosine - partner(query, lane) * sine
            query_grads.append(query.astype(BF16))
            key = mm_tn(score_grad, stacked) * scale
            key_sides.append(key + pltpu.roll(key, HEAD_SIZE, 1))
            value = mm_tn(probs.astype(BF16), mix_grad)
            value_sides.append(value + pltpu.roll(value, HEAD_SIZE, 1))
        key = jnp.where(low, key_sides[0], key_sides[1])
        key_grads.append((key * cosine - partner(key, lane) * sine).astype(BF16))
        value_grads.append(jnp.where(low, value_sides[0], value_sides[1]).astype(BF16))
    query_grad = jnp.concatenate(query_grads, axis=1)
    key_grad = jnp.concatenate(key_grads, axis=1)
    value_grad = jnp.concatenate(value_grads, axis=1)
    attention_part = (
        mm_nt(query_grad, wq[...]) + mm_nt(key_grad, wk[...]) + mm_nt(value_grad, wv[...])
    )
    part_out[...] = attention_part
    stream = x[...]
    rows_scratch[5:6, :] = jnp.sum(
        attention_part * stream * row_factor(stream), axis=0, keepdims=True
    )

    totals = [mm_tn(a_full, query_grad), mm_tn(a_full, key_grad), mm_tn(a_full, value_grad)]
    totals.append(projection)
    pieces = [total[:, at : at + LANES] for total in totals for at in range(0, total.shape[1], LANES)]
    small = jnp.transpose(rows_scratch[...])
    per_stream = len(pieces) // STREAMS
    for stream_index in range(STREAMS):
        column = stream_columns(stream_index, per_stream * LANES)
        mine = pieces[stream_index * per_stream : (stream_index + 1) * per_stream]
        if stream_index == 0:
            mine = [small] + mine
        for piece in mine:
            store_blocks(
                keep, send, piece, column, LANES, stream_index, my_core, places[stream_index]
            )
            column += LANES


def attention_backward(
    layer, places, g, own, other, gate_own, gate_other, saved_experts, weights, saved, tables,
    segment, late_gain,
):
    middle, xi, share = saved_experts
    gain, router_rows, wo, wq, wk, wv = weights
    x, a, q, kk, vv, mix = saved
    length, features = middle.shape
    columns = SMALL + wq.shape[2] + wk.shape[2] + wv.shape[2] + wo.shape[1]
    ins = [
        places, g, own, other, gate_own, gate_other, middle, xi, share, gain, router_rows,
        wo, mix, q, kk, vv, a, wq, wk, wv, *tables, *segment, x, late_gain,
    ]
    layered = {9, 10, 11, 17, 18, 19}
    in_specs = [SMEM]
    for at, array in enumerate(ins[1:], 1):
        in_specs.append(of_layer(layer, array.shape[1:]) if at in layered else whole(array.shape))
    outs = [
        ((length, features), F32),
        ((length, features), F32),
        ((features // 2, columns), F32),
        ((features // 2, columns), F32),
    ]
    return pl.pallas_call(
        attention_backward_kernel,
        grid=(1,),
        in_specs=in_specs,
        out_specs=[whole(shape) for shape, _ in outs],
        out_shape=[jax.ShapeDtypeStruct(*out) for out in outs],
        scratch_shapes=[pltpu.VMEM((LANES, features), F32)],
        compiler_params=params(56),
        cost_estimate=cost(3 << 30, 18 * MIB),
        name="attention_backward",
    )(*ins)


SWAP = ((0, 1), (1, 0))
RING = {"u": tuple((i, i ^ 1) for i in range(4)), "v": tuple((i, 3 - i) for i in range(4))}


def exchange(array):
    return lax.ppermute(array, "tensor", SWAP)


def scatter_streams(keep, send, columns):
    received = lax.ppermute(send, "dp_3", SWAP)
    streams = [
        (keep[:, start : start + width], received[:, start : start + width])
        for start, width in columns
    ]
    for step in range(4):
        half = 256 >> step
        sends = [first[half:] + second[half:] for first, second in streams]
        moved = []
        for stream, block in enumerate(sends):
            ring, kind = ORDERS[stream][step]
            moved.append(lax.ppermute(block, "dp_0" if ring == "x" else "dp_2", RING[kind]))
        streams = [
            (first[:half] + second[:half], block)
            for (first, second), block in zip(streams, moved)
        ]
    summed = [first + second for first, second in streams]
    packed = jnp.concatenate(summed, axis=1)
    half = packed.shape[0] // 2
    packed = packed[:half] + lax.ppermute(packed[half:], "dp_1", SWAP)
    starts = np.cumsum([0] + [width for _, width in columns])
    return [packed[:, a:b] for a, b in zip(starts[:-1], starts[1:])]


def scatter_natural(keep, send):
    summed = keep + lax.ppermute(send, "dp_3", SWAP)
    return lax.psum_scatter(
        summed, ("dp_0", "dp_1", "dp_2"), scatter_dimension=0, tiled=True
    )


def rope_tables(length):
    half = HEAD_SIZE // 2
    frequency = np.float32(THETA) ** (-2.0 * np.arange(half, dtype=np.float32) / HEAD_SIZE)
    angles = np.arange(length, dtype=np.float32)[:, None] * frequency[None].astype(np.float32)
    angles = angles.astype(np.float32)
    cosine = np.tile(np.cos(angles), (1, LANES // half)).astype(np.float32)
    sine = np.sin(angles)
    sine = np.tile(np.concatenate([-sine, sine], axis=1), (1, LANES // HEAD_SIZE))
    return jnp.asarray(cosine), jnp.asarray(sine.astype(np.float32))


def shards(
    tokens, segments, routes, norm_attention, query_weight, key_matrix, value_matrix,
    output_weight, norm_experts, router_weight, gate_weight, up_weight, down_weight, cotangent,
):
    length, features = tokens.shape
    experts = gate_weight.shape[1]
    hidden = gate_weight.shape[3]
    tables = rope_tables(length)
    segment = (segments.reshape(1, length), segments.reshape(length, 1))
    gain_attention = norm_attention[:, None, :]
    gain_experts = norm_experts[:, None, :]
    router = jnp.pad(router_weight, ((0, 0), (0, 0), (0, LANES - experts)))
    router_rows = jnp.pad(
        jnp.swapaxes(router_weight, 1, 2).astype(F32), ((0, 0), (0, 8 - experts), (0, 0))
    )
    mask = jnp.any(
        routes[..., None] == jnp.arange(LANES, dtype=jnp.int32), axis=2
    ).astype(F32)
    x_at, y_at, z_at = (lax.axis_index(name) for name in DP[:3])
    places = jnp.stack(
        [place(stream, x_at, y_at, z_at) for stream in range(STREAMS)]
        + [lax.axis_index("dp_3")]
    ).astype(jnp.int32)

    attention_weights = (gain_attention, query_weight, key_matrix, value_matrix, output_weight)
    expert_weights = (gate_weight, up_weight, down_weight)
    back_weights = (
        gain_experts, router_rows, output_weight, query_weight, key_matrix, value_matrix,
    )

    x1, *saved1, part = attention_forward(0, [tokens], attention_weights, tables, segment)
    middle1, xi1, share1, gate1, linear1, part = expert_forward(
        0, x1, part, exchange(part), gain_experts, router, mask, *expert_weights
    )
    x2, *saved2, part = attention_forward(
        1, [middle1, part, exchange(part)], attention_weights, tables, segment
    )
    middle2, xi2, share2, last, back, gate_grad, keep_e2, send_e2 = expert_both(
        1, places, x2, part, exchange(part), gain_experts, router, mask, *expert_weights, cotangent
    )
    no_gain = jnp.zeros((8, features), F32)
    g2, part, keep_a2, send_a2 = attention_backward(
        1, places, cotangent, back, exchange(back), gate_grad, exchange(gate_grad),
        (middle2, xi2, share2), back_weights, (x2, *saved2), tables, segment, no_gain,
    )
    g1, late_gain, back, gate_grad, keep_e1, send_e1 = expert_backward(
        0, places, g2, x2, gain_attention, part, exchange(part), xi1, share1, gate1, linear1,
        *expert_weights,
    )
    g0, part, keep_a1, send_a1 = attention_backward(
        0, places, g1, back, exchange(back), gate_grad, exchange(gate_grad),
        (middle1, xi1, share1), back_weights, (x1, *saved1), tables, segment, late_gain,
    )
    gain = norm_attention[0].astype(F32)
    change, _ = norm_back(x1, row_factor(x1), gain, part + exchange(part))
    gradient = g0 + change
    output = (middle2 + (last + exchange(last))).astype(BF16)

    width = (query_weight.shape[2] + 2 * key_matrix.shape[2] + output_weight.shape[1]) // STREAMS
    attention_columns = [
        (stream_columns(s, width), width + (0 if s else SMALL)) for s in range(STREAMS)
    ]
    expert_columns = [(s * 3 * hidden, 3 * hidden) for s in range(STREAMS)]
    block_e2 = scatter_natural(keep_e2, send_e2)
    blocks_a2 = scatter_streams(keep_a2, send_a2, attention_columns)
    blocks_e1 = scatter_streams(keep_e1, send_e1, expert_columns)
    blocks_a1 = scatter_streams(keep_a1, send_a1, attention_columns)

    def split_attention(blocks):
        whole_row = jnp.concatenate(blocks, axis=1)
        bounds = np.cumsum(
            [0, SMALL, query_weight.shape[2], key_matrix.shape[2], value_matrix.shape[2],
             output_weight.shape[1]]
        )
        return [whole_row[:, a:b] for a, b in zip(bounds[:-1], bounds[1:])]

    def split_experts(block):
        block = block.reshape(block.shape[0], experts, 3, hidden)
        return [jnp.swapaxes(block[:, :, kind], 0, 1) for kind in range(3)]

    attention_sums = [split_attention(blocks) for blocks in (blocks_a1, blocks_a2)]
    expert_sums = [split_experts(jnp.concatenate(blocks_e1, axis=1)), split_experts(block_e2)]
    small = jnp.stack([sums[0] for sums in attention_sums])
    attention_gain = small[:, :, 5]
    attention_gain = attention_gain + exchange(attention_gain)
    return (
        output,
        gradient,
        attention_gain,
        *(jnp.stack([sums[at] for sums in attention_sums]) for at in (1, 2, 3)),
        jnp.swapaxes(jnp.stack([sums[4] for sums in attention_sums]), 1, 2),
        small[:, :, 4],
        small[:, :, :experts],
        *(jnp.stack([sums[kind] for sums in expert_sums]) for kind in (0, 1)),
        jnp.swapaxes(jnp.stack([sums[2] for sums in expert_sums]), 2, 3),
    )


def solution(mesh):
    torus = Mesh(
        mesh.devices.reshape(*DP_SIZES, mesh.shape["tensor"]), (*DP, "tensor")
    )
    rows, copied, last = P(DP, None), P(), P(None, None, "tensor")
    in_specs = (
        rows, rows, P(None, DP, None), copied, last, last, last, P(None, "tensor", None),
        copied, copied, P(None, None, None, "tensor"), P(None, None, None, "tensor"),
        P(None, None, "tensor", None), rows,
    )
    out_specs = (
        rows, rows, P(None, DP), P(None, DP, "tensor"), P(None, DP, "tensor"),
        P(None, DP, "tensor"), P(None, "tensor", DP), P(None, DP), P(None, DP, None),
        P(None, None, DP, "tensor"), P(None, None, DP, "tensor"), P(None, None, "tensor", DP),
    )
    return jax.shard_map(
        shards, mesh=torus, in_specs=in_specs, out_specs=out_specs, check_vma=False
    )
```

```python
import functools

import jax
import jax.numpy as jnp
import numpy as np
from jax import lax
from jax.experimental import pallas as pl
from jax.experimental.pallas import tpu as pltpu
from jax.sharding import Mesh
from jax.sharding import PartitionSpec as P

HEAD_SIZE = 64
LANES = 128
STREAMS = 4
SMALL = 128
DP = ("dp_0", "dp_1", "dp_2", "dp_3")
DP_SIZES = (4, 2, 4, 2)
EPSILON = 1e-06
THETA = 10000.0
EXCLUDED = -1e30
F32 = jnp.float32
BF16 = jnp.bfloat16
MIB = 1024 * 1024

EXPERT_ORDERS = (
    (("x", "u"), ("z", "u"), ("x", "v"), ("z", "v")),
    (("z", "v"), ("x", "v"), ("z", "u"), ("x", "u")),
)
ATTENTION_ORDERS = (
    (("x", "v"), ("z", "v"), ("x", "u"), ("z", "u")),
    (("z", "u"), ("x", "u"), ("z", "v"), ("x", "v")),
)


def pair_bit(index, kind):
    high = index // 2
    if kind == "v":
        return high
    return high ^ (index % 2)


def place(order, x, yh, z):
    at = 0
    for ring, kind in order:
        at = at * 2 + pair_bit(x if ring == "x" else z, kind)
    return at * 2 + yh


def mm(a, b):
    return lax.dot_general(a, b, (((1,), (0,)), ((), ())), preferred_element_type=F32)


def mm_nt(a, b):
    return lax.dot_general(a, b, (((1,), (1,)), ((), ())), preferred_element_type=F32)


def mm_tn(a, b):
    return lax.dot_general(a, b, (((0,), (0,)), ((), ())), preferred_element_type=F32)


def row_factor(stream):
    return lax.rsqrt(jnp.mean(stream * stream, axis=-1, keepdims=True) + EPSILON)


def norm_back(stream, factor, gain, gradient):
    weighted = gradient * gain
    inner = jnp.sum(weighted * stream, axis=-1, keepdims=True) * (1.0 / stream.shape[-1])
    change = factor * weighted - stream * (factor * factor * factor) * inner
    return change, jnp.sum(gradient * stream * factor, axis=0, keepdims=True)


def lane_of(rows):
    return lax.broadcasted_iota(jnp.int32, (rows, LANES), 1)


def partner(block, lane):
    back = pltpu.roll(block, LANES - HEAD_SIZE // 2, 1)
    ahead = pltpu.roll(block, HEAD_SIZE // 2, 1)
    return jnp.where(lane % HEAD_SIZE < HEAD_SIZE // 2, back, ahead)


def both_heads(block, lane):
    rolled = pltpu.roll(block, HEAD_SIZE, 1)
    low = lane < HEAD_SIZE
    return jnp.where(low, block, rolled), jnp.where(low, rolled, block)


def stacked_pair(block, lane):
    zero = jnp.zeros_like(block)
    low = lane < HEAD_SIZE
    return jnp.concatenate(
        [jnp.where(low, block, zero), jnp.where(low, zero, block)], axis=0
    )


def allowed_pairs(seg_row, seg_column):
    length = seg_column.shape[0]
    rows = lax.broadcasted_iota(jnp.int32, (length, length), 0)
    columns = lax.broadcasted_iota(jnp.int32, (length, length), 1)
    allowed = (columns <= rows) & (seg_column == seg_row)
    bias = jnp.where(allowed, 0.0, 1.0)
    return jnp.concatenate([bias, bias], axis=0) < 0.5


def block_places(orders, places):
    core = places[2]
    found = []
    for block in range(32):
        x, yh, z = block // 8, (block // 4) % 2, block % 4
        one, two = (place(order, x, yh, z) for order in orders)
        found.append(
            (jnp.where(core == 0, one, two) ^ places[0], jnp.where(core == 0, two, one) ^ places[1])
        )
    return core, found


def store_blocks(keep_ref, send_ref, value, column, where_to):
    core, found = where_to
    rows = value.shape[0] // 64
    columns = slice(column, column + value.shape[1])
    for block, (kept, sent) in enumerate(found):
        first = value[2 * block * rows : (2 * block + 1) * rows]
        second = value[(2 * block + 1) * rows : (2 * block + 2) * rows]
        keep_ref[pl.ds(pl.multiple_of(kept * rows, rows), rows), columns] = jnp.where(
            core == 0, first, second
        )
        send_ref[pl.ds(pl.multiple_of(sent * rows, rows), rows), columns] = jnp.where(
            core == 0, second, first
        )


def attention_forward_kernel(count, *refs):
    parts = refs[:count]
    (gain, wq, wk, wv, wo, cos, sin, seg_row, seg_column) = refs[count : count + 9]
    (x_out, a_out, q_out, kk_out, vv_out, mix_out, part_out) = refs[count + 9 :]
    x = parts[0][...].astype(F32)
    if count == 3:
        x = x + (parts[1][...] + parts[2][...])
    x_out[...] = x
    length = x.shape[0]
    a = (x * row_factor(x) * gain[...].astype(F32)).astype(BF16)
    a_out[...] = a
    lane = lane_of(length)
    cosine, sine = cos[...], sin[...]
    q = mm(a, wq[...])
    k = mm(a, wk[...])
    v = mm(a, wv[...])
    allowed = allowed_pairs(seg_row[...], seg_column[...])
    scale = HEAD_SIZE**-0.5
    pairs = k.shape[1] // LANES
    for pair in range(pairs):
        at = slice(pair * LANES, (pair + 1) * LANES)
        k_block = k[:, at] * cosine + partner(k[:, at], lane) * sine
        k_twice = both_heads(k_block, lane)
        v_twice = both_heads(v[:, at], lane)
        for side in range(2):
            head = 2 * pair + side
            columns = slice(head * LANES, (head + 1) * LANES)
            kk = k_twice[side].astype(BF16)
            vv = v_twice[side].astype(BF16)
            kk_out[head] = kk
            vv_out[head] = vv
            q_block = q[:, columns]
            q_block = (q_block * cosine + partner(q_block, lane) * sine).astype(BF16)
            q_out[:, columns] = q_block
            scores = mm_nt(stacked_pair(q_block, lane), kk) * scale
            scores = jnp.where(allowed, scores, EXCLUDED)
            shifted = jnp.exp(scores - jnp.max(scores, axis=-1, keepdims=True))
            probs = (shifted / jnp.sum(shifted, axis=-1, keepdims=True)).astype(BF16)
            mixed = mm(probs, vv)
            mix_out[:, columns] = jnp.where(
                lane < HEAD_SIZE, mixed[:length], mixed[length:]
            ).astype(BF16)
    part_out[...] = mm(mix_out[...], wo[...])


def whole(shape):
    return pl.BlockSpec(shape, lambda i: (0,) * len(shape))


def of_layer(layer, shape):
    return pl.BlockSpec((None, *shape), lambda i: (layer,) + (0,) * len(shape))


def params(mib):
    return pltpu.CompilerParams(
        vmem_limit_bytes=mib * MIB, dimension_semantics=("arbitrary",)
    )


def cost(flops, nbytes):
    return pl.CostEstimate(flops=flops, bytes_accessed=nbytes, transcendentals=0)


def attention_forward(layer, parts, weights, tables, segment):
    gain, wq, wk, wv, wo = weights
    length, features = parts[0].shape
    q_width, k_width = wq.shape[2], wk.shape[2]
    heads = 2 * k_width // LANES
    ins = [*parts, gain, wq, wk, wv, wo, *tables, *segment]
    in_specs = [whole(part.shape) for part in parts]
    in_specs += [of_layer(layer, w.shape[1:]) for w in (gain, wq, wk, wv, wo)]
    in_specs += [whole(t.shape) for t in (*tables, *segment)]
    outs = [
        ((length, features), F32),
        ((length, features), BF16),
        ((length, q_width), BF16),
        ((heads, length, LANES), BF16),
        ((heads, length, LANES), BF16),
        ((length, q_width), BF16),
        ((length, features), F32),
    ]
    return pl.pallas_call(
        functools.partial(attention_forward_kernel, len(parts)),
        grid=(1,),
        in_specs=in_specs,
        out_specs=[whole(shape) for shape, _ in outs],
        out_shape=[jax.ShapeDtypeStruct(*out) for out in outs],
        compiler_params=params(60),
        cost_estimate=cost(6 << 30, 8 * MIB),
        name="attention_forward",
    )(*ins)


def column_of(table, lane, index):
    return jnp.sum(jnp.where(lane == index, table, 0.0), axis=1, keepdims=True)


def expert_prologue(x, own, other, gain, router, mask, middle_out, xi_out, share_out):
    middle = x[...] + (own[...] + other[...])
    middle_out[...] = middle
    xi = (middle * row_factor(middle) * gain[...].astype(F32)).astype(BF16)
    xi_out[...] = xi
    logits = mm(xi, router[...])
    chosen = mask[...] > 0.5
    logits = jnp.where(chosen, logits, EXCLUDED)
    shifted = jnp.exp(logits - jnp.max(logits, axis=-1, keepdims=True))
    shifted = jnp.where(chosen, shifted, 0.0)
    share_out[...] = shifted / jnp.sum(shifted, axis=-1, keepdims=True)


def expert_step(gate_in, linear, wd, share):
    squashed = 1.0 / (1.0 + jnp.exp(-gate_in))
    silu = gate_in * squashed
    activation = (silu * linear).astype(BF16)
    return squashed, silu, activation, mm(activation, wd)


def expert_backward_step(places, g, xi, share, gate_in, linear, wg, wu, wd, keep, send):
    where_to = block_places(EXPERT_ORDERS, places)
    squashed, silu, activation, expert_out = expert_step(gate_in, linear, wd, share)
    gate_grad = jnp.sum(g * expert_out, axis=1, keepdims=True)
    expert_grad = (share * g).astype(BF16)
    activation_grad = mm_nt(expert_grad, wd)
    gate_in_grad = (
        activation_grad * linear * squashed * (1.0 + gate_in * (1.0 - squashed))
    ).astype(BF16)
    linear_grad = (activation_grad * silu).astype(BF16)
    width = activation.shape[1]
    store_blocks(keep, send, mm_tn(xi, gate_in_grad), 0, where_to)
    store_blocks(keep, send, mm_tn(xi, linear_grad), width, where_to)
    store_blocks(keep, send, mm_tn(expert_grad, activation), 2 * width, where_to)
    return gate_grad, mm_nt(gate_in_grad, wg) + mm_nt(linear_grad, wu), expert_out


def expert_forward_kernel(
    x, own, other, gain, router, mask, wg, wu, wd,
    middle_out, xi_out, share_out, gate_out, linear_out, part_out,
):
    expert = pl.program_id(0)

    @pl.when(expert == 0)
    def _():
        expert_prologue(x, own, other, gain, router, mask, middle_out, xi_out, share_out)
        part_out[...] = jnp.zeros_like(part_out)

    share = column_of(share_out[...], lane_of(share_out.shape[0]), expert)
    xi = xi_out[...]
    gate_in = mm(xi, wg[...])
    linear = mm(xi, wu[...])
    gate_out[...] = gate_in
    linear_out[...] = linear
    part_out[...] += share * expert_step(gate_in, linear, wd[...], share)[3]


def expert_both_kernel(
    places, x, own, other, gain, router, mask, wg, wu, wd, cotangent,
    middle_out, xi_out, share_out, part_out, back_out, gate_grad_out, keep, send,
):
    expert = pl.program_id(0)
    lane = lane_of(share_out.shape[0])

    @pl.when(expert == 0)
    def _():
        expert_prologue(x, own, other, gain, router, mask, middle_out, xi_out, share_out)
        part_out[...] = jnp.zeros_like(part_out)
        back_out[...] = jnp.zeros_like(back_out)
        gate_grad_out[...] = jnp.zeros_like(gate_grad_out)

    share = column_of(share_out[...], lane, expert)
    xi = xi_out[...]
    gate_in = mm(xi, wg[...])
    linear = mm(xi, wu[...])
    gate_grad, back, expert_out = expert_backward_step(
        places, cotangent[...].astype(F32), xi, share, gate_in, linear, wg[...], wu[...],
        wd[...], keep, send,
    )
    part_out[...] += share * expert_out
    back_out[...] += back
    gate_grad_out[...] += jnp.where(lane == expert, gate_grad, 0.0)


def expert_backward_kernel(
    places, g_in, x, gain, own, other, xi_ref, share_ref, gate_ref, linear_ref, wg, wu, wd,
    *rest,
):
    g_out, gain_out, back_out, gate_grad_out, keep, send = rest[-6:]
    expert = pl.program_id(0)
    lane = lane_of(share_ref.shape[0])

    @pl.when(expert == 0)
    def _():
        stream = x[...]
        change, gain_row = norm_back(
            stream, row_factor(stream), gain[...].astype(F32), own[...] + other[...]
        )
        g_out[...] = g_in[...] + change
        gain_out[...] = jnp.broadcast_to(gain_row, gain_out.shape)
        back_out[...] = jnp.zeros_like(back_out)
        gate_grad_out[...] = jnp.zeros_like(gate_grad_out)

    share = column_of(share_ref[...], lane, expert)
    gate_grad, back, _ = expert_backward_step(
        places, g_out[...], xi_ref[...], share, gate_ref[...], linear_ref[...], wg[...],
        wu[...], wd[...], keep, send,
    )
    back_out[...] += back
    gate_grad_out[...] += jnp.where(lane == expert, gate_grad, 0.0)


def of_expert(layer, shape):
    return pl.BlockSpec((None, None, *shape), lambda e: (layer, e, 0, 0))


def each_expert(shape):
    return pl.BlockSpec((None, *shape), lambda e: (e, 0, 0))


def gradient_outs(rows, width):
    spec = pl.BlockSpec((rows, 3 * width), lambda e: (0, e))
    shape = ((rows, 3 * width * STREAMS), F32)
    return [(spec, shape)] * 2


SMEM = pl.BlockSpec(memory_space=pltpu.SMEM)
ANYWHERE = pl.BlockSpec(memory_space=pl.ANY)


def run_experts(kernel, name, ins, in_specs, outs, flops, nbytes, mib):
    return pl.pallas_call(
        kernel,
        grid=(STREAMS,),
        in_specs=in_specs,
        out_specs=[spec for spec, _ in outs],
        out_shape=[jax.ShapeDtypeStruct(*out) for _, out in outs],
        compiler_params=params(mib),
        cost_estimate=cost(flops, nbytes),
        name=name,
    )(*ins)


def expert_forward(layer, x, own, other, gain, router, mask, wg, wu, wd):
    length, features = x.shape
    width = wg.shape[3]
    big, low = ((length, features), F32), ((length, features), BF16)
    hidden = (each_expert((length, width)), ((STREAMS, length, width), F32))
    ins = [x, own, other, gain, router, mask, wg, wu, wd]
    in_specs = [whole(x.shape)] * 3 + [
        of_layer(layer, gain.shape[1:]),
        of_layer(layer, router.shape[1:]),
        of_layer(layer, mask.shape[1:]),
        *(of_expert(layer, w.shape[2:]) for w in (wg, wu, wd)),
    ]
    outs = [
        (whole(big[0]), big),
        (whole(low[0]), low),
        (whole((length, LANES)), ((length, LANES), F32)),
        hidden,
        hidden,
        (whole(big[0]), big),
    ]
    return run_experts(
        expert_forward_kernel, "experts_forward", ins, in_specs, outs, 8 << 30, 12 * MIB, 60
    )


def expert_both(layer, places, x, own, other, gain, router, mask, wg, wu, wd, cotangent):
    length, features = x.shape
    width = wg.shape[3]
    big, low = ((length, features), F32), ((length, features), BF16)
    table = (whole((length, LANES)), ((length, LANES), F32))
    ins = [places, x, own, other, gain, router, mask, wg, wu, wd, cotangent]
    in_specs = [SMEM] + [whole(x.shape)] * 3 + [
        of_layer(layer, gain.shape[1:]),
        of_layer(layer, router.shape[1:]),
        of_layer(layer, mask.shape[1:]),
        *(of_expert(layer, w.shape[2:]) for w in (wg, wu, wd)),
        whole(cotangent.shape),
    ]
    outs = [
        (whole(big[0]), big),
        (whole(low[0]), low),
        table,
        (whole(big[0]), big),
        (whole(big[0]), big),
        table,
        *gradient_outs(features // 2, width),
    ]
    return run_experts(
        expert_both_kernel, "experts_both", ins, in_specs, outs, 16 << 30, 30 * MIB, 60
    )


def expert_backward(
    layer, places, g, x, gain, own, other, xi, share, gate_in, linear, wg, wu, wd, after
):
    length, features = x.shape
    width = wg.shape[3]
    big = ((length, features), F32)
    table = (whole((length, LANES)), ((length, LANES), F32))
    hidden = each_expert((length, width))
    ins = [places, g, x, gain, own, other, xi, share, gate_in, linear, wg, wu, wd, *after]
    in_specs = [SMEM, whole(x.shape), whole(x.shape)] + [
        of_layer(layer + 1, gain.shape[1:]),
        whole(x.shape),
        whole(x.shape),
        whole(x.shape),
        whole(share.shape),
        hidden,
        hidden,
        *(of_expert(layer, w.shape[2:]) for w in (wg, wu, wd)),
        *([ANYWHERE] * len(after)),
    ]
    outs = [
        (whole(big[0]), big),
        (whole((8, features)), ((8, features), F32)),
        (whole(big[0]), big),
        table,
        *gradient_outs(features // 2, width),
    ]
    return run_experts(
        expert_backward_kernel, "experts_backward", ins, in_specs, outs, 16 << 30, 30 * MIB, 60
    )


def attention_backward_kernel(
    count, places, g, own, other, gate_own, gate_other, middle, xi, share, gain, router_rows,
    wo, mix, q, kk, vv, a, wq, wk, wv, cos, sin, seg_row, seg_column, x, late_gain, *rest,
):
    g_out, part_out, keep, send = rest[count : count + 4]
    rows_scratch = rest[-1]
    where_to = block_places(ATTENTION_ORDERS, places)
    length = middle.shape[0]
    lane = lane_of(length)
    shares = share[...]
    gate_grad = gate_own[...] + gate_other[...]
    pick = shares * (gate_grad - jnp.sum(shares * gate_grad, axis=1, keepdims=True))
    input_grad = own[...] + other[...]
    xi_full = xi[...].astype(F32)
    rows_scratch[...] = jnp.zeros_like(rows_scratch)
    for expert in range(STREAMS):
        logit_grad = column_of(pick, lane, expert)
        input_grad = input_grad + logit_grad * router_rows[expert : expert + 1, :]
        rows_scratch[expert : expert + 1, :] = jnp.sum(
            xi_full * logit_grad, axis=0, keepdims=True
        )
    mid = middle[...]
    change, gain_row = norm_back(mid, row_factor(mid), gain[...].astype(F32), input_grad)
    rows_scratch[4:5, :] = gain_row
    rows_scratch[6:7, :] = late_gain[0:1, :]
    gradient = g[...].astype(F32) + change
    g_out[...] = gradient
    output_grad = gradient.astype(BF16)
    mixture_grad = mm_nt(output_grad, wo[...]).astype(BF16)

    part = q.shape[1] // LANES
    cosine, sine = cos[...], sin[...]
    allowed = allowed_pairs(seg_row[...], seg_column[...])
    scale = HEAD_SIZE**-0.5
    low = lane < HEAD_SIZE
    a_full = a[...]
    query_grads, key_grads, value_grads = [], [], []
    for pair in range(part // 2):
        key_sides, value_sides = [], []
        for side in range(2):
            head = 2 * pair + side
            columns = slice(head * LANES, (head + 1) * LANES)
            stacked = stacked_pair(q[:, columns], lane)
            scores = jnp.where(allowed, mm_nt(stacked, kk[head]) * scale, EXCLUDED)
            shifted = jnp.exp(scores - jnp.max(scores, axis=-1, keepdims=True))
            probs = shifted / jnp.sum(shifted, axis=-1, keepdims=True)
            mix_grad = stacked_pair(mixture_grad[:, columns], lane)
            prob_grad = mm_nt(mix_grad, vv[head])
            inner = jnp.sum(probs * prob_grad, axis=-1, keepdims=True)
            score_grad = (probs * (prob_grad - inner)).astype(BF16)
            query = mm(score_grad, kk[head])
            query = jnp.where(low, query[:length], query[length:]) * scale
            query = query * cosine - partner(query, lane) * sine
            query_grads.append(query.astype(BF16))
            key = mm_tn(score_grad, stacked) * scale
            key_sides.append(key + pltpu.roll(key, HEAD_SIZE, 1))
            value = mm_tn(probs.astype(BF16), mix_grad)
            value_sides.append(value + pltpu.roll(value, HEAD_SIZE, 1))
        key = jnp.where(low, key_sides[0], key_sides[1])
        key_grads.append((key * cosine - partner(key, lane) * sine).astype(BF16))
        value_grads.append(jnp.where(low, value_sides[0], value_sides[1]).astype(BF16))
    query_grad = jnp.concatenate(query_grads, axis=1)
    key_grad = jnp.concatenate(key_grads, axis=1)
    value_grad = jnp.concatenate(value_grads, axis=1)
    attention_part = (
        mm_nt(query_grad, wq[...]) + mm_nt(key_grad, wk[...]) + mm_nt(value_grad, wv[...])
    )
    part_out[...] = attention_part
    stream = x[...]
    rows_scratch[5:6, :] = jnp.sum(
        attention_part * stream * row_factor(stream), axis=0, keepdims=True
    )

    column = 0
    for total in (
        jnp.transpose(rows_scratch[...]),
        mm_tn(a_full, query_grad),
        mm_tn(a_full, key_grad),
        mm_tn(a_full, value_grad),
        mm_tn(output_grad, mix[...]),
    ):
        store_blocks(keep, send, total, column, where_to)
        column += total.shape[1]


def attention_backward(
    layer, places, g, own, other, gate_own, gate_other, saved_experts, weights, saved, tables,
    segment, late_gain, after, held=(),
):
    middle, xi, share = saved_experts
    gain, router_rows, wo, wq, wk, wv = weights
    x, a, q, kk, vv, mix = saved
    length, features = middle.shape
    columns = SMALL + wq.shape[2] + wk.shape[2] + wv.shape[2] + wo.shape[1]
    ins = [
        places, g, own, other, gate_own, gate_other, middle, xi, share, gain, router_rows,
        wo, mix, q, kk, vv, a, wq, wk, wv, *tables, *segment, x, late_gain,
    ]
    layered = {9, 10, 11, 17, 18, 19}
    in_specs = [SMEM]
    for at, array in enumerate(ins[1:], 1):
        in_specs.append(of_layer(layer, array.shape[1:]) if at in layered else whole(array.shape))
    ins += [*after, *held]
    in_specs += [ANYWHERE] * len((*after, *held))
    outs = [
        ((length, features), F32),
        ((length, features), F32),
        ((features // 2, columns), F32),
        ((features // 2, columns), F32),
    ]
    out_specs = [whole(shape) for shape, _ in outs] + [ANYWHERE] * len(held)
    outs += [(array.shape, array.dtype) for array in held]
    return pl.pallas_call(
        functools.partial(attention_backward_kernel, len(after) + len(held)),
        grid=(1,),
        in_specs=in_specs,
        out_specs=out_specs,
        out_shape=[jax.ShapeDtypeStruct(*out) for out in outs],
        input_output_aliases={len(ins) - len(held) + at: 4 + at for at in range(len(held))},
        scratch_shapes=[pltpu.VMEM((LANES, features), F32)],
        compiler_params=params(60),
        cost_estimate=cost(16 << 30, 18 * MIB),
        name="attention_backward",
    )(*ins)


SWAP = ((0, 1), (1, 0))
RING = {"u": tuple((i, i ^ 1) for i in range(4)), "v": tuple((i, 3 - i) for i in range(4))}


def exchange(array):
    return lax.ppermute(array, "tensor", SWAP)


RING_AXES = ("dp_0", "dp_2", "dp_3")


def ring_pairs(orders, step):
    pairs = []
    for x in range(4):
        for z in range(4):
            for core in range(2):
                ring, kind = orders[core][step]
                at = x if ring == "x" else z
                to = at ^ 1 if kind == "u" else 3 - at
                there = (to, z) if ring == "x" else (x, to)
                pairs.append(((x * 4 + z) * 2 + core, (there[0] * 4 + there[1]) * 2 + core))
    return pairs


class Scatter:
    def __init__(self, keep, send, orders):
        self.parts = (keep, lax.ppermute(send, "dp_3", SWAP))
        self.orders = orders
        self.step = 0

    def halve(self):
        first, second = self.parts
        half = first.shape[0] // 2
        self.kept = first[:half] + second[:half]
        return first[half:] + second[half:]

    def move(self, send):
        if self.step < 4:
            moved = lax.ppermute(send, RING_AXES, ring_pairs(self.orders, self.step))
        else:
            moved = lax.ppermute(send, "dp_1", SWAP)
        self.parts = (self.kept, moved)
        self.step += 1

    def advance(self, count=1):
        for _ in range(count):
            self.move(self.halve())

    def finish(self):
        return self.parts[0] + self.parts[1]


def rope_tables(length):
    half = HEAD_SIZE // 2
    frequency = np.float32(THETA) ** (-2.0 * np.arange(half, dtype=np.float32) / HEAD_SIZE)
    angles = np.arange(length, dtype=np.float32)[:, None] * frequency[None].astype(np.float32)
    angles = angles.astype(np.float32)
    cosine = np.tile(np.cos(angles), (1, LANES // half)).astype(np.float32)
    sine = np.sin(angles)
    sine = np.tile(np.concatenate([-sine, sine], axis=1), (1, LANES // HEAD_SIZE))
    return jnp.asarray(cosine), jnp.asarray(sine.astype(np.float32))


def shards(
    tokens, segments, routes, norm_attention, query_weight, key_matrix, value_matrix,
    output_weight, norm_experts, router_weight, gate_weight, up_weight, down_weight, cotangent,
):
    length, features = tokens.shape
    experts = gate_weight.shape[1]
    hidden = gate_weight.shape[3]
    tables = rope_tables(length)
    segment = (segments.reshape(1, length), segments.reshape(length, 1))
    gain_attention = norm_attention[:, None, :]
    gain_experts = norm_experts[:, None, :]
    router = jnp.pad(router_weight, ((0, 0), (0, 0), (0, LANES - experts)))
    router_rows = jnp.pad(
        jnp.swapaxes(router_weight, 1, 2).astype(F32), ((0, 0), (0, 8 - experts), (0, 0))
    )
    mask = jnp.any(
        routes[..., None] == jnp.arange(LANES, dtype=jnp.int32), axis=2
    ).astype(F32)
    x_at, y_at, z_at = (lax.axis_index(name) for name in DP[:3])
    core = lax.axis_index("dp_3")

    def places_in(orders):
        one, two = (place(order, x_at, y_at, z_at) for order in orders)
        kept, sent = jnp.where(core == 0, one, two), jnp.where(core == 0, two, one)
        return jnp.stack([kept, sent, core]).astype(jnp.int32)

    expert_places, attention_places = places_in(EXPERT_ORDERS), places_in(ATTENTION_ORDERS)

    attention_weights = (gain_attention, query_weight, key_matrix, value_matrix, output_weight)
    expert_weights = (gate_weight, up_weight, down_weight)
    back_weights = (
        gain_experts, router_rows, output_weight, query_weight, key_matrix, value_matrix,
    )

    x1, *saved1, part = attention_forward(0, [tokens], attention_weights, tables, segment)
    middle1, xi1, share1, gate1, linear1, part = expert_forward(
        0, x1, part, exchange(part), gain_experts, router, mask, *expert_weights
    )
    x2, *saved2, part = attention_forward(
        1, [middle1, part, exchange(part)], attention_weights, tables, segment
    )
    middle2, xi2, share2, last, back, gate_grad, keep, send = expert_both(
        1, expert_places, x2, part, exchange(part), gain_experts, router, mask, *expert_weights,
        cotangent,
    )
    sum_e2 = Scatter(keep, send, EXPERT_ORDERS)
    sends = [sum_e2.halve()]
    other, gate_other = exchange(back), exchange(gate_grad)
    no_gain = jnp.zeros((8, features), F32)
    sum_e2.move(sends[0])
    g2, part, keep, send = attention_backward(
        1, attention_places, cotangent, back, other, gate_grad, gate_other,
        (middle2, xi2, share2), back_weights, (x2, *saved2), tables, segment, no_gain, sends,
    )
    sum_a2 = Scatter(keep, send, ATTENTION_ORDERS)
    sends = [sum_e2.halve(), sum_a2.halve()]
    other = exchange(part)
    sum_e2.move(sends[0])
    sum_a2.move(sends[1])
    g1, late_gain, back, gate_grad, keep, send = expert_backward(
        0, expert_places, g2, x2, gain_attention, part, other, xi1, share1, gate1,
        linear1, *expert_weights, sends,
    )
    sum_e1 = Scatter(keep, send, EXPERT_ORDERS)
    sends = [sum_e2.halve(), sum_a2.halve(), sum_e1.halve()]
    other, gate_other = exchange(back), exchange(gate_grad)
    sum_e2.move(sends[0])
    sum_a2.move(sends[1])
    sum_e1.move(sends[2])
    g0, part, keep, send, last = attention_backward(
        0, attention_places, g1, back, other, gate_grad, gate_other,
        (middle1, xi1, share1), back_weights, (x1, *saved1), tables, segment, late_gain,
        sends, (last,),
    )
    sum_a1 = Scatter(keep, send, ATTENTION_ORDERS)
    sum_e1.advance(2)
    sum_a1.advance(2)
    blocks = []
    for one, two in ((sum_a1, sum_a2), (sum_e1, sum_e2)):
        one.parts = tuple(
            jnp.stack([one.parts[at], two.parts[at]], axis=1) for at in range(2)
        )
        one.advance(5 - one.step)
        blocks.append(one.finish())
    gain = norm_attention[0].astype(F32)
    change, _ = norm_back(x1, row_factor(x1), gain, part + exchange(part))
    gradient = g0 + change
    output = (middle2 + (last + exchange(last))).astype(BF16)

    def layers_first(block):
        return jnp.swapaxes(block, 0, 1)

    attention_sums, expert_sums = (layers_first(block) for block in blocks)
    bounds = np.cumsum(
        [0, SMALL, query_weight.shape[2], key_matrix.shape[2], value_matrix.shape[2],
         output_weight.shape[1]]
    )
    attention_sums = [attention_sums[..., a:b] for a, b in zip(bounds[:-1], bounds[1:])]
    expert_sums = expert_sums.reshape(*expert_sums.shape[:2], experts, 3, hidden)
    expert_sums = [jnp.swapaxes(expert_sums[:, :, :, kind], 1, 2) for kind in range(3)]
    small = attention_sums[0]
    attention_gain = small[:, :, 5]
    attention_gain = attention_gain + exchange(attention_gain)
    return (
        output,
        gradient,
        attention_gain,
        *attention_sums[1:4],
        jnp.swapaxes(attention_sums[4], 1, 2),
        small[:, :, 4],
        small[:, :, :experts],
        expert_sums[0],
        expert_sums[1],
        jnp.swapaxes(expert_sums[2], 2, 3),
    )


def solution(mesh):
    torus = Mesh(
        mesh.devices.reshape(*DP_SIZES, mesh.shape["tensor"]), (*DP, "tensor")
    )
    rows, copied, last = P(DP, None), P(), P(None, None, "tensor")
    in_specs = (
        rows, rows, P(None, DP, None), copied, last, last, last, P(None, "tensor", None),
        copied, copied, P(None, None, None, "tensor"), P(None, None, None, "tensor"),
        P(None, None, "tensor", None), rows,
    )
    out_specs = (
        rows, rows, P(None, DP), P(None, DP, "tensor"), P(None, DP, "tensor"),
        P(None, DP, "tensor"), P(None, "tensor", DP), P(None, DP), P(None, DP, None),
        P(None, None, DP, "tensor"), P(None, None, DP, "tensor"), P(None, None, "tensor", DP),
    )
    return jax.shard_map(
        shards, mesh=torus, in_specs=in_specs, out_specs=out_specs, check_vma=False
    )
```

```python
import functools

import jax
import jax.numpy as jnp
import numpy as np
from jax import lax
from jax.experimental import pallas as pl
from jax.experimental.pallas import tpu as pltpu
from jax.sharding import Mesh
from jax.sharding import PartitionSpec as P

HEAD_SIZE = 64
LANES = 128
STREAMS = 4
SMALL = 128
DP = ("dp_0", "dp_1", "dp_2", "dp_3")
DP_SIZES = (4, 2, 4, 2)
EPSILON = 1e-06
THETA = 10000.0
EXCLUDED = -1e30
F32 = jnp.float32
BF16 = jnp.bfloat16
MIB = 1024 * 1024

EXPERT_ORDERS = (
    (("x", "u"), ("z", "u"), ("z", "v"), ("x", "v")),
    (("z", "v"), ("x", "v"), ("x", "u"), ("z", "u")),
)
ATTENTION_ORDERS = (
    (("z", "v"), ("x", "v"), ("x", "u"), ("z", "u")),
    (("x", "u"), ("z", "u"), ("z", "v"), ("x", "v")),
)


def swapped(order):
    return (order[1], order[0], *order[2:])


def pair_bit(index, kind):
    high = index // 2
    if kind == "v":
        return high
    return high ^ (index % 2)


def ring_place(order, x, z):
    at = 0
    for ring, kind in order:
        at = at * 2 + pair_bit(x if ring == "x" else z, kind)
    return at


def place(order, x, yh, z):
    return ring_place(order, x, z) * 2 + yh


def mm(a, b):
    return lax.dot_general(a, b, (((1,), (0,)), ((), ())), preferred_element_type=F32)


def mm_nt(a, b):
    return lax.dot_general(a, b, (((1,), (1,)), ((), ())), preferred_element_type=F32)


def mm_tn(a, b):
    return lax.dot_general(a, b, (((0,), (0,)), ((), ())), preferred_element_type=F32)


def row_factor(stream):
    return lax.rsqrt(jnp.mean(stream * stream, axis=-1, keepdims=True) + EPSILON)


def norm_back(stream, factor, gain, gradient):
    weighted = gradient * gain
    inner = jnp.sum(weighted * stream, axis=-1, keepdims=True) * (1.0 / stream.shape[-1])
    change = factor * weighted - stream * (factor * factor * factor) * inner
    return change, jnp.sum(gradient * stream * factor, axis=0, keepdims=True)


def lane_of(rows):
    return lax.broadcasted_iota(jnp.int32, (rows, LANES), 1)


def partner(block, lane):
    back = pltpu.roll(block, LANES - HEAD_SIZE // 2, 1)
    ahead = pltpu.roll(block, HEAD_SIZE // 2, 1)
    return jnp.where(lane % HEAD_SIZE < HEAD_SIZE // 2, back, ahead)


def both_heads(block, lane):
    rolled = pltpu.roll(block, HEAD_SIZE, 1)
    low = lane < HEAD_SIZE
    return jnp.where(low, block, rolled), jnp.where(low, rolled, block)


def stacked_pair(block, lane):
    zero = jnp.zeros_like(block)
    low = lane < HEAD_SIZE
    return jnp.concatenate(
        [jnp.where(low, block, zero), jnp.where(low, zero, block)], axis=0
    )


def allowed_pairs(seg_row, seg_column):
    length = seg_column.shape[0]
    rows = lax.broadcasted_iota(jnp.int32, (length, length), 0)
    columns = lax.broadcasted_iota(jnp.int32, (length, length), 1)
    allowed = (columns <= rows) & (seg_column == seg_row)
    bias = jnp.where(allowed, 0.0, 1.0)
    return jnp.concatenate([bias, bias], axis=0) < 0.5


def block_places(orders, places, later=False):
    core = places[4]
    found = []
    for block in range(32):
        x, yh, z = block // 8, (block // 4) % 2, block % 4
        one, two = (
            jnp.where(later, place(swapped(order), x, yh, z), place(order, x, yh, z))
            for order in orders
        )
        own = jnp.where(later, places[2], places[0])
        far = jnp.where(later, places[3], places[1])
        found.append((jnp.where(core == 0, one, two) ^ own, jnp.where(core == 0, two, one) ^ far))
    return core, found


def store_blocks(keep_ref, send_ref, value, column, where_to):
    core, found = where_to
    rows = value.shape[0] // 64
    columns = slice(column, column + value.shape[1])
    for block, (kept, sent) in enumerate(found):
        first = value[2 * block * rows : (2 * block + 1) * rows]
        second = value[(2 * block + 1) * rows : (2 * block + 2) * rows]
        keep_ref[pl.ds(pl.multiple_of(kept * rows, rows), rows), columns] = jnp.where(
            core == 0, first, second
        )
        send_ref[pl.ds(pl.multiple_of(sent * rows, rows), rows), columns] = jnp.where(
            core == 0, second, first
        )


def attend(a, wq, wk, wv, q_out, kk_out, vv_out, mix_out, cosine, sine, allowed):
    length = a.shape[0]
    lane = lane_of(length)
    q = mm(a, wq)
    k = mm(a, wk)
    v = mm(a, wv)
    scale = HEAD_SIZE**-0.5
    for pair in range(k.shape[1] // LANES):
        at = slice(pair * LANES, (pair + 1) * LANES)
        k_block = k[:, at] * cosine + partner(k[:, at], lane) * sine
        k_twice = both_heads(k_block, lane)
        v_twice = both_heads(v[:, at], lane)
        for side in range(2):
            head = 2 * pair + side
            columns = slice(head * LANES, (head + 1) * LANES)
            kk = k_twice[side].astype(BF16)
            vv = v_twice[side].astype(BF16)
            kk_out[head] = kk
            vv_out[head] = vv
            q_block = q[:, columns]
            q_block = (q_block * cosine + partner(q_block, lane) * sine).astype(BF16)
            q_out[:, columns] = q_block
            scores = mm_nt(stacked_pair(q_block, lane), kk) * scale
            scores = jnp.where(allowed, scores, EXCLUDED)
            shifted = jnp.exp(scores - jnp.max(scores, axis=-1, keepdims=True))
            probs = (shifted / jnp.sum(shifted, axis=-1, keepdims=True)).astype(BF16)
            mixed = mm(probs, vv)
            mix_out[:, columns] = jnp.where(
                lane < HEAD_SIZE, mixed[:length], mixed[length:]
            ).astype(BF16)


def halves_of(weights):
    depth = 2 * weights.shape[0] // 3
    quarter = depth // 4
    return (
        weights.at[:depth, : 2 * quarter],
        weights.at[:depth, 2 * quarter : 3 * quarter],
        weights.at[:depth, 3 * quarter :],
        weights.at[depth:, :],
    )


def unpack_gathered(places, gathered, weights):
    core = places[4]
    rows = gathered[0].shape[0] // 8
    width = gathered[0].shape[1]
    top, low = 2 * rows // 3, rows // 3
    for piece in range(32):
        x, z, side = piece // 8, (piece // 2) % 4, piece % 2
        for part in range(2):
            order = EXPERT_ORDERS[side] if part == 0 else swapped(EXPERT_ORDERS[side])
            at = ring_place(order, x, z) ^ places[2 * part + side]
            rows_at = pl.ds(pl.multiple_of((at & 7) * rows, rows), rows)
            columns = slice(part * width, (part + 1) * width)
            first, second, far_first, far_second = (
                gathered[2 * pair + part][rows_at, :] for pair in range(4)
            )
            near, far = jnp.where(at < 8, first, second), jnp.where(at < 8, far_first, far_second)
            value = jnp.where(core == side, near, far).astype(BF16)
            weights[piece * top : (piece + 1) * top, columns] = value[:top]
            start = 32 * top + piece * low
            weights[start : start + low, columns] = value[top:]


def attention_forward_kernel(count, full, *refs):
    parts = refs[:count]
    (gain, wq, wk, wv, wo, cos, sin, seg_row, seg_column) = refs[count : count + 9]
    refs = refs[count + 9 :]
    if full:
        places, gathered = refs[0], refs[1:9]
        refs = refs[9:]
    (x_out, a_out, q_out, kk_out, vv_out, mix_out, part_out) = refs[:7]
    x = parts[0][...].astype(F32)
    if count == 3:
        x = x + (parts[1][...] + parts[2][...])
    x_out[...] = x
    a = (x * row_factor(x) * gain[...].astype(F32)).astype(BF16)
    a_out[...] = a
    common = (cos[...], sin[...], allowed_pairs(seg_row[...], seg_column[...]))
    attend(a, wq[...], wk[...], wv[...], q_out, kk_out, vv_out, mix_out, *common)
    part_out[...] = mm(mix_out[...], wo[...])
    if full:
        q_other, kk_other, vv_other, part_other, weights, mix_other = refs[7:]
        unpack_gathered(places, gathered, weights)
        wq, wk, wv, wo = halves_of(weights)
        attend(a, wq[...], wk[...], wv[...], q_other, kk_other, vv_other, mix_other, *common)
        part_other[...] = mm(mix_other[...], wo[...])


ONCE = pl.Buffered(1)
SMEM = pl.BlockSpec(memory_space=pltpu.SMEM)
ANYWHERE = pl.BlockSpec(memory_space=pl.ANY)


def whole(shape):
    return pl.BlockSpec(shape, lambda i: (0,) * len(shape), pipeline_mode=ONCE)


def of_layer(layer, shape):
    return pl.BlockSpec(
        (None, *shape), lambda i: (layer,) + (0,) * len(shape), pipeline_mode=ONCE
    )


def params(mib):
    return pltpu.CompilerParams(
        vmem_limit_bytes=mib * MIB, dimension_semantics=("arbitrary",)
    )


def cost(flops, nbytes):
    return pl.CostEstimate(flops=flops, bytes_accessed=nbytes, transcendentals=0)


def attention_forward(layer, parts, weights, tables, segment, gathered=()):
    gain, wq, wk, wv, wo = weights
    length, features = parts[0].shape
    q_width, k_width = wq.shape[2], wk.shape[2]
    heads = 2 * k_width // LANES
    ins = [*parts, gain, wq, wk, wv, wo, *tables, *segment]
    in_specs = [whole(part.shape) for part in parts]
    in_specs += [of_layer(layer, w.shape[1:]) for w in (gain, wq, wk, wv, wo)]
    in_specs += [whole(t.shape) for t in (*tables, *segment)]
    outs = [
        ((length, features), F32),
        ((length, features), BF16),
        ((length, q_width), BF16),
        ((heads, length, LANES), BF16),
        ((heads, length, LANES), BF16),
        ((length, q_width), BF16),
        ((length, features), F32),
    ]
    scratch = []
    if gathered:
        ins += gathered
        in_specs += [SMEM, *(whole(array.shape) for array in gathered[1:])]
        outs += [outs[2], outs[3], outs[4], outs[6], ((4 * gathered[1].shape[0], features), BF16)]
        scratch = [pltpu.VMEM((length, q_width), BF16)]
    return pl.pallas_call(
        functools.partial(attention_forward_kernel, len(parts), bool(gathered)),
        grid=(1,),
        scratch_shapes=scratch,
        in_specs=in_specs,
        out_specs=[whole(shape) for shape, _ in outs],
        out_shape=[jax.ShapeDtypeStruct(*out) for out in outs],
        compiler_params=params(60),
        cost_estimate=cost(6 << 30, 8 * MIB),
        name="attention_forward",
    )(*ins)


def column_of(table, lane, index):
    return jnp.sum(jnp.where(lane == index, table, 0.0), axis=1, keepdims=True)


def expert_prologue(x, own, other, gain, router, mask, middle_out, xi_out, share_out):
    middle = x[...] + (own[...] + other[...])
    middle_out[...] = middle
    xi = (middle * row_factor(middle) * gain[...].astype(F32)).astype(BF16)
    xi_out[...] = xi
    logits = mm(xi, router[...])
    chosen = mask[...] > 0.5
    logits = jnp.where(chosen, logits, EXCLUDED)
    shifted = jnp.exp(logits - jnp.max(logits, axis=-1, keepdims=True))
    shifted = jnp.where(chosen, shifted, 0.0)
    share_out[...] = shifted / jnp.sum(shifted, axis=-1, keepdims=True)


def expert_step(gate_in, linear, wd, share):
    squashed = 1.0 / (1.0 + jnp.exp(-gate_in))
    silu = gate_in * squashed
    activation = (silu * linear).astype(BF16)
    return squashed, silu, activation, mm(activation, wd)


def expert_backward_step(places, g, xi, share, gate_in, linear, wg, wu, wd, keep, send):
    where_to = block_places(EXPERT_ORDERS, places, pl.program_id(0) >= STREAMS // 2)
    squashed, silu, activation, expert_out = expert_step(gate_in, linear, wd, share)
    gate_grad = jnp.sum(g * expert_out, axis=1, keepdims=True)
    expert_grad = (share * g).astype(BF16)
    activation_grad = mm_nt(expert_grad, wd)
    gate_in_grad = (
        activation_grad * linear * squashed * (1.0 + gate_in * (1.0 - squashed))
    ).astype(BF16)
    linear_grad = (activation_grad * silu).astype(BF16)
    width = activation.shape[1]
    store_blocks(keep, send, mm_tn(xi, gate_in_grad), 0, where_to)
    store_blocks(keep, send, mm_tn(xi, linear_grad), width, where_to)
    store_blocks(keep, send, mm_tn(expert_grad, activation), 2 * width, where_to)
    return gate_grad, mm_nt(gate_in_grad, wg) + mm_nt(linear_grad, wu), expert_out


def expert_forward_kernel(
    x, own, other, gain, router, mask, wg, wu, wd,
    middle_out, xi_out, share_out, gate_out, linear_out, part_out,
):
    expert = pl.program_id(0)

    @pl.when(expert == 0)
    def _():
        expert_prologue(x, own, other, gain, router, mask, middle_out, xi_out, share_out)
        part_out[...] = jnp.zeros_like(part_out)

    share = column_of(share_out[...], lane_of(share_out.shape[0]), expert)
    xi = xi_out[...]
    gate_in = mm(xi, wg[...])
    linear = mm(xi, wu[...])
    gate_out[...] = gate_in
    linear_out[...] = linear
    part_out[...] += share * expert_step(gate_in, linear, wd[...], share)[3]


def expert_both_kernel(
    places, x, own, other, gain, router, mask, wg, wu, wd, cotangent,
    middle_out, xi_out, share_out, part_out, back_out, gate_grad_out, keep, send,
):
    expert = pl.program_id(0)
    lane = lane_of(share_out.shape[0])

    @pl.when(expert == 0)
    def _():
        expert_prologue(x, own, other, gain, router, mask, middle_out, xi_out, share_out)
        part_out[...] = jnp.zeros_like(part_out)
        back_out[...] = jnp.zeros_like(back_out)
        gate_grad_out[...] = jnp.zeros_like(gate_grad_out)

    share = column_of(share_out[...], lane, expert)
    xi = xi_out[...]
    gate_in = mm(xi, wg[...])
    linear = mm(xi, wu[...])
    gate_grad, back, expert_out = expert_backward_step(
        places, cotangent[...].astype(F32), xi, share, gate_in, linear, wg[...], wu[...],
        wd[...], keep, send,
    )
    part_out[...] += share * expert_out
    back_out[...] += back
    gate_grad_out[...] += jnp.where(lane == expert, gate_grad, 0.0)


def expert_backward_kernel(
    places, g_in, x, gain, own, other, xi_ref, share_ref, gate_ref, linear_ref, wg, wu, wd,
    *rest,
):
    g_out, gain_out, back_out, gate_grad_out, keep, send = rest[-6:]
    expert = pl.program_id(0)
    lane = lane_of(share_ref.shape[0])

    @pl.when(expert == 0)
    def _():
        stream = x[...]
        change, gain_row = norm_back(
            stream, row_factor(stream), gain[...].astype(F32), own[...] + other[...]
        )
        g_out[...] = g_in[...] + change
        gain_out[...] = jnp.broadcast_to(gain_row, gain_out.shape)
        back_out[...] = jnp.zeros_like(back_out)
        gate_grad_out[...] = jnp.zeros_like(gate_grad_out)

    share = column_of(share_ref[...], lane, expert)
    gate_grad, back, _ = expert_backward_step(
        places, g_out[...], xi_ref[...], share, gate_ref[...], linear_ref[...], wg[...],
        wu[...], wd[...], keep, send,
    )
    back_out[...] += back
    gate_grad_out[...] += jnp.where(lane == expert, gate_grad, 0.0)


def of_expert(layer, shape):
    return pl.BlockSpec((None, None, *shape), lambda e: (layer, e, 0, 0))


def each_expert(shape):
    return pl.BlockSpec((None, *shape), lambda e: (e, 0, 0))


def gradient_outs(rows, width):
    spec = pl.BlockSpec((rows, 3 * width), lambda e: (0, e))
    shape = ((rows, 3 * width * STREAMS), F32)
    return [(spec, shape)] * 2


def run_experts(kernel, name, ins, in_specs, outs, flops, nbytes, mib):
    return pl.pallas_call(
        kernel,
        grid=(STREAMS,),
        in_specs=in_specs,
        out_specs=[spec for spec, _ in outs],
        out_shape=[jax.ShapeDtypeStruct(*out) for _, out in outs],
        compiler_params=params(mib),
        cost_estimate=cost(flops, nbytes),
        name=name,
    )(*ins)


def expert_forward(layer, x, own, other, gain, router, mask, wg, wu, wd):
    length, features = x.shape
    width = wg.shape[3]
    big, low = ((length, features), F32), ((length, features), BF16)
    hidden = (each_expert((length, width)), ((STREAMS, length, width), F32))
    ins = [x, own, other, gain, router, mask, wg, wu, wd]
    in_specs = [whole(x.shape)] * 3 + [
        of_layer(layer, gain.shape[1:]),
        of_layer(layer, router.shape[1:]),
        of_layer(layer, mask.shape[1:]),
        *(of_expert(layer, w.shape[2:]) for w in (wg, wu, wd)),
    ]
    outs = [
        (whole(big[0]), big),
        (whole(low[0]), low),
        (whole((length, LANES)), ((length, LANES), F32)),
        hidden,
        hidden,
        (whole(big[0]), big),
    ]
    return run_experts(
        expert_forward_kernel, "experts_forward", ins, in_specs, outs, 8 << 30, 12 * MIB, 60
    )


def expert_both(layer, places, x, own, other, gain, router, mask, wg, wu, wd, cotangent):
    length, features = x.shape
    width = wg.shape[3]
    big, low = ((length, features), F32), ((length, features), BF16)
    table = (whole((length, LANES)), ((length, LANES), F32))
    ins = [places, x, own, other, gain, router, mask, wg, wu, wd, cotangent]
    in_specs = [SMEM] + [whole(x.shape)] * 3 + [
        of_layer(layer, gain.shape[1:]),
        of_layer(layer, router.shape[1:]),
        of_layer(layer, mask.shape[1:]),
        *(of_expert(layer, w.shape[2:]) for w in (wg, wu, wd)),
        whole(cotangent.shape),
    ]
    outs = [
        (whole(big[0]), big),
        (whole(low[0]), low),
        table,
        (whole(big[0]), big),
        (whole(big[0]), big),
        table,
        *gradient_outs(features // 2, width),
    ]
    return run_experts(
        expert_both_kernel, "experts_both", ins, in_specs, outs, 16 << 30, 30 * MIB, 60
    )


def expert_backward(
    layer, places, g, x, gain, own, other, xi, share, gate_in, linear, wg, wu, wd, after
):
    length, features = x.shape
    width = wg.shape[3]
    big = ((length, features), F32)
    table = (whole((length, LANES)), ((length, LANES), F32))
    hidden = each_expert((length, width))
    ins = [places, g, x, gain, own, other, xi, share, gate_in, linear, wg, wu, wd, *after]
    in_specs = [SMEM, whole(x.shape), whole(x.shape)] + [
        of_layer(layer + 1, gain.shape[1:]),
        whole(x.shape),
        whole(x.shape),
        whole(x.shape),
        whole(share.shape),
        hidden,
        hidden,
        *(of_expert(layer, w.shape[2:]) for w in (wg, wu, wd)),
        *([ANYWHERE] * len(after)),
    ]
    outs = [
        (whole(big[0]), big),
        (whole((8, features)), ((8, features), F32)),
        (whole(big[0]), big),
        table,
        *gradient_outs(features // 2, width),
    ]
    return run_experts(
        expert_backward_kernel, "experts_backward", ins, in_specs, outs, 4 << 30, 30 * MIB, 60
    )


def attend_backward(mixture_grad, q, kk, vv, cosine, sine, allowed):
    length = mixture_grad.shape[0]
    lane = lane_of(length)
    low = lane < HEAD_SIZE
    scale = HEAD_SIZE**-0.5
    query_grads, key_grads, value_grads = [], [], []
    for pair in range(q.shape[1] // LANES // 2):
        key_sides, value_sides = [], []
        for side in range(2):
            head = 2 * pair + side
            columns = slice(head * LANES, (head + 1) * LANES)
            stacked = stacked_pair(q[:, columns], lane)
            scores = jnp.where(allowed, mm_nt(stacked, kk[head]) * scale, EXCLUDED)
            shifted = jnp.exp(scores - jnp.max(scores, axis=-1, keepdims=True))
            probs = shifted / jnp.sum(shifted, axis=-1, keepdims=True)
            mix_grad = stacked_pair(mixture_grad[:, columns], lane)
            prob_grad = mm_nt(mix_grad, vv[head])
            inner = jnp.sum(probs * prob_grad, axis=-1, keepdims=True)
            score_grad = (probs * (prob_grad - inner)).astype(BF16)
            query = mm(score_grad, kk[head])
            query = jnp.where(low, query[:length], query[length:]) * scale
            query = query * cosine - partner(query, lane) * sine
            query_grads.append(query.astype(BF16))
            key = mm_tn(score_grad, stacked) * scale
            key_sides.append(key + pltpu.roll(key, HEAD_SIZE, 1))
            value = mm_tn(probs.astype(BF16), mix_grad)
            value_sides.append(value + pltpu.roll(value, HEAD_SIZE, 1))
        key = jnp.where(low, key_sides[0], key_sides[1])
        key_grads.append((key * cosine - partner(key, lane) * sine).astype(BF16))
        value_grads.append(jnp.where(low, value_sides[0], value_sides[1]).astype(BF16))
    return tuple(
        jnp.concatenate(grads, axis=1) for grads in (query_grads, key_grads, value_grads)
    )


def attention_backward_kernel(
    count, full, orders, places, g, own, other, gate_own, gate_other, middle, xi, share, gain, router_rows,
    wo, mix, q, kk, vv, a, wq, wk, wv, cos, sin, seg_row, seg_column, x, late_gain, *rest,
):
    if full:
        q_other, kk_other, vv_other, weights = rest[:4]
        part_other = rest[-2]
        rest = rest[4:]
    g_out, part_out, keep, send = rest[count : count + 4]
    rows_scratch = rest[-1]
    where_to = block_places(orders, places)
    length = middle.shape[0]
    lane = lane_of(length)
    shares = share[...]
    gate_grad = gate_own[...] + gate_other[...]
    pick = shares * (gate_grad - jnp.sum(shares * gate_grad, axis=1, keepdims=True))
    input_grad = own[...] + other[...]
    xi_full = xi[...].astype(F32)
    rows_scratch[...] = jnp.zeros_like(rows_scratch)
    for expert in range(STREAMS):
        logit_grad = column_of(pick, lane, expert)
        input_grad = input_grad + logit_grad * router_rows[expert : expert + 1, :]
        rows_scratch[expert : expert + 1, :] = jnp.sum(
            xi_full * logit_grad, axis=0, keepdims=True
        )
    mid = middle[...]
    change, gain_row = norm_back(mid, row_factor(mid), gain[...].astype(F32), input_grad)
    rows_scratch[4:5, :] = gain_row
    rows_scratch[6:7, :] = late_gain[0:1, :]
    gradient = g[...].astype(F32) + change
    g_out[...] = gradient
    output_grad = gradient.astype(BF16)
    common = (cos[...], sin[...], allowed_pairs(seg_row[...], seg_column[...]))

    def half(output_weight, weights, *saved):
        mixture_grad = mm_nt(output_grad, output_weight[...]).astype(BF16)
        grads = attend_backward(mixture_grad, *saved, *common)
        part = sum(mm_nt(grad, weight[...]) for grad, weight in zip(grads, weights))
        return grads, part

    if full:
        wq_other, wk_other, wv_other, wo_other = halves_of(weights)
        part_other[...] = half(
            wo_other, (wq_other, wk_other, wv_other), q_other, kk_other, vv_other
        )[1]
    grads, attention_part = half(wo, (wq, wk, wv), q, kk, vv)
    part_out[...] = attention_part
    stream = x[...]
    rows_scratch[5:6, :] = jnp.sum(
        attention_part * stream * row_factor(stream), axis=0, keepdims=True
    )
    a_full = a[...]
    column = 0
    for total in (
        jnp.transpose(rows_scratch[...]),
        *(mm_tn(a_full, grad) for grad in grads),
        mm_tn(output_grad, mix[...]),
    ):
        store_blocks(keep, send, total, column, where_to)
        column += total.shape[1]


def attention_backward(
    layer, orders, places, g, own, other, gate_own, gate_other, saved_experts, weights, saved,
    tables, segment, late_gain, after, others=(),
):
    middle, xi, share = saved_experts
    gain, router_rows, wo, wq, wk, wv = weights
    x, a, q, kk, vv, mix = saved
    length, features = middle.shape
    columns = SMALL + wq.shape[2] + wk.shape[2] + wv.shape[2] + wo.shape[1]
    ins = [
        places, g, own, other, gate_own, gate_other, middle, xi, share, gain, router_rows,
        wo, mix, q, kk, vv, a, wq, wk, wv, *tables, *segment, x, late_gain,
    ]
    layered = {9, 10, 11, 17, 18, 19}
    in_specs = [SMEM]
    for at, array in enumerate(ins[1:], 1):
        in_specs.append(of_layer(layer, array.shape[1:]) if at in layered else whole(array.shape))
    ins += [*others, *after]
    in_specs += [whole(array.shape) for array in others]
    in_specs += [ANYWHERE] * len(after)
    outs = [
        ((length, features), F32),
        ((length, features), F32),
        ((features // 2, columns), F32),
        ((features // 2, columns), F32),
    ]
    if others:
        outs.append(((length, features), F32))
    return pl.pallas_call(
        functools.partial(
            attention_backward_kernel, len(after), bool(others), orders
        ),
        grid=(1,),
        in_specs=in_specs,
        out_specs=[whole(shape) for shape, _ in outs],
        out_shape=[jax.ShapeDtypeStruct(*out) for out in outs],
        scratch_shapes=[pltpu.VMEM((LANES, features), F32)],
        compiler_params=params(60),
        cost_estimate=cost(16 << 30, 18 * MIB),
        name="attention_backward",
    )(*ins)


SWAP = ((0, 1), (1, 0))
RING = {"u": tuple((i, i ^ 1) for i in range(4)), "v": tuple((i, 3 - i) for i in range(4))}


def exchange(array):
    return lax.ppermute(array, "tensor", SWAP)


RING_AXES = ("dp_0", "dp_2", "dp_3")


def ring_pairs(orders, step):
    pairs = []
    for x in range(4):
        for z in range(4):
            for core in range(2):
                ring, kind = orders[core][step]
                at = x if ring == "x" else z
                to = at ^ 1 if kind == "u" else 3 - at
                there = (to, z) if ring == "x" else (x, to)
                pairs.append(((x * 4 + z) * 2 + core, (there[0] * 4 + there[1]) * 2 + core))
    return pairs


class Scatter:
    def __init__(self, keep, send, *orders):
        received = lax.ppermute(send, "dp_3", SWAP)
        width = keep.shape[1] // len(orders)
        self.orders = orders
        self.parts = [
            [array[:, at * width : (at + 1) * width] for array in (keep, received)]
            for at in range(len(orders))
        ]
        self.step = 0

    def halve(self):
        half = self.parts[0][0].shape[0] // 2
        self.kept = [first[:half] + second[:half] for first, second in self.parts]
        return [first[half:] + second[half:] for first, second in self.parts]

    def move(self, sends):
        moved = [
            lax.ppermute(send, RING_AXES, ring_pairs(orders, self.step))
            for send, orders in zip(sends, self.orders)
        ]
        self.parts = [list(pair) for pair in zip(self.kept, moved)]
        self.step += 1

    def received(self):
        return [second for _, second in self.parts]

    def advance(self, count=1):
        for _ in range(count):
            self.move(self.halve())

    def join(self, other):
        self.parts = [
            [jnp.concatenate(pair, axis=1) for pair in zip(*both)]
            for both in zip(self.parts, other.parts)
        ]

    def finish(self):
        sends = jnp.concatenate(self.halve(), axis=-1)
        return jnp.concatenate(self.kept, axis=-1) + lax.ppermute(sends, "dp_1", SWAP)


class Gather:
    def __init__(self, weights, layer):
        x, z, core = (lax.axis_index(name) for name in RING_AXES)
        piece = (x * 4 + z) * 2 + core

        def rows_of(weight):
            rows = weight.shape[1] // 32
            return lax.dynamic_slice_in_dim(weight[layer], piece * rows, rows, 0).astype(F32)

        *inputs, output = (rows_of(weight) for weight in weights)
        self.piece = jnp.concatenate([jnp.concatenate(inputs, axis=1), output], axis=0)
        orders = [*EXPERT_ORDERS, *(swapped(order) for order in EXPERT_ORDERS)]
        places = [ring_place(order, x, z) for order in orders]
        self.places = jnp.stack([*places, core]).astype(jnp.int32)

        self.crossed = exchange(self.piece)

    def begin(self, after, received):
        held, *_ = behind([self.crossed], after)
        for step in (3, 2):
            moved = lax.ppermute(held, RING_AXES, ring_pairs(EXPERT_ORDERS, step))
            held = jnp.concatenate([held, moved], axis=0)
        half = held.shape[1] // 2
        self.held = behind([held[:, :half], held[:, half:]], received)
        self.moved = self.moves(self.held, 1)

    def moves(self, held, step):
        return [
            lax.ppermute(half, RING_AXES, ring_pairs(EXPERT_ORDERS, at))
            for half, at in zip(held, (step, 1 - step))
        ]

    def finish(self, after):
        held = behind(self.held, after)
        held = [jnp.concatenate(pair, axis=0) for pair in zip(held, self.moved)]
        near = [*held, *self.moves(held, 0)]
        return [self.places, *near, *(lax.ppermute(half, "dp_3", SWAP) for half in near)]


def behind(arrays, *after):
    return pl.pallas_call(
        lambda *refs: None,
        in_specs=[ANYWHERE] * (len(arrays) + len(after)),
        out_specs=[ANYWHERE] * len(arrays),
        out_shape=[jax.ShapeDtypeStruct(array.shape, array.dtype) for array in arrays],
        input_output_aliases={at: at for at in range(len(arrays))},
        name="behind",
    )(*arrays, *after)


def rope_tables(length):
    half = HEAD_SIZE // 2
    frequency = np.float32(THETA) ** (-2.0 * np.arange(half, dtype=np.float32) / HEAD_SIZE)
    angles = np.arange(length, dtype=np.float32)[:, None] * frequency[None].astype(np.float32)
    angles = angles.astype(np.float32)
    cosine = np.tile(np.cos(angles), (1, LANES // half)).astype(np.float32)
    sine = np.sin(angles)
    sine = np.tile(np.concatenate([-sine, sine], axis=1), (1, LANES // HEAD_SIZE))
    return jnp.asarray(cosine), jnp.asarray(sine.astype(np.float32))


def shards(
    tokens, segments, routes, norm_attention, query_weight, key_matrix, value_matrix,
    output_weight, norm_experts, router_weight, gate_weight, up_weight, down_weight, cotangent,
):
    length, features = tokens.shape
    experts = gate_weight.shape[1]
    hidden = gate_weight.shape[3]
    tables = rope_tables(length)
    segment = (segments.reshape(1, length), segments.reshape(length, 1))
    gain_attention = norm_attention[:, None, :]
    gain_experts = norm_experts[:, None, :]
    router = jnp.pad(router_weight, ((0, 0), (0, 0), (0, LANES - experts)))
    router_rows = jnp.pad(
        jnp.swapaxes(router_weight, 1, 2).astype(F32), ((0, 0), (0, 8 - experts), (0, 0))
    )
    mask = jnp.any(
        routes[..., None] == jnp.arange(LANES, dtype=jnp.int32), axis=2
    ).astype(F32)
    x_at, y_at, z_at = (lax.axis_index(name) for name in DP[:3])
    core = lax.axis_index("dp_3")

    def places_in(orders):
        found = []
        for which in (orders, [swapped(order) for order in orders]):
            one, two = (place(order, x_at, y_at, z_at) for order in which)
            found += [jnp.where(core == 0, one, two), jnp.where(core == 0, two, one)]
        return jnp.stack([*found, core]).astype(jnp.int32)

    expert_places = places_in(EXPERT_ORDERS)
    late_orders = tuple(swapped(order) for order in ATTENTION_ORDERS)

    attention_weights = (gain_attention, query_weight, key_matrix, value_matrix, output_weight)
    expert_weights = (gate_weight, up_weight, down_weight)
    back_weights = (
        gain_experts, router_rows, output_weight, query_weight, key_matrix, value_matrix,
    )

    others = Gather(attention_weights[1:], 1)
    x1, *saved1, part = attention_forward(0, [tokens], attention_weights, tables, segment)
    other = exchange(part)
    others.begin(part, other)
    middle1, xi1, share1, gate1, linear1, part = expert_forward(
        0, x1, part, other, gain_experts, router, mask, *expert_weights
    )
    x2, *saved2, part, q_other, kk_other, vv_other, part_other, weights_other = attention_forward(
        1, [middle1, part, exchange(part)], attention_weights, tables, segment,
        others.finish(part),
    )
    middle2, xi2, share2, last, back, gate_grad, keep, send = expert_both(
        1, expert_places, x2, part, part_other, gain_experts, router, mask, *expert_weights,
        cotangent,
    )
    both_orders = (EXPERT_ORDERS, tuple(swapped(order) for order in EXPERT_ORDERS))
    sum_e2 = Scatter(keep, send, *both_orders)
    other, gate_other = exchange(back), exchange(gate_grad)
    *sends, last = behind([*sum_e2.halve(), last], other)
    sum_e2.move(sends)
    last_other = exchange(last)
    no_gain = jnp.zeros((8, features), F32)
    g2, part, keep, send, part_other = attention_backward(
        1, late_orders, places_in(late_orders), cotangent, back, other, gate_grad, gate_other,
        (middle2, xi2, share2), back_weights, (x2, *saved2), tables, segment, no_gain, sends,
        (q_other, kk_other, vv_other, weights_other),
    )
    sum_a2 = Scatter(keep, send, late_orders)
    sends = sum_e2.halve()
    g1, late_gain, back, gate_grad, keep, send = expert_backward(
        0, expert_places, g2, x2, gain_attention, part, part_other, xi1, share1, gate1,
        linear1, *expert_weights, [*sends, last_other],
    )
    sum_e2.move(sends)
    sum_e1 = Scatter(keep, send, *both_orders)
    other, gate_other = exchange(back), exchange(gate_grad)
    sends_a, sends_e = sum_a2.halve(), sum_e1.halve()
    sum_a2.move(sends_a)
    sum_e1.move(sends_e)
    sends = sends_a + sends_e + sum_e2.received()
    g0, part, keep, send = attention_backward(
        0, ATTENTION_ORDERS, places_in(ATTENTION_ORDERS), g1, back, other, gate_grad, gate_other,
        (middle1, xi1, share1), back_weights, (x1, *saved1), tables, segment, late_gain,
        sends,
    )
    (send,) = behind([send], *sum_a2.received(), *sum_e1.received())
    sum_a1 = Scatter(keep, send, ATTENTION_ORDERS)
    sum_a1.advance()
    (other,) = behind([exchange(part)], *sum_a1.received())
    sum_a1.advance()
    sum_e1.advance()
    sum_a2.advance()
    sums = ((sum_a1, sum_a2), (sum_e1, sum_e2))
    for one, two in sums:
        one.join(two)
        one.advance(2)
    gain = norm_attention[0].astype(F32)
    change, _ = norm_back(x1, row_factor(x1), gain, part + other)
    gradient = g0 + change
    output = (middle2 + (last + last_other)).astype(BF16)
    blocks = [one.finish() for one, _ in sums]

    attention_sums, expert_sums = blocks
    rows = attention_sums.shape[0]
    layers = query_weight.shape[0]
    attention_sums = jnp.swapaxes(attention_sums.reshape(rows, layers, -1), 0, 1)
    bounds = np.cumsum(
        [0, SMALL, query_weight.shape[2], key_matrix.shape[2], value_matrix.shape[2],
         output_weight.shape[1]]
    )
    attention_sums = [attention_sums[..., a:b] for a, b in zip(bounds[:-1], bounds[1:])]
    expert_sums = expert_sums.reshape(rows, 2, layers, experts // 2, 3, hidden)
    expert_sums = [
        expert_sums[..., kind, :].transpose(2, 1, 3, 0, 4).reshape(layers, experts, rows, hidden)
        for kind in range(3)
    ]
    small = attention_sums[0]
    attention_gain = small[:, :, 5]
    attention_gain = attention_gain + exchange(attention_gain)
    return (
        output,
        gradient,
        attention_gain,
        *attention_sums[1:4],
        jnp.swapaxes(attention_sums[4], 1, 2),
        small[:, :, 4],
        small[:, :, :experts],
        expert_sums[0],
        expert_sums[1],
        jnp.swapaxes(expert_sums[2], 2, 3),
    )


def solution(mesh):
    torus = Mesh(
        mesh.devices.reshape(*DP_SIZES, mesh.shape["tensor"]), (*DP, "tensor")
    )
    rows, copied, last = P(DP, None), P(), P(None, None, "tensor")
    in_specs = (
        rows, rows, P(None, DP, None), copied, last, last, last, P(None, "tensor", None),
        copied, copied, P(None, None, None, "tensor"), P(None, None, None, "tensor"),
        P(None, None, "tensor", None), rows,
    )
    out_specs = (
        rows, rows, P(None, DP), P(None, DP, "tensor"), P(None, DP, "tensor"),
        P(None, DP, "tensor"), P(None, "tensor", DP), P(None, DP), P(None, DP, None),
        P(None, None, DP, "tensor"), P(None, None, DP, "tensor"), P(None, None, "tensor", DP),
    )
    return jax.shard_map(
        shards, mesh=torus, in_specs=in_specs, out_specs=out_specs, check_vma=False
    )
```

```python
import functools

import jax
import jax.numpy as jnp
import numpy as np
from jax import lax
from jax.experimental import pallas as pl
from jax.experimental.pallas import tpu as pltpu
from jax.sharding import Mesh
from jax.sharding import PartitionSpec as P

HEAD_SIZE = 64
LANES = 128
STREAMS = 4
SMALL = 128
DP = ("dp_0", "dp_1", "dp_2", "dp_3")
DP_SIZES = (4, 2, 4, 2)
EPSILON = 1e-06
THETA = 10000.0
EXCLUDED = -1e30
F32 = jnp.float32
BF16 = jnp.bfloat16
MIB = 1024 * 1024

EXPERT_ORDERS = (
    (("x", "u"), ("z", "u"), ("z", "v"), ("x", "v")),
    (("z", "v"), ("x", "v"), ("x", "u"), ("z", "u")),
)
ATTENTION_ORDERS = (
    (("z", "v"), ("x", "v"), ("x", "u"), ("z", "u")),
    (("x", "u"), ("z", "u"), ("z", "v"), ("x", "v")),
)


def swapped(order):
    return (order[1], order[0], *order[2:])


def crossed(orders):
    return tuple((order[1], order[0], order[3], order[2]) for order in orders)


def pair_bit(index, kind):
    high = index // 2
    if kind == "v":
        return high
    return high ^ (index % 2)


def ring_place(order, x, z):
    at = 0
    for ring, kind in order:
        at = at * 2 + pair_bit(x if ring == "x" else z, kind)
    return at


def place(order, x, yh, z):
    return ring_place(order, x, z) * 2 + yh


def mm(a, b):
    return lax.dot_general(a, b, (((1,), (0,)), ((), ())), preferred_element_type=F32)


def mm_nt(a, b):
    return lax.dot_general(a, b, (((1,), (1,)), ((), ())), preferred_element_type=F32)


def mm_tn(a, b):
    return lax.dot_general(a, b, (((0,), (0,)), ((), ())), preferred_element_type=F32)


def row_factor(stream):
    return lax.rsqrt(jnp.mean(stream * stream, axis=-1, keepdims=True) + EPSILON)


def norm_back(stream, factor, gain, gradient):
    weighted = gradient * gain
    inner = jnp.sum(weighted * stream, axis=-1, keepdims=True) * (1.0 / stream.shape[-1])
    change = factor * weighted - stream * (factor * factor * factor) * inner
    return change, jnp.sum(gradient * stream * factor, axis=0, keepdims=True)


def lane_of(rows):
    return lax.broadcasted_iota(jnp.int32, (rows, LANES), 1)


def partner(block, lane):
    back = pltpu.roll(block, LANES - HEAD_SIZE // 2, 1)
    ahead = pltpu.roll(block, HEAD_SIZE // 2, 1)
    return jnp.where(lane % HEAD_SIZE < HEAD_SIZE // 2, back, ahead)


def both_heads(block, lane):
    rolled = pltpu.roll(block, HEAD_SIZE, 1)
    low = lane < HEAD_SIZE
    return jnp.where(low, block, rolled), jnp.where(low, rolled, block)


def stacked_pair(block, lane):
    zero = jnp.zeros_like(block)
    low = lane < HEAD_SIZE
    return jnp.concatenate(
        [jnp.where(low, block, zero), jnp.where(low, zero, block)], axis=0
    )


def allowed_pairs(seg_row, seg_column):
    length = seg_column.shape[0]
    rows = lax.broadcasted_iota(jnp.int32, (length, length), 0)
    columns = lax.broadcasted_iota(jnp.int32, (length, length), 1)
    allowed = (columns <= rows) & (seg_column == seg_row)
    bias = jnp.where(allowed, 0.0, 1.0)
    return jnp.concatenate([bias, bias], axis=0) < 0.5


def block_places(orders, places, later=False):
    core = places[4]
    found = []
    for block in range(32):
        x, yh, z = block // 8, (block // 4) % 2, block % 4
        one, two = (
            jnp.where(later, place(second, x, yh, z), place(first, x, yh, z))
            for first, second in zip(orders, crossed(orders))
        )
        own = jnp.where(later, places[2], places[0])
        far = jnp.where(later, places[3], places[1])
        found.append((jnp.where(core == 0, one, two) ^ own, jnp.where(core == 0, two, one) ^ far))
    return core, found


def store_blocks(keep_ref, send_ref, value, column, where_to):
    core, found = where_to
    rows = value.shape[0] // 64
    columns = slice(column, column + value.shape[1])
    for block, (kept, sent) in enumerate(found):
        first = value[2 * block * rows : (2 * block + 1) * rows]
        second = value[(2 * block + 1) * rows : (2 * block + 2) * rows]
        keep_ref[pl.ds(pl.multiple_of(kept * rows, rows), rows), columns] = jnp.where(
            core == 0, first, second
        )
        send_ref[pl.ds(pl.multiple_of(sent * rows, rows), rows), columns] = jnp.where(
            core == 0, second, first
        )


def attend(a, wq, wk, wv, q_out, kk_out, vv_out, mix_out, cosine, sine, allowed):
    length = a.shape[0]
    lane = lane_of(length)
    q = mm(a, wq)
    k = mm(a, wk)
    v = mm(a, wv)
    scale = HEAD_SIZE**-0.5
    for pair in range(k.shape[1] // LANES):
        at = slice(pair * LANES, (pair + 1) * LANES)
        k_block = k[:, at] * cosine + partner(k[:, at], lane) * sine
        k_twice = both_heads(k_block, lane)
        v_twice = both_heads(v[:, at], lane)
        for side in range(2):
            head = 2 * pair + side
            columns = slice(head * LANES, (head + 1) * LANES)
            kk = k_twice[side].astype(BF16)
            vv = v_twice[side].astype(BF16)
            kk_out[head] = kk
            vv_out[head] = vv
            q_block = q[:, columns]
            q_block = (q_block * cosine + partner(q_block, lane) * sine).astype(BF16)
            q_out[:, columns] = q_block
            scores = mm_nt(stacked_pair(q_block, lane), kk) * scale
            scores = jnp.where(allowed, scores, EXCLUDED)
            shifted = jnp.exp(scores - jnp.max(scores, axis=-1, keepdims=True))
            probs = (shifted / jnp.sum(shifted, axis=-1, keepdims=True)).astype(BF16)
            mixed = mm(probs, vv)
            mix_out[:, columns] = jnp.where(
                lane < HEAD_SIZE, mixed[:length], mixed[length:]
            ).astype(BF16)


def halves_of(weights):
    depth = 2 * weights.shape[0] // 3
    quarter = depth // 4
    return (
        weights.at[:depth, : 2 * quarter],
        weights.at[:depth, 2 * quarter : 3 * quarter],
        weights.at[:depth, 3 * quarter :],
        weights.at[depth:, :],
    )


def unpack_gathered(places, gathered, weights):
    core = places[4]
    rows = gathered[0].shape[0] // 8
    width = gathered[0].shape[1]
    top, low = 2 * rows // 3, rows // 3
    for piece in range(32):
        x, z, side = piece // 8, (piece // 2) % 4, piece % 2
        for part in range(2):
            order = EXPERT_ORDERS[side] if part == 0 else swapped(EXPERT_ORDERS[side])
            at = ring_place(order, x, z) ^ places[2 * part + side]
            rows_at = pl.ds(pl.multiple_of((at & 7) * rows, rows), rows)
            columns = slice(part * width, (part + 1) * width)
            first, second, far_first, far_second = (
                gathered[2 * pair + part][rows_at, :] for pair in range(4)
            )
            near, far = jnp.where(at < 8, first, second), jnp.where(at < 8, far_first, far_second)
            value = jnp.where(core == side, near, far).astype(BF16)
            weights[piece * top : (piece + 1) * top, columns] = value[:top]
            start = 32 * top + piece * low
            weights[start : start + low, columns] = value[top:]


def attention_forward_kernel(count, full, *refs):
    parts = refs[:count]
    (gain, wq, wk, wv, wo, cos, sin, seg_row, seg_column) = refs[count : count + 9]
    refs = refs[count + 9 :]
    if full:
        places, gathered = refs[0], refs[1:9]
        refs = refs[9:]
    (x_out, a_out, q_out, kk_out, vv_out, mix_out, part_out) = refs[:7]
    x = parts[0][...].astype(F32)
    if count == 3:
        x = x + (parts[1][...] + parts[2][...])
    x_out[...] = x
    a = (x * row_factor(x) * gain[...].astype(F32)).astype(BF16)
    a_out[...] = a
    common = (cos[...], sin[...], allowed_pairs(seg_row[...], seg_column[...]))
    attend(a, wq[...], wk[...], wv[...], q_out, kk_out, vv_out, mix_out, *common)
    part_out[...] = mm(mix_out[...], wo[...])
    if full:
        q_other, kk_other, vv_other, part_other, weights, mix_other = refs[7:]
        unpack_gathered(places, gathered, weights)
        wq, wk, wv, wo = halves_of(weights)
        attend(a, wq[...], wk[...], wv[...], q_other, kk_other, vv_other, mix_other, *common)
        part_other[...] = mm(mix_other[...], wo[...])


ONCE = pl.Buffered(1)
SMEM = pl.BlockSpec(memory_space=pltpu.SMEM)
ANYWHERE = pl.BlockSpec(memory_space=pl.ANY)


def whole(shape):
    return pl.BlockSpec(shape, lambda i: (0,) * len(shape), pipeline_mode=ONCE)


def of_layer(layer, shape):
    return pl.BlockSpec(
        (None, *shape), lambda i: (layer,) + (0,) * len(shape), pipeline_mode=ONCE
    )


def params(mib):
    return pltpu.CompilerParams(
        vmem_limit_bytes=mib * MIB, dimension_semantics=("arbitrary",)
    )


def cost(flops, nbytes):
    return pl.CostEstimate(flops=flops, bytes_accessed=nbytes, transcendentals=0)


def attention_forward(layer, parts, weights, tables, segment, gathered=()):
    gain, wq, wk, wv, wo = weights
    length, features = parts[0].shape
    q_width, k_width = wq.shape[2], wk.shape[2]
    heads = 2 * k_width // LANES
    ins = [*parts, gain, wq, wk, wv, wo, *tables, *segment]
    in_specs = [whole(part.shape) for part in parts]
    in_specs += [of_layer(layer, w.shape[1:]) for w in (gain, wq, wk, wv, wo)]
    in_specs += [whole(t.shape) for t in (*tables, *segment)]
    outs = [
        ((length, features), F32),
        ((length, features), BF16),
        ((length, q_width), BF16),
        ((heads, length, LANES), BF16),
        ((heads, length, LANES), BF16),
        ((length, q_width), BF16),
        ((length, features), F32),
    ]
    scratch = []
    if gathered:
        ins += gathered
        in_specs += [SMEM, *(whole(array.shape) for array in gathered[1:])]
        outs += [outs[2], outs[3], outs[4], outs[6], ((4 * gathered[1].shape[0], features), BF16)]
        scratch = [pltpu.VMEM((length, q_width), BF16)]
    return pl.pallas_call(
        functools.partial(attention_forward_kernel, len(parts), bool(gathered)),
        grid=(1,),
        scratch_shapes=scratch,
        in_specs=in_specs,
        out_specs=[whole(shape) for shape, _ in outs],
        out_shape=[jax.ShapeDtypeStruct(*out) for out in outs],
        compiler_params=params(60),
        cost_estimate=cost(6 << 30, 8 * MIB),
        name="attention_forward",
    )(*ins)


def column_of(table, lane, index):
    return jnp.sum(jnp.where(lane == index, table, 0.0), axis=1, keepdims=True)


def expert_prologue(x, own, other, gain, router, mask, middle_out, xi_out, share_out):
    middle = x[...] + (own[...] + other[...])
    middle_out[...] = middle
    xi = (middle * row_factor(middle) * gain[...].astype(F32)).astype(BF16)
    xi_out[...] = xi
    logits = mm(xi, router[...])
    chosen = mask[...] > 0.5
    logits = jnp.where(chosen, logits, EXCLUDED)
    shifted = jnp.exp(logits - jnp.max(logits, axis=-1, keepdims=True))
    shifted = jnp.where(chosen, shifted, 0.0)
    share_out[...] = shifted / jnp.sum(shifted, axis=-1, keepdims=True)


def expert_step(gate_in, linear, wd, share):
    squashed = 1.0 / (1.0 + jnp.exp(-gate_in))
    silu = gate_in * squashed
    activation = (silu * linear).astype(BF16)
    return squashed, silu, activation, mm(activation, wd)


def expert_backward_step(places, g, xi, share, gate_in, linear, wg, wu, wd, keep, send):
    where_to = block_places(EXPERT_ORDERS, places, pl.program_id(0) >= STREAMS // 2)
    squashed, silu, activation, expert_out = expert_step(gate_in, linear, wd, share)
    gate_grad = jnp.sum(g * expert_out, axis=1, keepdims=True)
    expert_grad = (share * g).astype(BF16)
    activation_grad = mm_nt(expert_grad, wd)
    gate_in_grad = (
        activation_grad * linear * squashed * (1.0 + gate_in * (1.0 - squashed))
    ).astype(BF16)
    linear_grad = (activation_grad * silu).astype(BF16)
    width = activation.shape[1]
    store_blocks(keep, send, mm_tn(xi, gate_in_grad), 0, where_to)
    store_blocks(keep, send, mm_tn(xi, linear_grad), width, where_to)
    store_blocks(keep, send, mm_tn(expert_grad, activation), 2 * width, where_to)
    return gate_grad, mm_nt(gate_in_grad, wg) + mm_nt(linear_grad, wu), expert_out


def expert_forward_kernel(
    x, own, other, gain, router, mask, wg, wu, wd,
    middle_out, xi_out, share_out, gate_out, linear_out, part_out,
):
    expert = pl.program_id(0)

    @pl.when(expert == 0)
    def _():
        expert_prologue(x, own, other, gain, router, mask, middle_out, xi_out, share_out)
        part_out[...] = jnp.zeros_like(part_out)

    share = column_of(share_out[...], lane_of(share_out.shape[0]), expert)
    xi = xi_out[...]
    gate_in = mm(xi, wg[...])
    linear = mm(xi, wu[...])
    gate_out[...] = gate_in
    linear_out[...] = linear
    part_out[...] += share * expert_step(gate_in, linear, wd[...], share)[3]


def expert_both_kernel(
    places, x, own, other, gain, router, mask, wg, wu, wd, cotangent,
    middle_out, xi_out, share_out, part_out, back_out, keep, send,
):
    expert = pl.program_id(0)
    lane = lane_of(share_out.shape[0])

    @pl.when(expert == 0)
    def _():
        expert_prologue(x, own, other, gain, router, mask, middle_out, xi_out, share_out)
        part_out[...] = jnp.zeros_like(part_out)
        back_out[...] = jnp.zeros_like(back_out)

    share = column_of(share_out[...], lane, expert)
    xi = xi_out[...]
    gate_in = mm(xi, wg[...])
    linear = mm(xi, wu[...])
    gate_grad, back, expert_out = expert_backward_step(
        places, cotangent[...].astype(F32), xi, share, gate_in, linear, wg[...], wu[...],
        wd[...], keep, send,
    )
    part_out[...] += share * expert_out
    back_out[:, : back.shape[1]] += back
    back_out[:, back.shape[1] :] += jnp.where(lane == expert, gate_grad, 0.0)


def expert_backward_kernel(
    places, g_in, x, gain, own, other, xi_ref, share_ref, gate_ref, linear_ref, wg, wu, wd,
    *rest,
):
    g_out, gain_out, back_out, keep, send = rest[-5:]
    expert = pl.program_id(0)
    lane = lane_of(share_ref.shape[0])

    @pl.when(expert == 0)
    def _():
        stream = x[...]
        change, gain_row = norm_back(
            stream, row_factor(stream), gain[...].astype(F32), own[...] + other[...]
        )
        g_out[...] = g_in[...] + change
        gain_out[...] = jnp.broadcast_to(gain_row, gain_out.shape)
        back_out[...] = jnp.zeros_like(back_out)

    share = column_of(share_ref[...], lane, expert)
    gate_grad, back, _ = expert_backward_step(
        places, g_out[...], xi_ref[...], share, gate_ref[...], linear_ref[...], wg[...],
        wu[...], wd[...], keep, send,
    )
    back_out[:, : back.shape[1]] += back
    back_out[:, back.shape[1] :] += jnp.where(lane == expert, gate_grad, 0.0)


def of_expert(layer, shape):
    return pl.BlockSpec((None, None, *shape), lambda e: (layer, e, 0, 0))


def each_expert(shape):
    return pl.BlockSpec((None, *shape), lambda e: (e, 0, 0))


def with_gates(length, features):
    shape = (length, features + LANES)
    return whole(shape), (shape, F32)


def gradient_outs(rows, width):
    spec = pl.BlockSpec((rows, 3 * width), lambda e: (0, e))
    shape = ((rows, 3 * width * STREAMS), F32)
    return [(spec, shape)] * 2


def run_experts(kernel, name, ins, in_specs, outs, flops, nbytes, mib):
    return pl.pallas_call(
        kernel,
        grid=(STREAMS,),
        in_specs=in_specs,
        out_specs=[spec for spec, _ in outs],
        out_shape=[jax.ShapeDtypeStruct(*out) for _, out in outs],
        compiler_params=params(mib),
        cost_estimate=cost(flops, nbytes),
        name=name,
    )(*ins)


def expert_forward(layer, x, own, other, gain, router, mask, wg, wu, wd):
    length, features = x.shape
    width = wg.shape[3]
    big, low = ((length, features), F32), ((length, features), BF16)
    hidden = (each_expert((length, width)), ((STREAMS, length, width), F32))
    ins = [x, own, other, gain, router, mask, wg, wu, wd]
    in_specs = [whole(x.shape)] * 3 + [
        of_layer(layer, gain.shape[1:]),
        of_layer(layer, router.shape[1:]),
        of_layer(layer, mask.shape[1:]),
        *(of_expert(layer, w.shape[2:]) for w in (wg, wu, wd)),
    ]
    outs = [
        (whole(big[0]), big),
        (whole(low[0]), low),
        (whole((length, LANES)), ((length, LANES), F32)),
        hidden,
        hidden,
        (whole(big[0]), big),
    ]
    return run_experts(
        expert_forward_kernel, "experts_forward", ins, in_specs, outs, 8 << 30, 12 * MIB, 60
    )


def expert_both(layer, places, x, own, other, gain, router, mask, wg, wu, wd, cotangent):
    length, features = x.shape
    width = wg.shape[3]
    big, low = ((length, features), F32), ((length, features), BF16)
    table = (whole((length, LANES)), ((length, LANES), F32))
    ins = [places, x, own, other, gain, router, mask, wg, wu, wd, cotangent]
    in_specs = [SMEM] + [whole(x.shape)] * 3 + [
        of_layer(layer, gain.shape[1:]),
        of_layer(layer, router.shape[1:]),
        of_layer(layer, mask.shape[1:]),
        *(of_expert(layer, w.shape[2:]) for w in (wg, wu, wd)),
        whole(cotangent.shape),
    ]
    outs = [
        (whole(big[0]), big),
        (whole(low[0]), low),
        table,
        (whole(big[0]), big),
        with_gates(length, features),
        *gradient_outs(features // 2, width),
    ]
    return run_experts(
        expert_both_kernel, "experts_both", ins, in_specs, outs, 16 << 30, 30 * MIB, 60
    )


def expert_backward(
    layer, places, g, x, gain, own, other, xi, share, gate_in, linear, wg, wu, wd, after
):
    length, features = x.shape
    width = wg.shape[3]
    big = ((length, features), F32)
    hidden = each_expert((length, width))
    ins = [places, g, x, gain, own, other, xi, share, gate_in, linear, wg, wu, wd, *after]
    in_specs = [SMEM, whole(x.shape), whole(x.shape)] + [
        of_layer(layer + 1, gain.shape[1:]),
        whole(x.shape),
        whole(x.shape),
        whole(x.shape),
        whole(share.shape),
        hidden,
        hidden,
        *(of_expert(layer, w.shape[2:]) for w in (wg, wu, wd)),
        *([ANYWHERE] * len(after)),
    ]
    outs = [
        (whole(big[0]), big),
        (whole((8, features)), ((8, features), F32)),
        with_gates(length, features),
        *gradient_outs(features // 2, width),
    ]
    return run_experts(
        expert_backward_kernel, "experts_backward", ins, in_specs, outs, 4 << 30, 30 * MIB, 60
    )


def attend_backward(mixture_grad, q, kk, vv, cosine, sine, allowed):
    length = mixture_grad.shape[0]
    lane = lane_of(length)
    low = lane < HEAD_SIZE
    scale = HEAD_SIZE**-0.5
    query_grads, key_grads, value_grads = [], [], []
    for pair in range(q.shape[1] // LANES // 2):
        key_sides, value_sides = [], []
        for side in range(2):
            head = 2 * pair + side
            columns = slice(head * LANES, (head + 1) * LANES)
            stacked = stacked_pair(q[:, columns], lane)
            scores = jnp.where(allowed, mm_nt(stacked, kk[head]) * scale, EXCLUDED)
            shifted = jnp.exp(scores - jnp.max(scores, axis=-1, keepdims=True))
            probs = shifted / jnp.sum(shifted, axis=-1, keepdims=True)
            mix_grad = stacked_pair(mixture_grad[:, columns], lane)
            prob_grad = mm_nt(mix_grad, vv[head])
            inner = jnp.sum(probs * prob_grad, axis=-1, keepdims=True)
            score_grad = (probs * (prob_grad - inner)).astype(BF16)
            query = mm(score_grad, kk[head])
            query = jnp.where(low, query[:length], query[length:]) * scale
            query = query * cosine - partner(query, lane) * sine
            query_grads.append(query.astype(BF16))
            key = mm_tn(score_grad, stacked) * scale
            key_sides.append(key + pltpu.roll(key, HEAD_SIZE, 1))
            value = mm_tn(probs.astype(BF16), mix_grad)
            value_sides.append(value + pltpu.roll(value, HEAD_SIZE, 1))
        key = jnp.where(low, key_sides[0], key_sides[1])
        key_grads.append((key * cosine - partner(key, lane) * sine).astype(BF16))
        value_grads.append(jnp.where(low, value_sides[0], value_sides[1]).astype(BF16))
    return tuple(
        jnp.concatenate(grads, axis=1) for grads in (query_grads, key_grads, value_grads)
    )


def attention_backward_kernel(
    count, full, places, g, own, other, middle, xi, share, gain, router_rows,
    wo, mix, q, kk, vv, a, wq, wk, wv, cos, sin, seg_row, seg_column, x, late_gain, *rest,
):
    if full:
        q_other, kk_other, vv_other, weights = rest[:4]
        part_other = rest[-2]
        rest = rest[4:]
    g_out, part_out, keep, send = rest[count : count + 4]
    rows_scratch = rest[-1]
    first, second = (block_places(ATTENTION_ORDERS, places, later) for later in (False, True))
    length = middle.shape[0]
    lane = lane_of(length)
    shares = share[...]
    features = middle.shape[1]
    gate_grad = own[:, features:] + other[:, features:]
    pick = shares * (gate_grad - jnp.sum(shares * gate_grad, axis=1, keepdims=True))
    input_grad = own[:, :features] + other[:, :features]
    xi_full = xi[...].astype(F32)
    rows_scratch[...] = jnp.zeros_like(rows_scratch)
    for expert in range(STREAMS):
        logit_grad = column_of(pick, lane, expert)
        input_grad = input_grad + logit_grad * router_rows[expert : expert + 1, :]
        rows_scratch[expert : expert + 1, :] = jnp.sum(
            xi_full * logit_grad, axis=0, keepdims=True
        )
    mid = middle[...]
    change, gain_row = norm_back(mid, row_factor(mid), gain[...].astype(F32), input_grad)
    rows_scratch[4:5, :] = gain_row
    rows_scratch[6:7, :] = late_gain[0:1, :]
    gradient = g[...].astype(F32) + change
    g_out[...] = gradient
    output_grad = gradient.astype(BF16)
    common = (cos[...], sin[...], allowed_pairs(seg_row[...], seg_column[...]))

    def half(output_weight, weights, *saved):
        mixture_grad = mm_nt(output_grad, output_weight[...]).astype(BF16)
        grads = attend_backward(mixture_grad, *saved, *common)
        part = sum(mm_nt(grad, weight[...]) for grad, weight in zip(grads, weights))
        return grads, part

    if full:
        wq_other, wk_other, wv_other, wo_other = halves_of(weights)
        part_other[...] = half(
            wo_other, (wq_other, wk_other, wv_other), q_other, kk_other, vv_other
        )[1]
    grads, attention_part = half(wo, (wq, wk, wv), q, kk, vv)
    part_out[...] = attention_part
    stream = x[...]
    rows_scratch[5:6, :] = jnp.sum(
        attention_part * stream * row_factor(stream), axis=0, keepdims=True
    )
    a_full = a[...]
    column = 0
    query_grad, key_grad, value_grad = grads
    for total, where_to in (
        (jnp.transpose(rows_scratch[...]), first),
        (mm_tn(a_full, query_grad), first),
        (mm_tn(a_full, key_grad), first),
        (mm_tn(a_full, value_grad), second),
        (mm_tn(output_grad, mix[...]), second),
    ):
        store_blocks(keep, send, total, column, where_to)
        column += total.shape[1]


def attention_backward(
    layer, places, g, own, other, saved_experts, weights, saved, tables, segment, late_gain, after,
    others=(),
):
    middle, xi, share = saved_experts
    gain, router_rows, wo, wq, wk, wv = weights
    x, a, q, kk, vv, mix = saved
    length, features = middle.shape
    columns = SMALL + wq.shape[2] + wk.shape[2] + wv.shape[2] + wo.shape[1]
    ins = [
        places, g, own, other, middle, xi, share, gain, router_rows, wo,
        mix, q, kk, vv, a, wq, wk, wv, *tables, *segment, x, late_gain,
    ]
    layered = {7, 8, 9, 15, 16, 17}
    in_specs = [SMEM]
    for at, array in enumerate(ins[1:], 1):
        in_specs.append(of_layer(layer, array.shape[1:]) if at in layered else whole(array.shape))
    ins += [*others, *after]
    in_specs += [whole(array.shape) for array in others]
    in_specs += [ANYWHERE] * len(after)
    outs = [
        ((length, features), F32),
        ((length, features), F32),
        ((features // 2, columns), F32),
        ((features // 2, columns), F32),
    ]
    if others:
        outs.append(((length, features), F32))
    return pl.pallas_call(
        functools.partial(
            attention_backward_kernel, len(after), bool(others)
        ),
        grid=(1,),
        in_specs=in_specs,
        out_specs=[whole(shape) for shape, _ in outs],
        out_shape=[jax.ShapeDtypeStruct(*out) for out in outs],
        scratch_shapes=[pltpu.VMEM((LANES, features), F32)],
        compiler_params=params(60),
        cost_estimate=cost(16 << 30, 18 * MIB),
        name="attention_backward",
    )(*ins)


SWAP = ((0, 1), (1, 0))
RING = {"u": tuple((i, i ^ 1) for i in range(4)), "v": tuple((i, 3 - i) for i in range(4))}


def exchange(array):
    return lax.ppermute(array, "tensor", SWAP)


RING_AXES = ("dp_0", "dp_2", "dp_3")


def ring_pairs(orders, step):
    pairs = []
    for x in range(4):
        for z in range(4):
            for core in range(2):
                ring, kind = orders[core][step]
                at = x if ring == "x" else z
                to = at ^ 1 if kind == "u" else 3 - at
                there = (to, z) if ring == "x" else (x, to)
                pairs.append(((x * 4 + z) * 2 + core, (there[0] * 4 + there[1]) * 2 + core))
    return pairs


class Scatter:
    def __init__(self, keep, send, orders, column):
        received = lax.ppermute(send, "dp_3", SWAP)
        self.orders = (orders, crossed(orders))
        self.parts = [
            [array[:, :column] for array in (keep, received)],
            [array[:, column:] for array in (keep, received)],
        ]
        self.step = 0

    def halve(self):
        half = self.parts[0][0].shape[0] // 2
        self.kept = [first[:half] + second[:half] for first, second in self.parts]
        return [first[half:] + second[half:] for first, second in self.parts]

    def move(self, sends):
        moved = [
            lax.ppermute(send, RING_AXES, ring_pairs(orders, self.step))
            for send, orders in zip(sends, self.orders)
        ]
        self.parts = [list(pair) for pair in zip(self.kept, moved)]
        self.step += 1

    def received(self):
        return [second for _, second in self.parts]

    def hold(self, *after):
        for pair, second in zip(self.parts, behind(self.received(), *after)):
            pair[1] = second

    def advance(self, count=1):
        for _ in range(count):
            self.move(self.halve())

    def join(self, other):
        self.parts = [
            [jnp.concatenate(pair, axis=1) for pair in zip(*both)]
            for both in zip(self.parts, other.parts)
        ]

    def finish(self):
        sends = jnp.concatenate(self.halve(), axis=-1)
        return jnp.concatenate(self.kept, axis=-1) + lax.ppermute(sends, "dp_1", SWAP)


class Gather:
    def __init__(self, weights, layer):
        x, z, core = (lax.axis_index(name) for name in RING_AXES)
        piece = (x * 4 + z) * 2 + core

        def rows_of(weight):
            rows = weight.shape[1] // 32
            return lax.dynamic_slice_in_dim(weight[layer], piece * rows, rows, 0).astype(F32)

        *inputs, output = (rows_of(weight) for weight in weights)
        self.piece = jnp.concatenate([jnp.concatenate(inputs, axis=1), output], axis=0)
        orders = [*EXPERT_ORDERS, *(swapped(order) for order in EXPERT_ORDERS)]
        places = [ring_place(order, x, z) for order in orders]
        self.places = jnp.stack([*places, core]).astype(jnp.int32)

        self.crossed = exchange(self.piece)

    def begin(self, after, received):
        held, *_ = behind([self.crossed], after)
        for step in (3, 2):
            moved = lax.ppermute(held, RING_AXES, ring_pairs(EXPERT_ORDERS, step))
            held = jnp.concatenate([held, moved], axis=0)
        half = held.shape[1] // 2
        self.held = behind([held[:, :half], held[:, half:]], received)
        self.moved = self.moves(self.held, 1)

    def moves(self, held, step):
        return [
            lax.ppermute(half, RING_AXES, ring_pairs(EXPERT_ORDERS, at))
            for half, at in zip(held, (step, 1 - step))
        ]

    def finish(self, after):
        held = behind(self.held, after)
        held = [jnp.concatenate(pair, axis=0) for pair in zip(held, self.moved)]
        near = [*held, *self.moves(held, 0)]
        return [self.places, *near, *(lax.ppermute(half, "dp_3", SWAP) for half in near)]


def behind(arrays, *after):
    return pl.pallas_call(
        lambda *refs: None,
        in_specs=[ANYWHERE] * (len(arrays) + len(after)),
        out_specs=[ANYWHERE] * len(arrays),
        out_shape=[jax.ShapeDtypeStruct(array.shape, array.dtype) for array in arrays],
        input_output_aliases={at: at for at in range(len(arrays))},
        name="behind",
    )(*arrays, *after)


def rope_tables(length):
    half = HEAD_SIZE // 2
    frequency = np.float32(THETA) ** (-2.0 * np.arange(half, dtype=np.float32) / HEAD_SIZE)
    angles = np.arange(length, dtype=np.float32)[:, None] * frequency[None].astype(np.float32)
    angles = angles.astype(np.float32)
    cosine = np.tile(np.cos(angles), (1, LANES // half)).astype(np.float32)
    sine = np.sin(angles)
    sine = np.tile(np.concatenate([-sine, sine], axis=1), (1, LANES // HEAD_SIZE))
    return jnp.asarray(cosine), jnp.asarray(sine.astype(np.float32))


def shards(
    tokens, segments, routes, norm_attention, query_weight, key_matrix, value_matrix,
    output_weight, norm_experts, router_weight, gate_weight, up_weight, down_weight, cotangent,
):
    length, features = tokens.shape
    experts = gate_weight.shape[1]
    hidden = gate_weight.shape[3]
    tables = rope_tables(length)
    segment = (segments.reshape(1, length), segments.reshape(length, 1))
    gain_attention = norm_attention[:, None, :]
    gain_experts = norm_experts[:, None, :]
    router = jnp.pad(router_weight, ((0, 0), (0, 0), (0, LANES - experts)))
    router_rows = jnp.pad(
        jnp.swapaxes(router_weight, 1, 2).astype(F32), ((0, 0), (0, 8 - experts), (0, 0))
    )
    mask = jnp.any(
        routes[..., None] == jnp.arange(LANES, dtype=jnp.int32), axis=2
    ).astype(F32)
    x_at, y_at, z_at = (lax.axis_index(name) for name in DP[:3])
    core = lax.axis_index("dp_3")

    def places_in(orders):
        found = []
        for which in (orders, crossed(orders)):
            one, two = (place(order, x_at, y_at, z_at) for order in which)
            found += [jnp.where(core == 0, one, two), jnp.where(core == 0, two, one)]
        return jnp.stack([*found, core]).astype(jnp.int32)

    expert_places = places_in(EXPERT_ORDERS)
    attention_places = places_in(ATTENTION_ORDERS)

    attention_weights = (gain_attention, query_weight, key_matrix, value_matrix, output_weight)
    expert_weights = (gate_weight, up_weight, down_weight)
    back_weights = (
        gain_experts, router_rows, output_weight, query_weight, key_matrix, value_matrix,
    )

    others = Gather(attention_weights[1:], 1)
    x1, *saved1, part = attention_forward(0, [tokens], attention_weights, tables, segment)
    other = exchange(part)
    others.begin(part, other)
    middle1, xi1, share1, gate1, linear1, part = expert_forward(
        0, x1, part, other, gain_experts, router, mask, *expert_weights
    )
    x2, *saved2, part, q_other, kk_other, vv_other, part_other, weights_other = attention_forward(
        1, [middle1, part, exchange(part)], attention_weights, tables, segment,
        others.finish(part),
    )
    middle2, xi2, share2, last, back, keep, send = expert_both(
        1, expert_places, x2, part, part_other, gain_experts, router, mask, *expert_weights,
        cotangent,
    )
    half = keep.shape[1] // 2
    split = SMALL + query_weight.shape[2] + key_matrix.shape[2]
    sum_e2 = Scatter(keep, send, EXPERT_ORDERS, half)
    other = exchange(back)
    *sends, last = behind([*sum_e2.halve(), last], other)
    sum_e2.move(sends)
    last_other = exchange(last)
    no_gain = jnp.zeros((8, features), F32)
    g2, part, keep, send, part_other = attention_backward(
        1, attention_places, cotangent, back, other, (middle2, xi2, share2), back_weights,
        (x2, *saved2), tables, segment, no_gain, sends,
        (q_other, kk_other, vv_other, weights_other),
    )
    sum_a2 = Scatter(keep, send, ATTENTION_ORDERS, split)
    sends = sum_e2.halve()
    g1, late_gain, back, keep, send = expert_backward(
        0, expert_places, g2, x2, gain_attention, part, part_other, xi1, share1, gate1,
        linear1, *expert_weights, [*sends, last_other],
    )
    sum_e2.move(sends)
    sum_e1 = Scatter(keep, send, EXPERT_ORDERS, half)
    other = exchange(back)
    sends_a, sends_e = sum_a2.halve(), sum_e1.halve()
    sum_a2.move(sends_a)
    sum_e1.move(sends_e)
    g0, part, keep, send = attention_backward(
        0, attention_places, g1, back, other, (middle1, xi1, share1), back_weights,
        (x1, *saved1), tables, segment, late_gain, sends_a + sends_e + sum_e2.received(),
    )
    (send,) = behind([send], *sum_a2.received(), *sum_e1.received())
    sum_a1 = Scatter(keep, send, ATTENTION_ORDERS, split)
    sends = sum_a1.halve()
    sum_a1.move(sends)
    (other,) = behind([exchange(part)], *sum_a1.received())
    sum_a1.advance()
    sum_a2.advance()
    sum_e1.advance()
    sum_e1.hold(*sends)
    sum_e1.join(sum_e2)
    sum_e1.advance(2)
    sum_a1.join(sum_a2)
    sum_a1.advance(2)
    sums = (sum_a1, sum_e1)
    gain = norm_attention[0].astype(F32)
    change, _ = norm_back(x1, row_factor(x1), gain, part + other)
    gradient = g0 + change
    output = (middle2 + (last + last_other)).astype(BF16)
    blocks = [one.finish() for one in sums]

    attention_sums, expert_sums = blocks
    rows = attention_sums.shape[0]
    layers = query_weight.shape[0]
    bounds = np.cumsum([0, SMALL, query_weight.shape[2], key_matrix.shape[2]])
    more_bounds = np.cumsum([0, value_matrix.shape[2], output_weight.shape[1]])
    one, two = (
        jnp.swapaxes(columns.reshape(rows, layers, -1), 0, 1)
        for columns in (attention_sums[:, : layers * split], attention_sums[:, layers * split :])
    )
    attention_sums = [one[..., a:b] for a, b in zip(bounds[:-1], bounds[1:])]
    attention_sums += [two[..., a:b] for a, b in zip(more_bounds[:-1], more_bounds[1:])]
    expert_sums = expert_sums.reshape(rows, 2, layers, experts // 2, 3, hidden)
    expert_sums = [
        expert_sums[..., kind, :].transpose(2, 1, 3, 0, 4).reshape(layers, experts, rows, hidden)
        for kind in range(3)
    ]
    small = attention_sums[0]
    attention_gain = small[:, :, 5]
    attention_gain = attention_gain + exchange(attention_gain)
    return (
        output,
        gradient,
        attention_gain,
        *attention_sums[1:4],
        jnp.swapaxes(attention_sums[4], 1, 2),
        small[:, :, 4],
        small[:, :, :experts],
        expert_sums[0],
        expert_sums[1],
        jnp.swapaxes(expert_sums[2], 2, 3),
    )


def solution(mesh):
    torus = Mesh(
        mesh.devices.reshape(*DP_SIZES, mesh.shape["tensor"]), (*DP, "tensor")
    )
    rows, copied, last = P(DP, None), P(), P(None, None, "tensor")
    in_specs = (
        rows, rows, P(None, DP, None), copied, last, last, last, P(None, "tensor", None),
        copied, copied, P(None, None, None, "tensor"), P(None, None, None, "tensor"),
        P(None, None, "tensor", None), rows,
    )
    out_specs = (
        rows, rows, P(None, DP), P(None, DP, "tensor"), P(None, DP, "tensor"),
        P(None, DP, "tensor"), P(None, "tensor", DP), P(None, DP), P(None, DP, None),
        P(None, None, DP, "tensor"), P(None, None, DP, "tensor"), P(None, None, "tensor", DP),
    )
    return jax.shard_map(
        shards, mesh=torus, in_specs=in_specs, out_specs=out_specs, check_vma=False
    )
```

```python
import functools

import jax
import jax.numpy as jnp
import numpy as np
from jax import lax
from jax.experimental import pallas as pl
from jax.experimental.pallas import tpu as pltpu
from jax.sharding import Mesh
from jax.sharding import PartitionSpec as P

HEAD_SIZE = 64
LANES = 128
STREAMS = 4
SMALL = 128
DP = ("dp_0", "dp_1", "dp_2", "dp_3")
DP_SIZES = (4, 2, 4, 2)
EPSILON = 1e-06
THETA = 10000.0
EXCLUDED = -1e30
F32 = jnp.float32
BF16 = jnp.bfloat16
MIB = 1024 * 1024

EXPERT_ORDERS = (
    (("x", "u"), ("z", "u"), ("z", "v"), ("x", "v")),
    (("z", "v"), ("x", "v"), ("x", "u"), ("z", "u")),
)
ATTENTION_ORDERS = (
    (("z", "v"), ("x", "v"), ("x", "u"), ("z", "u")),
    (("x", "u"), ("z", "u"), ("z", "v"), ("x", "v")),
)


def swapped(order):
    return (order[1], order[0], *order[2:])


def crossed(orders):
    return tuple((order[1], order[0], order[3], order[2]) for order in orders)


def pair_bit(index, kind):
    high = index // 2
    if kind == "v":
        return high
    return high ^ (index % 2)


def ring_place(order, x, z):
    at = 0
    for ring, kind in order:
        at = at * 2 + pair_bit(x if ring == "x" else z, kind)
    return at


def place(order, x, yh, z):
    return ring_place(order, x, z) * 2 + yh


def mm(a, b):
    return lax.dot_general(a, b, (((1,), (0,)), ((), ())), preferred_element_type=F32)


def mm_nt(a, b):
    return lax.dot_general(a, b, (((1,), (1,)), ((), ())), preferred_element_type=F32)


def mm_tn(a, b):
    return lax.dot_general(a, b, (((0,), (0,)), ((), ())), preferred_element_type=F32)


def row_factor(stream):
    return lax.rsqrt(jnp.mean(stream * stream, axis=-1, keepdims=True) + EPSILON)


def norm_back(stream, factor, gain, gradient):
    weighted = gradient * gain
    inner = jnp.sum(weighted * stream, axis=-1, keepdims=True) * (1.0 / stream.shape[-1])
    change = factor * weighted - stream * (factor * factor * factor) * inner
    return change, jnp.sum(gradient * stream * factor, axis=0, keepdims=True)


def lane_of(rows):
    return lax.broadcasted_iota(jnp.int32, (rows, LANES), 1)


def partner(block, lane):
    back = pltpu.roll(block, LANES - HEAD_SIZE // 2, 1)
    ahead = pltpu.roll(block, HEAD_SIZE // 2, 1)
    return jnp.where(lane % HEAD_SIZE < HEAD_SIZE // 2, back, ahead)


def both_heads(block, lane):
    rolled = pltpu.roll(block, HEAD_SIZE, 1)
    low = lane < HEAD_SIZE
    return jnp.where(low, block, rolled), jnp.where(low, rolled, block)


def stacked_pair(block, lane):
    zero = jnp.zeros_like(block)
    low = lane < HEAD_SIZE
    return jnp.concatenate(
        [jnp.where(low, block, zero), jnp.where(low, zero, block)], axis=0
    )


def allowed_pairs(seg_row, seg_column):
    length = seg_column.shape[0]
    rows = lax.broadcasted_iota(jnp.int32, (length, length), 0)
    columns = lax.broadcasted_iota(jnp.int32, (length, length), 1)
    allowed = (columns <= rows) & (seg_column == seg_row)
    bias = jnp.where(allowed, 0.0, 1.0)
    return jnp.concatenate([bias, bias], axis=0) < 0.5


def block_places(orders, places, later=False):
    core = places[4]
    found = []
    for block in range(32):
        x, yh, z = block // 8, (block // 4) % 2, block % 4
        one, two = (
            jnp.where(later, place(second, x, yh, z), place(first, x, yh, z))
            for first, second in zip(orders, crossed(orders))
        )
        own = jnp.where(later, places[2], places[0])
        far = jnp.where(later, places[3], places[1])
        found.append((jnp.where(core == 0, one, two) ^ own, jnp.where(core == 0, two, one) ^ far))
    return core, found


def store_blocks(keep_ref, send_ref, value, column, where_to):
    core, found = where_to
    rows = value.shape[0] // 64
    columns = slice(column, column + value.shape[1])
    for block, (kept, sent) in enumerate(found):
        first = value[2 * block * rows : (2 * block + 1) * rows]
        second = value[(2 * block + 1) * rows : (2 * block + 2) * rows]
        keep_ref[pl.ds(pl.multiple_of(kept * rows, rows), rows), columns] = jnp.where(
            core == 0, first, second
        )
        send_ref[pl.ds(pl.multiple_of(sent * rows, rows), rows), columns] = jnp.where(
            core == 0, second, first
        )


def attend(a, wq, wk, wv, q_out, kk_out, vv_out, mix_out, cosine, sine, allowed):
    length = a.shape[0]
    lane = lane_of(length)
    q = mm(a, wq)
    k = mm(a, wk)
    v = mm(a, wv)
    scale = HEAD_SIZE**-0.5
    for pair in range(k.shape[1] // LANES):
        at = slice(pair * LANES, (pair + 1) * LANES)
        k_block = k[:, at] * cosine + partner(k[:, at], lane) * sine
        k_twice = both_heads(k_block, lane)
        v_twice = both_heads(v[:, at], lane)
        for side in range(2):
            head = 2 * pair + side
            columns = slice(head * LANES, (head + 1) * LANES)
            kk = k_twice[side].astype(BF16)
            vv = v_twice[side].astype(BF16)
            kk_out[head] = kk
            vv_out[head] = vv
            q_block = q[:, columns]
            q_block = (q_block * cosine + partner(q_block, lane) * sine).astype(BF16)
            q_out[:, columns] = q_block
            scores = mm_nt(stacked_pair(q_block, lane), kk) * scale
            scores = jnp.where(allowed, scores, EXCLUDED)
            shifted = jnp.exp(scores - jnp.max(scores, axis=-1, keepdims=True))
            probs = (shifted / jnp.sum(shifted, axis=-1, keepdims=True)).astype(BF16)
            mixed = mm(probs, vv)
            mix_out[:, columns] = jnp.where(
                lane < HEAD_SIZE, mixed[:length], mixed[length:]
            ).astype(BF16)


def halves_of(weights):
    depth = 2 * weights.shape[0] // 3
    quarter = depth // 4
    return (
        weights.at[:depth, : 2 * quarter],
        weights.at[:depth, 2 * quarter : 3 * quarter],
        weights.at[:depth, 3 * quarter :],
        weights.at[depth:, :],
    )


def unpack_gathered(places, gathered, weights):
    core = places[4]
    rows = gathered[0].shape[0] // 8
    width = gathered[0].shape[1]
    top, low = 2 * rows // 3, rows // 3
    for piece in range(32):
        x, z, side = piece // 8, (piece // 2) % 4, piece % 2
        for part in range(2):
            order = EXPERT_ORDERS[side] if part == 0 else swapped(EXPERT_ORDERS[side])
            at = ring_place(order, x, z) ^ places[2 * part + side]
            rows_at = pl.ds(pl.multiple_of((at & 7) * rows, rows), rows)
            columns = slice(part * width, (part + 1) * width)
            first, second, far_first, far_second = (
                gathered[2 * pair + part][rows_at, :] for pair in range(4)
            )
            near, far = jnp.where(at < 8, first, second), jnp.where(at < 8, far_first, far_second)
            value = jnp.where(core == side, near, far).astype(BF16)
            weights[piece * top : (piece + 1) * top, columns] = value[:top]
            start = 32 * top + piece * low
            weights[start : start + low, columns] = value[top:]


def attention_forward_kernel(count, full, *refs):
    parts = refs[:count]
    (gain, wq, wk, wv, wo, cos, sin, seg_row, seg_column) = refs[count : count + 9]
    refs = refs[count + 9 :]
    if full:
        places, gathered = refs[0], refs[1:9]
        refs = refs[9:]
    (x_out, a_out, q_out, kk_out, vv_out, mix_out, part_out) = refs[:7]
    x = parts[0][...].astype(F32)
    if count == 3:
        x = x + (parts[1][...] + parts[2][...])
    x_out[...] = x
    a = (x * row_factor(x) * gain[...].astype(F32)).astype(BF16)
    a_out[...] = a
    common = (cos[...], sin[...], allowed_pairs(seg_row[...], seg_column[...]))
    attend(a, wq[...], wk[...], wv[...], q_out, kk_out, vv_out, mix_out, *common)
    part_out[...] = mm(mix_out[...], wo[...])
    if full:
        q_other, kk_other, vv_other, part_other, weights, mix_other = refs[7:]
        unpack_gathered(places, gathered, weights)
        wq, wk, wv, wo = halves_of(weights)
        attend(a, wq[...], wk[...], wv[...], q_other, kk_other, vv_other, mix_other, *common)
        part_other[...] = mm(mix_other[...], wo[...])


ONCE = pl.Buffered(1)
SMEM = pl.BlockSpec(memory_space=pltpu.SMEM)
ANYWHERE = pl.BlockSpec(memory_space=pl.ANY)


def whole(shape):
    return pl.BlockSpec(shape, lambda i: (0,) * len(shape), pipeline_mode=ONCE)


def of_layer(layer, shape):
    return pl.BlockSpec(
        (None, *shape), lambda i: (layer,) + (0,) * len(shape), pipeline_mode=ONCE
    )


def params(mib):
    return pltpu.CompilerParams(
        vmem_limit_bytes=mib * MIB, dimension_semantics=("arbitrary",)
    )


def cost(flops, nbytes):
    return pl.CostEstimate(flops=flops, bytes_accessed=nbytes, transcendentals=0)


def attention_forward(layer, parts, weights, tables, segment, gathered=()):
    gain, wq, wk, wv, wo = weights
    length, features = parts[0].shape
    q_width, k_width = wq.shape[2], wk.shape[2]
    heads = 2 * k_width // LANES
    ins = [*parts, gain, wq, wk, wv, wo, *tables, *segment]
    in_specs = [whole(part.shape) for part in parts]
    in_specs += [of_layer(layer, w.shape[1:]) for w in (gain, wq, wk, wv, wo)]
    in_specs += [whole(t.shape) for t in (*tables, *segment)]
    outs = [
        ((length, features), F32),
        ((length, features), BF16),
        ((length, q_width), BF16),
        ((heads, length, LANES), BF16),
        ((heads, length, LANES), BF16),
        ((length, q_width), BF16),
        ((length, features), F32),
    ]
    scratch = []
    if gathered:
        ins += gathered
        in_specs += [SMEM, *(whole(array.shape) for array in gathered[1:])]
        outs += [outs[2], outs[3], outs[4], outs[6], ((4 * gathered[1].shape[0], features), BF16)]
        scratch = [pltpu.VMEM((length, q_width), BF16)]
    return pl.pallas_call(
        functools.partial(attention_forward_kernel, len(parts), bool(gathered)),
        grid=(1,),
        scratch_shapes=scratch,
        in_specs=in_specs,
        out_specs=[whole(shape) for shape, _ in outs],
        out_shape=[jax.ShapeDtypeStruct(*out) for out in outs],
        compiler_params=params(60),
        cost_estimate=cost(6 << 30, 8 * MIB),
        name="attention_forward",
    )(*ins)


def column_of(table, lane, index):
    return jnp.sum(jnp.where(lane == index, table, 0.0), axis=1, keepdims=True)


def expert_prologue(x, own, other, gain, router, mask, middle_out, xi_out, share_out):
    middle = x[...] + (own[...] + other[...])
    middle_out[...] = middle
    xi = (middle * row_factor(middle) * gain[...].astype(F32)).astype(BF16)
    xi_out[...] = xi
    logits = mm(xi, router[...])
    chosen = mask[...] > 0.5
    logits = jnp.where(chosen, logits, EXCLUDED)
    shifted = jnp.exp(logits - jnp.max(logits, axis=-1, keepdims=True))
    shifted = jnp.where(chosen, shifted, 0.0)
    share_out[...] = shifted / jnp.sum(shifted, axis=-1, keepdims=True)


def expert_step(gate_in, linear, wd, share):
    squashed = 1.0 / (1.0 + jnp.exp(-gate_in))
    silu = gate_in * squashed
    activation = (silu * linear).astype(BF16)
    return squashed, silu, activation, mm(activation, wd)


def expert_backward_step(places, g, xi, share, gate_in, linear, wg, wu, wd, keep, send):
    where_to = block_places(EXPERT_ORDERS, places, pl.program_id(0) >= STREAMS // 2)
    squashed, silu, activation, expert_out = expert_step(gate_in, linear, wd, share)
    gate_grad = jnp.sum(g * expert_out, axis=1, keepdims=True)
    expert_grad = (share * g).astype(BF16)
    activation_grad = mm_nt(expert_grad, wd)
    gate_in_grad = (
        activation_grad * linear * squashed * (1.0 + gate_in * (1.0 - squashed))
    ).astype(BF16)
    linear_grad = (activation_grad * silu).astype(BF16)
    width = activation.shape[1]
    store_blocks(keep, send, mm_tn(xi, gate_in_grad), 0, where_to)
    store_blocks(keep, send, mm_tn(xi, linear_grad), width, where_to)
    store_blocks(keep, send, mm_tn(expert_grad, activation), 2 * width, where_to)
    return gate_grad, mm_nt(gate_in_grad, wg) + mm_nt(linear_grad, wu), expert_out


def expert_forward_kernel(
    x, own, other, gain, router, mask, wg, wu, wd,
    middle_out, xi_out, share_out, gate_out, linear_out, part_out,
):
    expert = pl.program_id(0)

    @pl.when(expert == 0)
    def _():
        expert_prologue(x, own, other, gain, router, mask, middle_out, xi_out, share_out)
        part_out[...] = jnp.zeros_like(part_out)

    share = column_of(share_out[...], lane_of(share_out.shape[0]), expert)
    xi = xi_out[...]
    gate_in = mm(xi, wg[...])
    linear = mm(xi, wu[...])
    gate_out[...] = gate_in
    linear_out[...] = linear
    part_out[...] += share * expert_step(gate_in, linear, wd[...], share)[3]


def expert_both_kernel(
    places, x, own, other, gain, router, mask, wg, wu, wd, cotangent,
    middle_out, xi_out, share_out, part_out, back_out, keep, send,
):
    expert = pl.program_id(0)
    lane = lane_of(share_out.shape[0])

    @pl.when(expert == 0)
    def _():
        expert_prologue(x, own, other, gain, router, mask, middle_out, xi_out, share_out)
        part_out[...] = jnp.zeros_like(part_out)
        back_out[...] = jnp.zeros_like(back_out)

    share = column_of(share_out[...], lane, expert)
    xi = xi_out[...]
    gate_in = mm(xi, wg[...])
    linear = mm(xi, wu[...])
    gate_grad, back, expert_out = expert_backward_step(
        places, cotangent[...].astype(F32), xi, share, gate_in, linear, wg[...], wu[...],
        wd[...], keep, send,
    )
    part_out[...] += share * expert_out
    back_out[:, : back.shape[1]] += back
    back_out[:, back.shape[1] :] += jnp.where(lane == expert, gate_grad, 0.0)


def expert_backward_kernel(
    places, g_in, x, gain, own, other, xi_ref, share_ref, gate_ref, linear_ref, wg, wu, wd,
    *rest,
):
    g_out, gain_out, back_out, keep, send = rest[-5:]
    expert = pl.program_id(0)
    lane = lane_of(share_ref.shape[0])

    @pl.when(expert == 0)
    def _():
        stream = x[...]
        change, gain_row = norm_back(
            stream, row_factor(stream), gain[...].astype(F32), own[...] + other[...]
        )
        g_out[...] = g_in[...] + change
        gain_out[...] = jnp.broadcast_to(gain_row, gain_out.shape)
        back_out[...] = jnp.zeros_like(back_out)

    share = column_of(share_ref[...], lane, expert)
    gate_grad, back, _ = expert_backward_step(
        places, g_out[...], xi_ref[...], share, gate_ref[...], linear_ref[...], wg[...],
        wu[...], wd[...], keep, send,
    )
    back_out[:, : back.shape[1]] += back
    back_out[:, back.shape[1] :] += jnp.where(lane == expert, gate_grad, 0.0)


def of_expert(layer, shape):
    return pl.BlockSpec((None, None, *shape), lambda e: (layer, e, 0, 0))


def each_expert(shape):
    return pl.BlockSpec((None, *shape), lambda e: (e, 0, 0))


def with_gates(length, features):
    shape = (length, features + LANES)
    return whole(shape), (shape, F32)


def gradient_outs(rows, width):
    spec = pl.BlockSpec((rows, 3 * width), lambda e: (0, e))
    shape = ((rows, 3 * width * STREAMS), F32)
    return [(spec, shape)] * 2


def run_experts(kernel, name, ins, in_specs, outs, flops, nbytes, mib):
    return pl.pallas_call(
        kernel,
        grid=(STREAMS,),
        in_specs=in_specs,
        out_specs=[spec for spec, _ in outs],
        out_shape=[jax.ShapeDtypeStruct(*out) for _, out in outs],
        compiler_params=params(mib),
        cost_estimate=cost(flops, nbytes),
        name=name,
    )(*ins)


def expert_forward(layer, x, own, other, gain, router, mask, wg, wu, wd):
    length, features = x.shape
    width = wg.shape[3]
    big, low = ((length, features), F32), ((length, features), BF16)
    hidden = (each_expert((length, width)), ((STREAMS, length, width), F32))
    ins = [x, own, other, gain, router, mask, wg, wu, wd]
    in_specs = [whole(x.shape)] * 3 + [
        of_layer(layer, gain.shape[1:]),
        of_layer(layer, router.shape[1:]),
        of_layer(layer, mask.shape[1:]),
        *(of_expert(layer, w.shape[2:]) for w in (wg, wu, wd)),
    ]
    outs = [
        (whole(big[0]), big),
        (whole(low[0]), low),
        (whole((length, LANES)), ((length, LANES), F32)),
        hidden,
        hidden,
        (whole(big[0]), big),
    ]
    return run_experts(
        expert_forward_kernel, "experts_forward", ins, in_specs, outs, 8 << 30, 12 * MIB, 60
    )


def expert_both(layer, places, x, own, other, gain, router, mask, wg, wu, wd, cotangent):
    length, features = x.shape
    width = wg.shape[3]
    big, low = ((length, features), F32), ((length, features), BF16)
    table = (whole((length, LANES)), ((length, LANES), F32))
    ins = [places, x, own, other, gain, router, mask, wg, wu, wd, cotangent]
    in_specs = [SMEM] + [whole(x.shape)] * 3 + [
        of_layer(layer, gain.shape[1:]),
        of_layer(layer, router.shape[1:]),
        of_layer(layer, mask.shape[1:]),
        *(of_expert(layer, w.shape[2:]) for w in (wg, wu, wd)),
        whole(cotangent.shape),
    ]
    outs = [
        (whole(big[0]), big),
        (whole(low[0]), low),
        table,
        (whole(big[0]), big),
        with_gates(length, features),
        *gradient_outs(features // 2, width),
    ]
    return run_experts(
        expert_both_kernel, "experts_both", ins, in_specs, outs, 16 << 30, 30 * MIB, 60
    )


def expert_backward(
    layer, places, g, x, gain, own, other, xi, share, gate_in, linear, wg, wu, wd, after
):
    length, features = x.shape
    width = wg.shape[3]
    big = ((length, features), F32)
    hidden = each_expert((length, width))
    ins = [places, g, x, gain, own, other, xi, share, gate_in, linear, wg, wu, wd, *after]
    in_specs = [SMEM, whole(x.shape), whole(x.shape)] + [
        of_layer(layer + 1, gain.shape[1:]),
        whole(x.shape),
        whole(x.shape),
        whole(x.shape),
        whole(share.shape),
        hidden,
        hidden,
        *(of_expert(layer, w.shape[2:]) for w in (wg, wu, wd)),
        *([ANYWHERE] * len(after)),
    ]
    outs = [
        (whole(big[0]), big),
        (whole((8, features)), ((8, features), F32)),
        with_gates(length, features),
        *gradient_outs(features // 2, width),
    ]
    return run_experts(
        expert_backward_kernel, "experts_backward", ins, in_specs, outs, 4 << 30, 30 * MIB, 60
    )


def attend_backward(mixture_grad, q, kk, vv, cosine, sine, allowed):
    length = mixture_grad.shape[0]
    lane = lane_of(length)
    low = lane < HEAD_SIZE
    scale = HEAD_SIZE**-0.5
    query_grads, key_grads, value_grads = [], [], []
    for pair in range(q.shape[1] // LANES // 2):
        key_sides, value_sides = [], []
        for side in range(2):
            head = 2 * pair + side
            columns = slice(head * LANES, (head + 1) * LANES)
            stacked = stacked_pair(q[:, columns], lane)
            scores = jnp.where(allowed, mm_nt(stacked, kk[head]) * scale, EXCLUDED)
            shifted = jnp.exp(scores - jnp.max(scores, axis=-1, keepdims=True))
            probs = shifted / jnp.sum(shifted, axis=-1, keepdims=True)
            mix_grad = stacked_pair(mixture_grad[:, columns], lane)
            prob_grad = mm_nt(mix_grad, vv[head])
            inner = jnp.sum(probs * prob_grad, axis=-1, keepdims=True)
            score_grad = (probs * (prob_grad - inner)).astype(BF16)
            query = mm(score_grad, kk[head])
            query = jnp.where(low, query[:length], query[length:]) * scale
            query = query * cosine - partner(query, lane) * sine
            query_grads.append(query.astype(BF16))
            key = mm_tn(score_grad, stacked) * scale
            key_sides.append(key + pltpu.roll(key, HEAD_SIZE, 1))
            value = mm_tn(probs.astype(BF16), mix_grad)
            value_sides.append(value + pltpu.roll(value, HEAD_SIZE, 1))
        key = jnp.where(low, key_sides[0], key_sides[1])
        key_grads.append((key * cosine - partner(key, lane) * sine).astype(BF16))
        value_grads.append(jnp.where(low, value_sides[0], value_sides[1]).astype(BF16))
    return tuple(
        jnp.concatenate(grads, axis=1) for grads in (query_grads, key_grads, value_grads)
    )


def attention_backward_kernel(
    count, full, places, g, own, other, middle, xi, share, gain, router_rows,
    wo, mix, q, kk, vv, a, wq, wk, wv, cos, sin, seg_row, seg_column, x, late_gain, *rest,
):
    if full:
        q_other, kk_other, vv_other, weights = rest[:4]
        part_other = rest[-2]
        rest = rest[4:]
    g_out, part_out, keep, send = rest[count : count + 4]
    rows_scratch = rest[-1]
    where_to = block_places(ATTENTION_ORDERS, places)
    length = middle.shape[0]
    lane = lane_of(length)
    shares = share[...]
    features = middle.shape[1]
    gate_grad = own[:, features:] + other[:, features:]
    pick = shares * (gate_grad - jnp.sum(shares * gate_grad, axis=1, keepdims=True))
    input_grad = own[:, :features] + other[:, :features]
    xi_full = xi[...].astype(F32)
    rows_scratch[...] = jnp.zeros_like(rows_scratch)
    for expert in range(STREAMS):
        logit_grad = column_of(pick, lane, expert)
        input_grad = input_grad + logit_grad * router_rows[expert : expert + 1, :]
        rows_scratch[expert : expert + 1, :] = jnp.sum(
            xi_full * logit_grad, axis=0, keepdims=True
        )
    mid = middle[...]
    change, gain_row = norm_back(mid, row_factor(mid), gain[...].astype(F32), input_grad)
    rows_scratch[4:5, :] = gain_row
    rows_scratch[6:7, :] = late_gain[0:1, :]
    gradient = g[...].astype(F32) + change
    g_out[...] = gradient
    output_grad = gradient.astype(BF16)
    common = (cos[...], sin[...], allowed_pairs(seg_row[...], seg_column[...]))

    def half(output_weight, weights, *saved):
        mixture_grad = mm_nt(output_grad, output_weight[...]).astype(BF16)
        grads = attend_backward(mixture_grad, *saved, *common)
        part = sum(mm_nt(grad, weight[...]) for grad, weight in zip(grads, weights))
        return grads, part

    if full:
        wq_other, wk_other, wv_other, wo_other = halves_of(weights)
        part_other[...] = half(
            wo_other, (wq_other, wk_other, wv_other), q_other, kk_other, vv_other
        )[1]
    grads, attention_part = half(wo, (wq, wk, wv), q, kk, vv)
    part_out[...] = attention_part
    stream = x[...]
    rows_scratch[5:6, :] = jnp.sum(
        attention_part * stream * row_factor(stream), axis=0, keepdims=True
    )
    a_full = a[...]
    column = 0
    for total in (
        jnp.transpose(rows_scratch[...]),
        *(mm_tn(a_full, grad) for grad in grads),
        mm_tn(output_grad, mix[...]),
    ):
        store_blocks(keep, send, total, column, where_to)
        column += total.shape[1]


def attention_backward(
    layer, places, g, own, other, saved_experts, weights, saved, tables, segment, late_gain, after,
    others=(),
):
    middle, xi, share = saved_experts
    gain, router_rows, wo, wq, wk, wv = weights
    x, a, q, kk, vv, mix = saved
    length, features = middle.shape
    columns = SMALL + wq.shape[2] + wk.shape[2] + wv.shape[2] + wo.shape[1]
    ins = [
        places, g, own, other, middle, xi, share, gain, router_rows, wo,
        mix, q, kk, vv, a, wq, wk, wv, *tables, *segment, x, late_gain,
    ]
    layered = {7, 8, 9, 15, 16, 17}
    in_specs = [SMEM]
    for at, array in enumerate(ins[1:], 1):
        in_specs.append(of_layer(layer, array.shape[1:]) if at in layered else whole(array.shape))
    ins += [*others, *after]
    in_specs += [whole(array.shape) for array in others]
    in_specs += [ANYWHERE] * len(after)
    outs = [
        ((length, features), F32),
        ((length, features), F32),
        ((features // 2, columns), F32),
        ((features // 2, columns), F32),
    ]
    if others:
        outs.append(((length, features), F32))
    return pl.pallas_call(
        functools.partial(
            attention_backward_kernel, len(after), bool(others)
        ),
        grid=(1,),
        in_specs=in_specs,
        out_specs=[whole(shape) for shape, _ in outs],
        out_shape=[jax.ShapeDtypeStruct(*out) for out in outs],
        scratch_shapes=[pltpu.VMEM((LANES, features), F32)],
        compiler_params=params(60),
        cost_estimate=cost(16 << 30, 18 * MIB),
        name="attention_backward",
    )(*ins)


SWAP = ((0, 1), (1, 0))
RING = {"u": tuple((i, i ^ 1) for i in range(4)), "v": tuple((i, 3 - i) for i in range(4))}


def exchange(array):
    return lax.ppermute(array, "tensor", SWAP)


RING_AXES = ("dp_0", "dp_2", "dp_3")


def ring_pairs(orders, step):
    pairs = []
    for x in range(4):
        for z in range(4):
            for core in range(2):
                ring, kind = orders[core][step]
                at = x if ring == "x" else z
                to = at ^ 1 if kind == "u" else 3 - at
                there = (to, z) if ring == "x" else (x, to)
                pairs.append(((x * 4 + z) * 2 + core, (there[0] * 4 + there[1]) * 2 + core))
    return pairs


def halve_kernel(groups, rows, *refs):
    count = sum(len(terms) for streams in groups for terms, _ in streams)
    ins, outs = iter(refs[:count]), iter(refs[count:])
    for streams in groups:
        kept, sent = next(outs), next(outs)
        column = 0
        for terms, width in streams:
            total = next(ins)[...]
            for _ in terms[1:]:
                total = total + next(ins)[...]
            kept[:, column : column + width] = total[: rows // 2]
            sent[:, column : column + width] = total[rows // 2 :]
            column += width


def halve(rows, *groups):
    plan, ins, in_specs, outs = [], [], [], []
    for streams in groups:
        plan.append([])
        for terms in streams:
            width = min((term[0] if isinstance(term, tuple) else term).shape[1] for term in terms)
            for term in terms:
                array, at = term if isinstance(term, tuple) else (term, 0)
                ins.append(array)
                in_specs.append(
                    pl.BlockSpec((rows, width), lambda i, at=at: (0, at), pipeline_mode=ONCE)
                )
            plan[-1].append((terms, width))
        outs += [(rows // 2, sum(width for _, width in plan[-1]))] * 2
    found = pl.pallas_call(
        functools.partial(halve_kernel, plan, rows),
        grid=(1,),
        in_specs=in_specs,
        out_specs=[whole(shape) for shape in outs],
        out_shape=[jax.ShapeDtypeStruct(shape, F32) for shape in outs],
        compiler_params=params(60),
        cost_estimate=cost(1 << 20, 8 * MIB),
        name="halve",
    )(*ins)
    return [list(found[at : at + 2]) for at in range(0, len(found), 2)]


def move(send, orders, step):
    return lax.ppermute(send, RING_AXES, ring_pairs(orders, step))


def both_streams(sends, step):
    return [
        move(send, orders, step) for send, orders in zip(sends, (EXPERT_ORDERS, crossed(EXPERT_ORDERS)))
    ]


def begin_experts(keep, received):
    half, width = keep.shape[0] // 2, keep.shape[1] // 2
    return [
        keep[half:, at : at + width] + received[half:, at : at + width] for at in (0, width)
    ]


def expert_streams(keep, received, moved):
    return [[[(keep, at), (received, at), moved[at]]] for at in range(2)]


def turned(block):
    rows, columns = block.shape
    filled = jnp.concatenate([block, jnp.zeros((LANES - rows, columns), F32)], axis=0)
    return jnp.transpose(filled)[:, :rows]


def unpack_kernel(
    layers, experts, kept, moved, small, query, key, value, projection, gate, up, down
):
    hidden = gate.shape[-1]
    total = kept[...] + moved[...]
    column = 0
    for stream in range(2):
        for layer in range(layers):
            for at in range(experts // 2):
                expert = stream * (experts // 2) + at
                gate[layer, expert] = total[:, column : column + hidden]
                up[layer, expert] = total[:, column + hidden : column + 2 * hidden]
                down[layer, expert] = turned(total[:, column + 2 * hidden : column + 3 * hidden])
                column += 3 * hidden
    for layer in range(layers):
        for out in (small, query, key, value):
            width = out.shape[-1]
            out[layer] = total[:, column : column + width]
            column += width
        width = projection.shape[1]
        projection[layer] = turned(total[:, column : column + width])
        column += width


def unpack_sums(kept, moved, layers, experts, hidden, widths, depth):
    rows = kept.shape[0]
    outs = [
        (layers, rows, SMALL),
        *((layers, rows, width) for width in widths),
        (layers, depth, rows),
        (layers, experts, rows, hidden),
        (layers, experts, rows, hidden),
        (layers, experts, hidden, rows),
    ]
    return pl.pallas_call(
        functools.partial(unpack_kernel, layers, experts),
        grid=(1,),
        in_specs=[whole(kept.shape)] * 2,
        out_specs=[whole(shape) for shape in outs],
        out_shape=[jax.ShapeDtypeStruct(shape, F32) for shape in outs],
        compiler_params=params(60),
        name="unpack_sums",
    )(kept, moved)


class Gather:
    def __init__(self, weights, layer):
        x, z, core = (lax.axis_index(name) for name in RING_AXES)
        piece = (x * 4 + z) * 2 + core

        def rows_of(weight):
            rows = weight.shape[1] // 32
            return lax.dynamic_slice_in_dim(weight[layer], piece * rows, rows, 0).astype(F32)

        *inputs, output = (rows_of(weight) for weight in weights)
        self.piece = jnp.concatenate([jnp.concatenate(inputs, axis=1), output], axis=0)
        orders = [*EXPERT_ORDERS, *(swapped(order) for order in EXPERT_ORDERS)]
        places = [ring_place(order, x, z) for order in orders]
        self.places = jnp.stack([*places, core]).astype(jnp.int32)

        self.crossed = exchange(self.piece)

    def begin(self, after, received):
        held, *_ = behind([self.crossed], after)
        for step in (3, 2):
            moved = lax.ppermute(held, RING_AXES, ring_pairs(EXPERT_ORDERS, step))
            held = jnp.concatenate([held, moved], axis=0)
        half = held.shape[1] // 2
        self.held = behind([held[:, :half], held[:, half:]], received)
        self.moved = self.moves(self.held, 1)

    def moves(self, held, step):
        return [
            lax.ppermute(half, RING_AXES, ring_pairs(EXPERT_ORDERS, at))
            for half, at in zip(held, (step, 1 - step))
        ]

    def finish(self, after):
        held = behind(self.held, after)
        held = [jnp.concatenate(pair, axis=0) for pair in zip(held, self.moved)]
        near = [*held, *self.moves(held, 0)]
        return [self.places, *near, *(lax.ppermute(half, "dp_3", SWAP) for half in near)]


def behind(arrays, *after):
    return pl.pallas_call(
        lambda *refs: None,
        in_specs=[ANYWHERE] * (len(arrays) + len(after)),
        out_specs=[ANYWHERE] * len(arrays),
        out_shape=[jax.ShapeDtypeStruct(array.shape, array.dtype) for array in arrays],
        input_output_aliases={at: at for at in range(len(arrays))},
        name="behind",
    )(*arrays, *after)


def rope_tables(length):
    half = HEAD_SIZE // 2
    frequency = np.float32(THETA) ** (-2.0 * np.arange(half, dtype=np.float32) / HEAD_SIZE)
    angles = np.arange(length, dtype=np.float32)[:, None] * frequency[None].astype(np.float32)
    angles = angles.astype(np.float32)
    cosine = np.tile(np.cos(angles), (1, LANES // half)).astype(np.float32)
    sine = np.sin(angles)
    sine = np.tile(np.concatenate([-sine, sine], axis=1), (1, LANES // HEAD_SIZE))
    return jnp.asarray(cosine), jnp.asarray(sine.astype(np.float32))


def shards(
    tokens, segments, routes, norm_attention, query_weight, key_matrix, value_matrix,
    output_weight, norm_experts, router_weight, gate_weight, up_weight, down_weight, cotangent,
):
    length, features = tokens.shape
    experts = gate_weight.shape[1]
    hidden = gate_weight.shape[3]
    tables = rope_tables(length)
    segment = (segments.reshape(1, length), segments.reshape(length, 1))
    gain_attention = norm_attention[:, None, :]
    gain_experts = norm_experts[:, None, :]
    router = jnp.pad(router_weight, ((0, 0), (0, 0), (0, LANES - experts)))
    router_rows = jnp.pad(
        jnp.swapaxes(router_weight, 1, 2).astype(F32), ((0, 0), (0, 8 - experts), (0, 0))
    )
    mask = jnp.any(
        routes[..., None] == jnp.arange(LANES, dtype=jnp.int32), axis=2
    ).astype(F32)
    x_at, y_at, z_at = (lax.axis_index(name) for name in DP[:3])
    core = lax.axis_index("dp_3")

    def places_in(orders):
        found = []
        for which in (orders, crossed(orders)):
            one, two = (place(order, x_at, y_at, z_at) for order in which)
            found += [jnp.where(core == 0, one, two), jnp.where(core == 0, two, one)]
        return jnp.stack([*found, core]).astype(jnp.int32)

    expert_places = places_in(EXPERT_ORDERS)
    attention_places = places_in(ATTENTION_ORDERS)

    attention_weights = (gain_attention, query_weight, key_matrix, value_matrix, output_weight)
    expert_weights = (gate_weight, up_weight, down_weight)
    back_weights = (
        gain_experts, router_rows, output_weight, query_weight, key_matrix, value_matrix,
    )

    others = Gather(attention_weights[1:], 1)
    x1, *saved1, part = attention_forward(0, [tokens], attention_weights, tables, segment)
    other = exchange(part)
    others.begin(part, other)
    middle1, xi1, share1, gate1, linear1, part = expert_forward(
        0, x1, part, other, gain_experts, router, mask, *expert_weights
    )
    x2, *saved2, part, q_other, kk_other, vv_other, part_other, weights_other = attention_forward(
        1, [middle1, part, exchange(part)], attention_weights, tables, segment,
        others.finish(part),
    )
    middle2, xi2, share2, last, back, keep, send = expert_both(
        1, expert_places, x2, part, part_other, gain_experts, router, mask, *expert_weights,
        cotangent,
    )
    half = features // 4
    keep_e2, received_e2 = keep, lax.ppermute(send, "dp_3", SWAP)
    other = exchange(back)
    *sends, last = behind([*begin_experts(keep_e2, received_e2), last], other)
    moved = both_streams(sends, 0)
    last_other = exchange(last)
    no_gain = jnp.zeros((8, features), F32)
    g2, part, keep, send, part_other = attention_backward(
        1, attention_places, cotangent, back, other, (middle2, xi2, share2), back_weights,
        (x2, *saved2), tables, segment, no_gain, sends,
        (q_other, kk_other, vv_other, weights_other),
    )
    keep_a2, received_a2 = keep, lax.ppermute(send, "dp_3", SWAP)
    held_e2 = halve(half, *expert_streams(keep_e2, received_e2, moved))
    sends = [send for _, send in held_e2]
    g1, late_gain, back, keep, send = expert_backward(
        0, expert_places, g2, x2, gain_attention, part, part_other, xi1, share1, gate1,
        linear1, *expert_weights, [*sends, last_other],
    )
    moved_e2 = both_streams(sends, 1)
    keep_e1, received_e1 = keep, lax.ppermute(send, "dp_3", SWAP)
    other = exchange(back)
    send_a2 = keep_a2[half:] + received_a2[half:]
    moved_a2 = move(send_a2, ATTENTION_ORDERS, 0)
    sends = begin_experts(keep_e1, received_e1)
    moved_e1 = both_streams(sends, 0)
    g0, part, keep, send = attention_backward(
        0, attention_places, g1, back, other, (middle1, xi1, share1), back_weights,
        (x1, *saved1), tables, segment, late_gain, [send_a2, *sends, *moved_e2],
    )
    (send,) = behind([send], moved_a2, *moved_e1)
    keep_a1, received_a1 = keep, lax.ppermute(send, "dp_3", SWAP)
    *held_e1, held_a2 = halve(
        half, *expert_streams(keep_e1, received_e1, moved_e1), [[keep_a2, received_a2, moved_a2]]
    )
    sends = [send for _, send in held_e1]
    moved_e1 = both_streams(sends, 1)
    moved_a2 = move(held_a2[1], ATTENTION_ORDERS, 1)
    (received_a1,) = behind([received_a1], *sends)
    ((kept_a1, send),) = halve(2 * half, [[keep_a1, received_a1]])
    moved_a1 = move(send, ATTENTION_ORDERS, 0)
    moved_e1 = behind(moved_e1, send)
    held_e = halve(
        half // 2,
        *(
            [[one[0], first], [two[0], second]]
            for one, first, two, second in zip(held_e1, moved_e1, held_e2, moved_e2)
        ),
    )
    sends = [send for _, send in held_e]
    moved_e = both_streams(sends, 2)
    other = exchange(part)
    (moved_a1,) = behind([moved_a1], *sends, other)
    (held_a1,) = halve(half, [[kept_a1, moved_a1]])
    moved_a1 = move(held_a1[1], ATTENTION_ORDERS, 1)
    held_e = halve(half // 4, *([[held[0], moved]] for held, moved in zip(held_e, moved_e)))
    sends = [send for _, send in held_e]
    moved_e = both_streams(sends, 3)
    (moved_a1,) = behind([moved_a1], *sends)
    (held_a,) = halve(half // 2, [[held_a1[0], moved_a1], [held_a2[0], moved_a2]])
    moved_a = move(held_a[1], ATTENTION_ORDERS, 2)
    (other,) = behind([other], moved_a)
    (held_a,) = halve(half // 4, [[held_a[0], moved_a]])
    moved_a = move(held_a[1], ATTENTION_ORDERS, 3)
    ((kept, send),) = halve(
        half // 8,
        [*([held[0], moved] for held, moved in zip(held_e, moved_e)), [held_a[0], moved_a]],
    )
    widths = (query_weight.shape[2], key_matrix.shape[2], value_matrix.shape[2])
    sums = unpack_sums(
        kept, lax.ppermute(send, "dp_1", SWAP), query_weight.shape[0], experts, hidden, widths,
        output_weight.shape[1],
    )
    gain = norm_attention[0].astype(F32)
    change, _ = norm_back(x1, row_factor(x1), gain, part + other)
    gradient = g0 + change
    output = (middle2 + (last + last_other)).astype(BF16)

    small, *attention_sums, gate_sum, up_sum, down_sum = sums
    attention_gain = small[:, :, 5]
    attention_gain = attention_gain + exchange(attention_gain)
    return (
        output,
        gradient,
        attention_gain,
        *attention_sums,
        small[:, :, 4],
        small[:, :, :experts],
        gate_sum,
        up_sum,
        down_sum,
    )


def solution(mesh):
    torus = Mesh(
        mesh.devices.reshape(*DP_SIZES, mesh.shape["tensor"]), (*DP, "tensor")
    )
    rows, copied, last = P(DP, None), P(), P(None, None, "tensor")
    in_specs = (
        rows, rows, P(None, DP, None), copied, last, last, last, P(None, "tensor", None),
        copied, copied, P(None, None, None, "tensor"), P(None, None, None, "tensor"),
        P(None, None, "tensor", None), rows,
    )
    out_specs = (
        rows, rows, P(None, DP), P(None, DP, "tensor"), P(None, DP, "tensor"),
        P(None, DP, "tensor"), P(None, "tensor", DP), P(None, DP), P(None, DP, None),
        P(None, None, DP, "tensor"), P(None, None, DP, "tensor"), P(None, None, "tensor", DP),
    )
    return jax.shard_map(
        shards, mesh=torus, in_specs=in_specs, out_specs=out_specs, check_vma=False
    )
```

```python
import functools

import jax
import jax.numpy as jnp
import numpy as np
from jax import lax
from jax.experimental import pallas as pl
from jax.experimental.pallas import tpu as pltpu
from jax.sharding import Mesh
from jax.sharding import PartitionSpec as P

HEAD_SIZE = 64
LANES = 128
STREAMS = 4
SMALL = 128
DP = ("dp_0", "dp_1", "dp_2", "dp_3")
DP_SIZES = (4, 2, 4, 2)
EPSILON = 1e-06
THETA = 10000.0
EXCLUDED = -1e30
F32 = jnp.float32
BF16 = jnp.bfloat16
MIB = 1024 * 1024

EXPERT_ORDERS = (
    (("x", "u"), ("z", "u"), ("z", "v"), ("x", "v")),
    (("z", "v"), ("x", "v"), ("x", "u"), ("z", "u")),
)
ATTENTION_ORDERS = (
    (("z", "v"), ("x", "v"), ("x", "u"), ("z", "u")),
    (("x", "u"), ("z", "u"), ("z", "v"), ("x", "v")),
)


def swapped(order):
    return (order[1], order[0], *order[2:])


def crossed(order):
    return (order[1], order[0], order[3], order[2])


def pair_bit(index, kind):
    high = index // 2
    if kind == "v":
        return high
    return high ^ (index % 2)


def ring_place(order, x, z):
    at = 0
    for ring, kind in order:
        at = at * 2 + pair_bit(x if ring == "x" else z, kind)
    return at


def place(order, x, yh, z):
    return ring_place(order, x, z) * 2 + yh


def mm(a, b):
    return lax.dot_general(a, b, (((1,), (0,)), ((), ())), preferred_element_type=F32)


def mm_nt(a, b):
    return lax.dot_general(a, b, (((1,), (1,)), ((), ())), preferred_element_type=F32)


def mm_tn(a, b):
    return lax.dot_general(a, b, (((0,), (0,)), ((), ())), preferred_element_type=F32)


def row_factor(stream):
    return lax.rsqrt(jnp.mean(stream * stream, axis=-1, keepdims=True) + EPSILON)


def norm_back(stream, factor, gain, gradient):
    weighted = gradient * gain
    inner = jnp.sum(weighted * stream, axis=-1, keepdims=True) * (1.0 / stream.shape[-1])
    change = factor * weighted - stream * (factor * factor * factor) * inner
    return change, jnp.sum(gradient * stream * factor, axis=0, keepdims=True)


def lane_of(rows):
    return lax.broadcasted_iota(jnp.int32, (rows, LANES), 1)


def partner(block, lane):
    back = pltpu.roll(block, LANES - HEAD_SIZE // 2, 1)
    ahead = pltpu.roll(block, HEAD_SIZE // 2, 1)
    return jnp.where(lane % HEAD_SIZE < HEAD_SIZE // 2, back, ahead)


def both_heads(block, lane):
    rolled = pltpu.roll(block, HEAD_SIZE, 1)
    low = lane < HEAD_SIZE
    return jnp.where(low, block, rolled), jnp.where(low, rolled, block)


def stacked_pair(block, lane):
    zero = jnp.zeros_like(block)
    low = lane < HEAD_SIZE
    return jnp.concatenate(
        [jnp.where(low, block, zero), jnp.where(low, zero, block)], axis=0
    )


def allowed_pairs(seg_row, seg_column):
    length = seg_column.shape[0]
    rows = lax.broadcasted_iota(jnp.int32, (length, length), 0)
    columns = lax.broadcasted_iota(jnp.int32, (length, length), 1)
    allowed = (columns <= rows) & (seg_column == seg_row)
    bias = jnp.where(allowed, 0.0, 1.0)
    return jnp.concatenate([bias, bias], axis=0) < 0.5


def block_places(orders, places, later=False):
    core = places[4]
    found = []
    for block in range(32):
        x, yh, z = block // 8, (block // 4) % 2, block % 4
        one, two = (
            jnp.where(later, place(crossed(order), x, yh, z), place(order, x, yh, z))
            for order in orders
        )
        own = jnp.where(later, places[2], places[0])
        far = jnp.where(later, places[3], places[1])
        found.append((jnp.where(core == 0, one, two) ^ own, jnp.where(core == 0, two, one) ^ far))
    return core, found


def store_blocks(keep_ref, send_ref, value, column, where_to):
    core, found = where_to
    rows = value.shape[0] // 64
    columns = slice(column, column + value.shape[1])
    for block, (kept, sent) in enumerate(found):
        first = value[2 * block * rows : (2 * block + 1) * rows]
        second = value[(2 * block + 1) * rows : (2 * block + 2) * rows]
        keep_ref[pl.ds(pl.multiple_of(kept * rows, rows), rows), columns] = jnp.where(
            core == 0, first, second
        )
        send_ref[pl.ds(pl.multiple_of(sent * rows, rows), rows), columns] = jnp.where(
            core == 0, second, first
        )


def attend(a, wq, wk, wv, q_out, kk_out, vv_out, mix_out, cosine, sine, allowed):
    length = a.shape[0]
    lane = lane_of(length)
    q = mm(a, wq)
    k = mm(a, wk)
    v = mm(a, wv)
    scale = HEAD_SIZE**-0.5
    for pair in range(k.shape[1] // LANES):
        at = slice(pair * LANES, (pair + 1) * LANES)
        k_block = k[:, at] * cosine + partner(k[:, at], lane) * sine
        k_twice = both_heads(k_block, lane)
        v_twice = both_heads(v[:, at], lane)
        for side in range(2):
            head = 2 * pair + side
            columns = slice(head * LANES, (head + 1) * LANES)
            kk = k_twice[side].astype(BF16)
            vv = v_twice[side].astype(BF16)
            kk_out[head] = kk
            vv_out[head] = vv
            q_block = q[:, columns]
            q_block = (q_block * cosine + partner(q_block, lane) * sine).astype(BF16)
            q_out[:, columns] = q_block
            scores = mm_nt(stacked_pair(q_block, lane), kk) * scale
            scores = jnp.where(allowed, scores, EXCLUDED)
            shifted = jnp.exp(scores - jnp.max(scores, axis=-1, keepdims=True))
            probs = (shifted / jnp.sum(shifted, axis=-1, keepdims=True)).astype(BF16)
            mixed = mm(probs, vv)
            mix_out[:, columns] = jnp.where(
                lane < HEAD_SIZE, mixed[:length], mixed[length:]
            ).astype(BF16)


def halves_of(weights):
    depth = 2 * weights.shape[0] // 3
    quarter = depth // 4
    return (
        weights.at[:depth, : 2 * quarter],
        weights.at[:depth, 2 * quarter : 3 * quarter],
        weights.at[:depth, 3 * quarter :],
        weights.at[depth:, :],
    )


def unpack_gathered(places, gathered, weights):
    core = places[4]
    rows = gathered[0].shape[0] // 8
    width = gathered[0].shape[1]
    top, low = 2 * rows // 3, rows // 3
    for piece in range(32):
        x, z, side = piece // 8, (piece // 2) % 4, piece % 2
        for part in range(2):
            order = EXPERT_ORDERS[side] if part == 0 else swapped(EXPERT_ORDERS[side])
            at = ring_place(order, x, z) ^ places[2 * part + side]
            rows_at = pl.ds(pl.multiple_of((at & 7) * rows, rows), rows)
            columns = slice(part * width, (part + 1) * width)
            first, second, far_first, far_second = (
                gathered[2 * pair + part][rows_at, :] for pair in range(4)
            )
            near, far = jnp.where(at < 8, first, second), jnp.where(at < 8, far_first, far_second)
            value = jnp.where(core == side, near, far).astype(BF16)
            weights[piece * top : (piece + 1) * top, columns] = value[:top]
            start = 32 * top + piece * low
            weights[start : start + low, columns] = value[top:]


def attention_forward_kernel(count, full, *refs):
    parts = refs[:count]
    (gain, wq, wk, wv, wo, cos, sin, seg_row, seg_column) = refs[count : count + 9]
    refs = refs[count + 9 :]
    if full:
        places, gathered = refs[0], refs[1:9]
        refs = refs[9:]
    (x_out, a_out, q_out, kk_out, vv_out, mix_out, part_out) = refs[:7]
    x = parts[0][...].astype(F32)
    if count == 3:
        x = x + (parts[1][...] + parts[2][...])
    x_out[...] = x
    a = (x * row_factor(x) * gain[...].astype(F32)).astype(BF16)
    a_out[...] = a
    common = (cos[...], sin[...], allowed_pairs(seg_row[...], seg_column[...]))
    attend(a, wq[...], wk[...], wv[...], q_out, kk_out, vv_out, mix_out, *common)
    part_out[...] = mm(mix_out[...], wo[...])
    if full:
        q_other, kk_other, vv_other, part_other, weights, mix_other = refs[7:]
        unpack_gathered(places, gathered, weights)
        wq, wk, wv, wo = halves_of(weights)
        attend(a, wq[...], wk[...], wv[...], q_other, kk_other, vv_other, mix_other, *common)
        part_other[...] = mm(mix_other[...], wo[...])


ONCE = pl.Buffered(1)
SMEM = pl.BlockSpec(memory_space=pltpu.SMEM)
ANYWHERE = pl.BlockSpec(memory_space=pl.ANY)


def whole(shape):
    return pl.BlockSpec(shape, lambda i: (0,) * len(shape), pipeline_mode=ONCE)


def of_layer(layer, shape):
    return pl.BlockSpec(
        (None, *shape), lambda i: (layer,) + (0,) * len(shape), pipeline_mode=ONCE
    )


def params(mib):
    return pltpu.CompilerParams(
        vmem_limit_bytes=mib * MIB, dimension_semantics=("arbitrary",)
    )


def cost(flops, nbytes):
    return pl.CostEstimate(flops=flops, bytes_accessed=nbytes, transcendentals=0)


def attention_forward(layer, parts, weights, tables, segment, gathered=()):
    gain, wq, wk, wv, wo = weights
    length, features = parts[0].shape
    q_width, k_width = wq.shape[2], wk.shape[2]
    heads = 2 * k_width // LANES
    ins = [*parts, gain, wq, wk, wv, wo, *tables, *segment]
    in_specs = [whole(part.shape) for part in parts]
    in_specs += [of_layer(layer, w.shape[1:]) for w in (gain, wq, wk, wv, wo)]
    in_specs += [whole(t.shape) for t in (*tables, *segment)]
    outs = [
        ((length, features), F32),
        ((length, features), BF16),
        ((length, q_width), BF16),
        ((heads, length, LANES), BF16),
        ((heads, length, LANES), BF16),
        ((length, q_width), BF16),
        ((length, features), F32),
    ]
    scratch = []
    if gathered:
        ins += gathered
        in_specs += [SMEM, *(whole(array.shape) for array in gathered[1:])]
        outs += [outs[2], outs[3], outs[4], outs[6], ((4 * gathered[1].shape[0], features), BF16)]
        scratch = [pltpu.VMEM((length, q_width), BF16)]
    return pl.pallas_call(
        functools.partial(attention_forward_kernel, len(parts), bool(gathered)),
        grid=(1,),
        scratch_shapes=scratch,
        in_specs=in_specs,
        out_specs=[whole(shape) for shape, _ in outs],
        out_shape=[jax.ShapeDtypeStruct(*out) for out in outs],
        compiler_params=params(60),
        cost_estimate=cost(6 << 30, 8 * MIB),
        name="attention_forward",
    )(*ins)


def column_of(table, lane, index):
    return jnp.sum(jnp.where(lane == index, table, 0.0), axis=1, keepdims=True)


def expert_prologue(x, own, other, gain, router, mask, middle_out, xi_out, share_out):
    middle = x[...] + (own[...] + other[...])
    middle_out[...] = middle
    xi = (middle * row_factor(middle) * gain[...].astype(F32)).astype(BF16)
    xi_out[...] = xi
    logits = mm(xi, router[...])
    chosen = mask[...] > 0.5
    logits = jnp.where(chosen, logits, EXCLUDED)
    shifted = jnp.exp(logits - jnp.max(logits, axis=-1, keepdims=True))
    shifted = jnp.where(chosen, shifted, 0.0)
    share_out[...] = shifted / jnp.sum(shifted, axis=-1, keepdims=True)


def expert_step(gate_in, linear, wd, share):
    squashed = 1.0 / (1.0 + jnp.exp(-gate_in))
    silu = gate_in * squashed
    activation = (silu * linear).astype(BF16)
    return squashed, silu, activation, mm(activation, wd)


def expert_backward_step(places, g, xi, share, gate_in, linear, wg, wu, wd, keep, send):
    where_to = block_places(EXPERT_ORDERS, places, pl.program_id(0) >= STREAMS // 2)
    squashed, silu, activation, expert_out = expert_step(gate_in, linear, wd, share)
    gate_grad = jnp.sum(g * expert_out, axis=1, keepdims=True)
    expert_grad = (share * g).astype(BF16)
    activation_grad = mm_nt(expert_grad, wd)
    gate_in_grad = (
        activation_grad * linear * squashed * (1.0 + gate_in * (1.0 - squashed))
    ).astype(BF16)
    linear_grad = (activation_grad * silu).astype(BF16)
    width = activation.shape[1]
    store_blocks(keep, send, mm_tn(xi, gate_in_grad), 0, where_to)
    store_blocks(keep, send, mm_tn(xi, linear_grad), width, where_to)
    store_blocks(keep, send, mm_tn(expert_grad, activation), 2 * width, where_to)
    return gate_grad, mm_nt(gate_in_grad, wg) + mm_nt(linear_grad, wu), expert_out


def expert_forward_kernel(
    x, own, other, gain, router, mask, wg, wu, wd,
    middle_out, xi_out, share_out, gate_out, linear_out, part_out,
):
    expert = pl.program_id(0)

    @pl.when(expert == 0)
    def _():
        expert_prologue(x, own, other, gain, router, mask, middle_out, xi_out, share_out)
        part_out[...] = jnp.zeros_like(part_out)

    share = column_of(share_out[...], lane_of(share_out.shape[0]), expert)
    xi = xi_out[...]
    gate_in = mm(xi, wg[...])
    linear = mm(xi, wu[...])
    gate_out[...] = gate_in
    linear_out[...] = linear
    part_out[...] += share * expert_step(gate_in, linear, wd[...], share)[3]


def expert_both_kernel(
    places, x, own, other, gain, router, mask, wg, wu, wd, cotangent,
    middle_out, xi_out, share_out, part_out, back_out, gate_grad_out, keep, send,
):
    expert = pl.program_id(0)
    lane = lane_of(share_out.shape[0])

    @pl.when(expert == 0)
    def _():
        expert_prologue(x, own, other, gain, router, mask, middle_out, xi_out, share_out)
        part_out[...] = jnp.zeros_like(part_out)
        back_out[...] = jnp.zeros_like(back_out)
        gate_grad_out[...] = jnp.zeros_like(gate_grad_out)

    share = column_of(share_out[...], lane, expert)
    xi = xi_out[...]
    gate_in = mm(xi, wg[...])
    linear = mm(xi, wu[...])
    gate_grad, back, expert_out = expert_backward_step(
        places, cotangent[...].astype(F32), xi, share, gate_in, linear, wg[...], wu[...],
        wd[...], keep, send,
    )
    part_out[...] += share * expert_out
    back_out[...] += back
    gate_grad_out[...] += jnp.where(lane == expert, gate_grad, 0.0)


def expert_backward_kernel(
    places, g_in, x, gain, own, other, xi_ref, share_ref, gate_ref, linear_ref, wg, wu, wd,
    *rest,
):
    g_out, gain_out, back_out, keep, send = rest[-5:]
    expert = pl.program_id(0)
    lane = lane_of(share_ref.shape[0])

    @pl.when(expert == 0)
    def _():
        stream = x[...]
        change, gain_row = norm_back(
            stream, row_factor(stream), gain[...].astype(F32), own[...] + other[...]
        )
        g_out[...] = g_in[...] + change
        gain_out[...] = jnp.broadcast_to(gain_row, gain_out.shape)
        back_out[...] = jnp.zeros_like(back_out)

    share = column_of(share_ref[...], lane, expert)
    gate_grad, back, _ = expert_backward_step(
        places, g_out[...], xi_ref[...], share, gate_ref[...], linear_ref[...], wg[...],
        wu[...], wd[...], keep, send,
    )
    back_out[:, : back.shape[1]] += back
    back_out[:, back.shape[1] :] += jnp.where(lane == expert, gate_grad, 0.0)


def of_expert(layer, shape):
    return pl.BlockSpec((None, None, *shape), lambda e: (layer, e, 0, 0))


def each_expert(shape):
    return pl.BlockSpec((None, *shape), lambda e: (e, 0, 0))


def gradient_outs(rows, width):
    spec = pl.BlockSpec((rows, 3 * width), lambda e: (0, e))
    shape = ((rows, 3 * width * STREAMS), F32)
    return [(spec, shape)] * 2


def run_experts(kernel, name, ins, in_specs, outs, flops, nbytes, mib):
    return pl.pallas_call(
        kernel,
        grid=(STREAMS,),
        in_specs=in_specs,
        out_specs=[spec for spec, _ in outs],
        out_shape=[jax.ShapeDtypeStruct(*out) for _, out in outs],
        compiler_params=params(mib),
        cost_estimate=cost(flops, nbytes),
        name=name,
    )(*ins)


def expert_forward(layer, x, own, other, gain, router, mask, wg, wu, wd):
    length, features = x.shape
    width = wg.shape[3]
    big, low = ((length, features), F32), ((length, features), BF16)
    hidden = (each_expert((length, width)), ((STREAMS, length, width), F32))
    ins = [x, own, other, gain, router, mask, wg, wu, wd]
    in_specs = [whole(x.shape)] * 3 + [
        of_layer(layer, gain.shape[1:]),
        of_layer(layer, router.shape[1:]),
        of_layer(layer, mask.shape[1:]),
        *(of_expert(layer, w.shape[2:]) for w in (wg, wu, wd)),
    ]
    outs = [
        (whole(big[0]), big),
        (whole(low[0]), low),
        (whole((length, LANES)), ((length, LANES), F32)),
        hidden,
        hidden,
        (whole(big[0]), big),
    ]
    return run_experts(
        expert_forward_kernel, "experts_forward", ins, in_specs, outs, 8 << 30, 12 * MIB, 60
    )


def expert_both(layer, places, x, own, other, gain, router, mask, wg, wu, wd, cotangent):
    length, features = x.shape
    width = wg.shape[3]
    big, low = ((length, features), F32), ((length, features), BF16)
    table = (whole((length, LANES)), ((length, LANES), F32))
    ins = [places, x, own, other, gain, router, mask, wg, wu, wd, cotangent]
    in_specs = [SMEM] + [whole(x.shape)] * 3 + [
        of_layer(layer, gain.shape[1:]),
        of_layer(layer, router.shape[1:]),
        of_layer(layer, mask.shape[1:]),
        *(of_expert(layer, w.shape[2:]) for w in (wg, wu, wd)),
        whole(cotangent.shape),
    ]
    outs = [
        (whole(big[0]), big),
        (whole(low[0]), low),
        table,
        (whole(big[0]), big),
        (whole(big[0]), big),
        table,
        *gradient_outs(features // 2, width),
    ]
    return run_experts(
        expert_both_kernel, "experts_both", ins, in_specs, outs, 16 << 30, 30 * MIB, 60
    )


def expert_backward(
    layer, places, g, x, gain, own, other, xi, share, gate_in, linear, wg, wu, wd, after
):
    length, features = x.shape
    width = wg.shape[3]
    big = ((length, features), F32)
    hidden = each_expert((length, width))
    ins = [places, g, x, gain, own, other, xi, share, gate_in, linear, wg, wu, wd, *after]
    in_specs = [SMEM, whole(x.shape), whole(x.shape)] + [
        of_layer(layer + 1, gain.shape[1:]),
        whole(x.shape),
        whole(x.shape),
        whole(x.shape),
        whole(share.shape),
        hidden,
        hidden,
        *(of_expert(layer, w.shape[2:]) for w in (wg, wu, wd)),
        *([ANYWHERE] * len(after)),
    ]
    outs = [
        (whole(big[0]), big),
        (whole((8, features)), ((8, features), F32)),
        (whole((length, features + LANES)), ((length, features + LANES), F32)),
        *gradient_outs(features // 2, width),
    ]
    return run_experts(
        expert_backward_kernel, "experts_backward", ins, in_specs, outs, 4 << 30, 30 * MIB, 60
    )


def attend_backward(mixture_grad, q, kk, vv, cosine, sine, allowed):
    length = mixture_grad.shape[0]
    lane = lane_of(length)
    low = lane < HEAD_SIZE
    scale = HEAD_SIZE**-0.5
    query_grads, key_grads, value_grads = [], [], []
    for pair in range(q.shape[1] // LANES // 2):
        key_sides, value_sides = [], []
        for side in range(2):
            head = 2 * pair + side
            columns = slice(head * LANES, (head + 1) * LANES)
            stacked = stacked_pair(q[:, columns], lane)
            scores = jnp.where(allowed, mm_nt(stacked, kk[head]) * scale, EXCLUDED)
            shifted = jnp.exp(scores - jnp.max(scores, axis=-1, keepdims=True))
            probs = shifted / jnp.sum(shifted, axis=-1, keepdims=True)
            mix_grad = stacked_pair(mixture_grad[:, columns], lane)
            prob_grad = mm_nt(mix_grad, vv[head])
            inner = jnp.sum(probs * prob_grad, axis=-1, keepdims=True)
            score_grad = (probs * (prob_grad - inner)).astype(BF16)
            query = mm(score_grad, kk[head])
            query = jnp.where(low, query[:length], query[length:]) * scale
            query = query * cosine - partner(query, lane) * sine
            query_grads.append(query.astype(BF16))
            key = mm_tn(score_grad, stacked) * scale
            key_sides.append(key + pltpu.roll(key, HEAD_SIZE, 1))
            value = mm_tn(probs.astype(BF16), mix_grad)
            value_sides.append(value + pltpu.roll(value, HEAD_SIZE, 1))
        key = jnp.where(low, key_sides[0], key_sides[1])
        key_grads.append((key * cosine - partner(key, lane) * sine).astype(BF16))
        value_grads.append(jnp.where(low, value_sides[0], value_sides[1]).astype(BF16))
    return tuple(
        jnp.concatenate(grads, axis=1) for grads in (query_grads, key_grads, value_grads)
    )


def attention_backward_kernel(
    count, full, orders, places, g, own, other, gate_own, gate_other, middle, xi, share, gain, router_rows,
    wo, mix, q, kk, vv, a, wq, wk, wv, cos, sin, seg_row, seg_column, x, late_gain, *rest,
):
    if full:
        q_other, kk_other, vv_other, weights = rest[:4]
        part_other = rest[-2]
        rest = rest[4:]
    g_out, part_out, keep, send = rest[count : count + 4]
    rows_scratch = rest[-1]
    where_to = block_places(orders, places)
    length = middle.shape[0]
    lane = lane_of(length)
    shares = share[...]
    gate_grad = gate_own[...] + gate_other[...]
    pick = shares * (gate_grad - jnp.sum(shares * gate_grad, axis=1, keepdims=True))
    input_grad = own[...] + other[...]
    xi_full = xi[...].astype(F32)
    rows_scratch[...] = jnp.zeros_like(rows_scratch)
    for expert in range(STREAMS):
        logit_grad = column_of(pick, lane, expert)
        input_grad = input_grad + logit_grad * router_rows[expert : expert + 1, :]
        rows_scratch[expert : expert + 1, :] = jnp.sum(
            xi_full * logit_grad, axis=0, keepdims=True
        )
    mid = middle[...]
    change, gain_row = norm_back(mid, row_factor(mid), gain[...].astype(F32), input_grad)
    rows_scratch[4:5, :] = gain_row
    rows_scratch[6:7, :] = late_gain[0:1, :]
    gradient = g[...].astype(F32) + change
    g_out[...] = gradient
    output_grad = gradient.astype(BF16)
    common = (cos[...], sin[...], allowed_pairs(seg_row[...], seg_column[...]))

    def half(output_weight, weights, *saved):
        mixture_grad = mm_nt(output_grad, output_weight[...]).astype(BF16)
        grads = attend_backward(mixture_grad, *saved, *common)
        part = sum(mm_nt(grad, weight[...]) for grad, weight in zip(grads, weights))
        return grads, part

    if full:
        wq_other, wk_other, wv_other, wo_other = halves_of(weights)
        part_other[...] = half(
            wo_other, (wq_other, wk_other, wv_other), q_other, kk_other, vv_other
        )[1]
    grads, attention_part = half(wo, (wq, wk, wv), q, kk, vv)
    part_out[...] = attention_part
    stream = x[...]
    rows_scratch[5:6, :] = jnp.sum(
        attention_part * stream * row_factor(stream), axis=0, keepdims=True
    )
    a_full = a[...]
    column = 0
    for total in (
        jnp.transpose(rows_scratch[...]),
        *(mm_tn(a_full, grad) for grad in grads),
        mm_tn(output_grad, mix[...]),
    ):
        store_blocks(keep, send, total, column, where_to)
        column += total.shape[1]


def attention_backward(
    layer, orders, places, g, own, other, gate_own, gate_other, saved_experts, weights, saved,
    tables, segment, late_gain, after, others=(),
):
    middle, xi, share = saved_experts
    gain, router_rows, wo, wq, wk, wv = weights
    x, a, q, kk, vv, mix = saved
    length, features = middle.shape
    columns = SMALL + wq.shape[2] + wk.shape[2] + wv.shape[2] + wo.shape[1]
    ins = [
        places, g, own, other, gate_own, gate_other, middle, xi, share, gain, router_rows,
        wo, mix, q, kk, vv, a, wq, wk, wv, *tables, *segment, x, late_gain,
    ]
    layered = {9, 10, 11, 17, 18, 19}
    in_specs = [SMEM]
    for at, array in enumerate(ins[1:], 1):
        if at in layered:
            in_specs.append(of_layer(layer, array.shape[1:]))
        elif at in (2, 3):
            in_specs.append(whole((length, features)))
        elif at in (4, 5):
            block = array.shape[1] // LANES - 1
            in_specs.append(
                pl.BlockSpec((length, LANES), lambda i, b=block: (0, b), pipeline_mode=ONCE)
            )
        else:
            in_specs.append(whole(array.shape))
    ins += [*others, *after]
    in_specs += [whole(array.shape) for array in others]
    in_specs += [ANYWHERE] * len(after)
    outs = [
        ((length, features), F32),
        ((length, features), F32),
        ((features // 2, columns), F32),
        ((features // 2, columns), F32),
    ]
    if others:
        outs.append(((length, features), F32))
    return pl.pallas_call(
        functools.partial(
            attention_backward_kernel, len(after), bool(others), orders
        ),
        grid=(1,),
        in_specs=in_specs,
        out_specs=[whole(shape) for shape, _ in outs],
        out_shape=[jax.ShapeDtypeStruct(*out) for out in outs],
        scratch_shapes=[pltpu.VMEM((LANES, features), F32)],
        compiler_params=params(60),
        cost_estimate=cost(16 << 30, 18 * MIB),
        name="attention_backward",
    )(*ins)


SWAP = ((0, 1), (1, 0))
RING = {"u": tuple((i, i ^ 1) for i in range(4)), "v": tuple((i, 3 - i) for i in range(4))}


def exchange(array):
    return lax.ppermute(array, "tensor", SWAP)


RING_AXES = ("dp_0", "dp_2", "dp_3")


def ring_pairs(orders, step):
    pairs = []
    for x in range(4):
        for z in range(4):
            for core in range(2):
                ring, kind = orders[core][step]
                at = x if ring == "x" else z
                to = at ^ 1 if kind == "u" else 3 - at
                there = (to, z) if ring == "x" else (x, to)
                pairs.append(((x * 4 + z) * 2 + core, (there[0] * 4 + there[1]) * 2 + core))
    return pairs


class Scatter:
    def __init__(self, keep, send, *orders):
        received = lax.ppermute(send, "dp_3", SWAP)
        width = keep.shape[1] // len(orders)
        self.orders = orders
        self.parts = [
            [array[:, at * width : (at + 1) * width] for array in (keep, received)]
            for at in range(len(orders))
        ]
        self.step = 0

    def halve(self):
        half = self.parts[0][0].shape[0] // 2
        self.kept = [first[:half] + second[:half] for first, second in self.parts]
        return [first[half:] + second[half:] for first, second in self.parts]

    def move(self, sends):
        moved = [
            lax.ppermute(send, RING_AXES, ring_pairs(orders, self.step))
            for send, orders in zip(sends, self.orders)
        ]
        self.parts = [list(pair) for pair in zip(self.kept, moved)]
        self.step += 1

    def received(self):
        return [second for _, second in self.parts]

    def hold(self, *after):
        for pair, second in zip(self.parts, behind(self.received(), *after)):
            pair[1] = second

    def advance(self, count=1):
        for _ in range(count):
            self.move(self.halve())

    def join(self, other):
        self.parts = [
            [jnp.concatenate(pair, axis=1) for pair in zip(*both)]
            for both in zip(self.parts, other.parts)
        ]

    def finish(self):
        sends = jnp.concatenate(self.halve(), axis=-1)
        return jnp.concatenate(self.kept, axis=-1) + lax.ppermute(sends, "dp_1", SWAP)


class Gather:
    def __init__(self, weights, layer):
        x, z, core = (lax.axis_index(name) for name in RING_AXES)
        piece = (x * 4 + z) * 2 + core

        def rows_of(weight):
            rows = weight.shape[1] // 32
            return lax.dynamic_slice_in_dim(weight[layer], piece * rows, rows, 0).astype(F32)

        *inputs, output = (rows_of(weight) for weight in weights)
        self.piece = jnp.concatenate([jnp.concatenate(inputs, axis=1), output], axis=0)
        orders = [*EXPERT_ORDERS, *(swapped(order) for order in EXPERT_ORDERS)]
        places = [ring_place(order, x, z) for order in orders]
        self.places = jnp.stack([*places, core]).astype(jnp.int32)

        self.crossed = exchange(self.piece)

    def begin(self, after, received):
        held, *_ = behind([self.crossed], after)
        for step in (3, 2):
            moved = lax.ppermute(held, RING_AXES, ring_pairs(EXPERT_ORDERS, step))
            held = jnp.concatenate([held, moved], axis=0)
        half = held.shape[1] // 2
        self.held = behind([held[:, :half], held[:, half:]], received)
        self.moved = self.moves(self.held, 1)

    def moves(self, held, step):
        return [
            lax.ppermute(half, RING_AXES, ring_pairs(EXPERT_ORDERS, at))
            for half, at in zip(held, (step, 1 - step))
        ]

    def finish(self, after):
        held = behind(self.held, after)
        held = [jnp.concatenate(pair, axis=0) for pair in zip(held, self.moved)]
        near = [*held, *self.moves(held, 0)]
        return [self.places, *near, *(lax.ppermute(half, "dp_3", SWAP) for half in near)]


def behind(arrays, *after):
    return pl.pallas_call(
        lambda *refs: None,
        in_specs=[ANYWHERE] * (len(arrays) + len(after)),
        out_specs=[ANYWHERE] * len(arrays),
        out_shape=[jax.ShapeDtypeStruct(array.shape, array.dtype) for array in arrays],
        input_output_aliases={at: at for at in range(len(arrays))},
        name="behind",
    )(*arrays, *after)


def rope_tables(length):
    half = HEAD_SIZE // 2
    frequency = np.float32(THETA) ** (-2.0 * np.arange(half, dtype=np.float32) / HEAD_SIZE)
    angles = np.arange(length, dtype=np.float32)[:, None] * frequency[None].astype(np.float32)
    angles = angles.astype(np.float32)
    cosine = np.tile(np.cos(angles), (1, LANES // half)).astype(np.float32)
    sine = np.sin(angles)
    sine = np.tile(np.concatenate([-sine, sine], axis=1), (1, LANES // HEAD_SIZE))
    return jnp.asarray(cosine), jnp.asarray(sine.astype(np.float32))


def shards(
    tokens, segments, routes, norm_attention, query_weight, key_matrix, value_matrix,
    output_weight, norm_experts, router_weight, gate_weight, up_weight, down_weight, cotangent,
):
    length, features = tokens.shape
    experts = gate_weight.shape[1]
    hidden = gate_weight.shape[3]
    tables = rope_tables(length)
    segment = (segments.reshape(1, length), segments.reshape(length, 1))
    gain_attention = norm_attention[:, None, :]
    gain_experts = norm_experts[:, None, :]
    router = jnp.pad(router_weight, ((0, 0), (0, 0), (0, LANES - experts)))
    router_rows = jnp.pad(
        jnp.swapaxes(router_weight, 1, 2).astype(F32), ((0, 0), (0, 8 - experts), (0, 0))
    )
    mask = jnp.any(
        routes[..., None] == jnp.arange(LANES, dtype=jnp.int32), axis=2
    ).astype(F32)
    x_at, y_at, z_at = (lax.axis_index(name) for name in DP[:3])
    core = lax.axis_index("dp_3")

    def places_in(orders):
        found = []
        for which in (orders, [crossed(order) for order in orders]):
            one, two = (place(order, x_at, y_at, z_at) for order in which)
            found += [jnp.where(core == 0, one, two), jnp.where(core == 0, two, one)]
        return jnp.stack([*found, core]).astype(jnp.int32)

    expert_places = places_in(EXPERT_ORDERS)
    late_orders = tuple(swapped(order) for order in ATTENTION_ORDERS)

    attention_weights = (gain_attention, query_weight, key_matrix, value_matrix, output_weight)
    expert_weights = (gate_weight, up_weight, down_weight)
    back_weights = (
        gain_experts, router_rows, output_weight, query_weight, key_matrix, value_matrix,
    )

    others = Gather(attention_weights[1:], 1)
    x1, *saved1, part = attention_forward(0, [tokens], attention_weights, tables, segment)
    other = exchange(part)
    others.begin(part, other)
    middle1, xi1, share1, gate1, linear1, part = expert_forward(
        0, x1, part, other, gain_experts, router, mask, *expert_weights
    )
    x2, *saved2, part, q_other, kk_other, vv_other, part_other, weights_other = attention_forward(
        1, [middle1, part, exchange(part)], attention_weights, tables, segment,
        others.finish(part),
    )
    middle2, xi2, share2, last, back, gate_grad, keep, send = expert_both(
        1, expert_places, x2, part, part_other, gain_experts, router, mask, *expert_weights,
        cotangent,
    )
    both_orders = (EXPERT_ORDERS, tuple(crossed(order) for order in EXPERT_ORDERS))
    sum_e2 = Scatter(keep, send, *both_orders)
    other, gate_other = exchange(back), exchange(gate_grad)
    *sends, last = behind([*sum_e2.halve(), last], other)
    sum_e2.move(sends)
    last_other = exchange(last)
    no_gain = jnp.zeros((8, features), F32)
    g2, part, keep, send, part_other = attention_backward(
        1, late_orders, places_in(late_orders), cotangent, back, other, gate_grad, gate_other,
        (middle2, xi2, share2), back_weights, (x2, *saved2), tables, segment, no_gain, sends,
        (q_other, kk_other, vv_other, weights_other),
    )
    sum_a2 = Scatter(keep, send, late_orders)
    sends = sum_e2.halve()
    g1, late_gain, back, keep, send = expert_backward(
        0, expert_places, g2, x2, gain_attention, part, part_other, xi1, share1, gate1,
        linear1, *expert_weights, [*sends, last_other],
    )
    sum_e2.move(sends)
    sum_e1 = Scatter(keep, send, *both_orders)
    other = exchange(back)
    sends_a, sends_e = sum_a2.halve(), sum_e1.halve()
    sum_a2.move(sends_a)
    sum_e1.move(sends_e)
    sends = sends_a + sends_e + sum_e2.received()
    g0, part, keep, send = attention_backward(
        0, late_orders, places_in(late_orders), g1, back, other, back, other,
        (middle1, xi1, share1), back_weights, (x1, *saved1), tables, segment, late_gain,
        sends,
    )
    (send,) = behind([send], *sum_a2.received(), *sum_e1.received())
    sum_a1 = Scatter(keep, send, late_orders)
    sum_e1.advance()
    sum_a1.advance()
    sum_a2.advance()
    (other,) = behind([exchange(part)], *sum_a1.received())
    sum_e1.hold(*sum_a1.received())
    sum_a1.advance()
    sums = ((sum_a1, sum_a2), (sum_e1, sum_e2))
    for one, two in sums:
        one.join(two)
        one.advance(2)
    gain = norm_attention[0].astype(F32)
    change, _ = norm_back(x1, row_factor(x1), gain, part + other)
    gradient = g0 + change
    output = (middle2 + (last + last_other)).astype(BF16)
    blocks = [one.finish() for one, _ in sums]

    attention_sums, expert_sums = blocks
    rows = attention_sums.shape[0]
    layers = query_weight.shape[0]
    attention_sums = jnp.swapaxes(attention_sums.reshape(rows, layers, -1), 0, 1)
    bounds = np.cumsum(
        [0, SMALL, query_weight.shape[2], key_matrix.shape[2], value_matrix.shape[2],
         output_weight.shape[1]]
    )
    attention_sums = [attention_sums[..., a:b] for a, b in zip(bounds[:-1], bounds[1:])]
    expert_sums = expert_sums.reshape(rows, 2, layers, experts // 2, 3, hidden)
    expert_sums = [
        expert_sums[..., kind, :].transpose(2, 1, 3, 0, 4).reshape(layers, experts, rows, hidden)
        for kind in range(3)
    ]
    small = attention_sums[0]
    attention_gain = small[:, :, 5]
    attention_gain = attention_gain + exchange(attention_gain)
    return (
        output,
        gradient,
        attention_gain,
        *attention_sums[1:4],
        jnp.swapaxes(attention_sums[4], 1, 2),
        small[:, :, 4],
        small[:, :, :experts],
        expert_sums[0],
        expert_sums[1],
        jnp.swapaxes(expert_sums[2], 2, 3),
    )


def solution(mesh):
    torus = Mesh(
        mesh.devices.reshape(*DP_SIZES, mesh.shape["tensor"]), (*DP, "tensor")
    )
    rows, copied, last = P(DP, None), P(), P(None, None, "tensor")
    in_specs = (
        rows, rows, P(None, DP, None), copied, last, last, last, P(None, "tensor", None),
        copied, copied, P(None, None, None, "tensor"), P(None, None, None, "tensor"),
        P(None, None, "tensor", None), rows,
    )
    out_specs = (
        rows, rows, P(None, DP), P(None, DP, "tensor"), P(None, DP, "tensor"),
        P(None, DP, "tensor"), P(None, "tensor", DP), P(None, DP), P(None, DP, None),
        P(None, None, DP, "tensor"), P(None, None, DP, "tensor"), P(None, None, "tensor", DP),
    )
    return jax.shard_map(
        shards, mesh=torus, in_specs=in_specs, out_specs=out_specs, check_vma=False
    )
```

```python
import functools

import jax
import jax.numpy as jnp
import numpy as np
from jax import lax
from jax.experimental import pallas as pl
from jax.experimental.pallas import tpu as pltpu
from jax.sharding import Mesh
from jax.sharding import PartitionSpec as P

HEAD_SIZE = 64
LANES = 128
STREAMS = 4
SMALL = 128
DP = ("dp_0", "dp_1", "dp_2", "dp_3")
DP_SIZES = (4, 2, 4, 2)
EPSILON = 1e-06
THETA = 10000.0
EXCLUDED = -1e30
F32 = jnp.float32
BF16 = jnp.bfloat16
MIB = 1024 * 1024

EXPERT_ORDERS = (
    (("x", "u"), ("z", "u"), ("z", "v"), ("x", "v")),
    (("z", "v"), ("x", "v"), ("x", "u"), ("z", "u")),
)
ATTENTION_ORDERS = (
    (("z", "v"), ("x", "v"), ("x", "u"), ("z", "u")),
    (("x", "u"), ("z", "u"), ("z", "v"), ("x", "v")),
)


def swapped(order):
    return (order[1], order[0], *order[2:])


def crossed(order):
    return (order[1], order[0], order[3], order[2])


def pair_bit(index, kind):
    high = index // 2
    if kind == "v":
        return high
    return high ^ (index % 2)


def ring_place(order, x, z):
    at = 0
    for ring, kind in order:
        at = at * 2 + pair_bit(x if ring == "x" else z, kind)
    return at


def place(order, x, yh, z):
    return ring_place(order, x, z) * 2 + yh


def mm(a, b):
    return lax.dot_general(a, b, (((1,), (0,)), ((), ())), preferred_element_type=F32)


def mm_nt(a, b):
    return lax.dot_general(a, b, (((1,), (1,)), ((), ())), preferred_element_type=F32)


def mm_tn(a, b):
    return lax.dot_general(a, b, (((0,), (0,)), ((), ())), preferred_element_type=F32)


def row_factor(stream):
    return lax.rsqrt(jnp.mean(stream * stream, axis=-1, keepdims=True) + EPSILON)


def norm_back(stream, factor, gain, gradient):
    weighted = gradient * gain
    inner = jnp.sum(weighted * stream, axis=-1, keepdims=True) * (1.0 / stream.shape[-1])
    change = factor * weighted - stream * (factor * factor * factor) * inner
    return change, jnp.sum(gradient * stream * factor, axis=0, keepdims=True)


def lane_of(rows):
    return lax.broadcasted_iota(jnp.int32, (rows, LANES), 1)


def partner(block, lane):
    back = pltpu.roll(block, LANES - HEAD_SIZE // 2, 1)
    ahead = pltpu.roll(block, HEAD_SIZE // 2, 1)
    return jnp.where(lane % HEAD_SIZE < HEAD_SIZE // 2, back, ahead)


def both_heads(block, lane):
    rolled = pltpu.roll(block, HEAD_SIZE, 1)
    low = lane < HEAD_SIZE
    return jnp.where(low, block, rolled), jnp.where(low, rolled, block)


def stacked_pair(block, lane):
    zero = jnp.zeros_like(block)
    low = lane < HEAD_SIZE
    return jnp.concatenate(
        [jnp.where(low, block, zero), jnp.where(low, zero, block)], axis=0
    )


def allowed_pairs(seg_row, seg_column):
    length = seg_column.shape[0]
    rows = lax.broadcasted_iota(jnp.int32, (length, length), 0)
    columns = lax.broadcasted_iota(jnp.int32, (length, length), 1)
    allowed = (columns <= rows) & (seg_column == seg_row)
    bias = jnp.where(allowed, 0.0, 1.0)
    return jnp.concatenate([bias, bias], axis=0) < 0.5


def block_places(orders, places, later=False):
    core = places[4]
    found = []
    for block in range(32):
        x, yh, z = block // 8, (block // 4) % 2, block % 4
        one, two = (
            jnp.where(later, place(crossed(order), x, yh, z), place(order, x, yh, z))
            for order in orders
        )
        own = jnp.where(later, places[2], places[0])
        far = jnp.where(later, places[3], places[1])
        found.append((jnp.where(core == 0, one, two) ^ own, jnp.where(core == 0, two, one) ^ far))
    return core, found


def store_blocks(keep_ref, send_ref, value, column, where_to):
    core, found = where_to
    rows = value.shape[0] // 64
    columns = slice(column, column + value.shape[1])
    for block, (kept, sent) in enumerate(found):
        first = value[2 * block * rows : (2 * block + 1) * rows]
        second = value[(2 * block + 1) * rows : (2 * block + 2) * rows]
        keep_ref[pl.ds(pl.multiple_of(kept * rows, rows), rows), columns] = jnp.where(
            core == 0, first, second
        )
        send_ref[pl.ds(pl.multiple_of(sent * rows, rows), rows), columns] = jnp.where(
            core == 0, second, first
        )


def attend(a, wq, wk, wv, q_out, kk_out, vv_out, mix_out, cosine, sine, allowed):
    length = a.shape[0]
    lane = lane_of(length)
    q = mm(a, wq)
    k = mm(a, wk)
    v = mm(a, wv)
    scale = HEAD_SIZE**-0.5
    for pair in range(k.shape[1] // LANES):
        at = slice(pair * LANES, (pair + 1) * LANES)
        k_block = k[:, at] * cosine + partner(k[:, at], lane) * sine
        k_twice = both_heads(k_block, lane)
        v_twice = both_heads(v[:, at], lane)
        for side in range(2):
            head = 2 * pair + side
            columns = slice(head * LANES, (head + 1) * LANES)
            kk = k_twice[side].astype(BF16)
            vv = v_twice[side].astype(BF16)
            kk_out[head] = kk
            vv_out[head] = vv
            q_block = q[:, columns]
            q_block = (q_block * cosine + partner(q_block, lane) * sine).astype(BF16)
            q_out[:, columns] = q_block
            scores = mm_nt(stacked_pair(q_block, lane), kk) * scale
            scores = jnp.where(allowed, scores, EXCLUDED)
            shifted = jnp.exp(scores - jnp.max(scores, axis=-1, keepdims=True))
            probs = (shifted / jnp.sum(shifted, axis=-1, keepdims=True)).astype(BF16)
            mixed = mm(probs, vv)
            mix_out[:, columns] = jnp.where(
                lane < HEAD_SIZE, mixed[:length], mixed[length:]
            ).astype(BF16)


def halves_of(weights):
    depth = 2 * weights.shape[0] // 3
    quarter = depth // 4
    return (
        weights.at[:depth, : 2 * quarter],
        weights.at[:depth, 2 * quarter : 3 * quarter],
        weights.at[:depth, 3 * quarter :],
        weights.at[depth:, :],
    )


def unpack_gathered(places, gathered, weights):
    core = places[4]
    rows = gathered[0].shape[0] // 8
    width = gathered[0].shape[1]
    top, low = 2 * rows // 3, rows // 3
    for piece in range(32):
        x, z, side = piece // 8, (piece // 2) % 4, piece % 2
        for part in range(2):
            order = EXPERT_ORDERS[side] if part == 0 else swapped(EXPERT_ORDERS[side])
            at = ring_place(order, x, z) ^ places[2 * part + side]
            rows_at = pl.ds(pl.multiple_of((at & 7) * rows, rows), rows)
            columns = slice(part * width, (part + 1) * width)
            first, second, far_first, far_second = (
                gathered[2 * pair + part][rows_at, :] for pair in range(4)
            )
            near, far = jnp.where(at < 8, first, second), jnp.where(at < 8, far_first, far_second)
            value = jnp.where(core == side, near, far).astype(BF16)
            weights[piece * top : (piece + 1) * top, columns] = value[:top]
            start = 32 * top + piece * low
            weights[start : start + low, columns] = value[top:]


def attention_forward_kernel(count, full, *refs):
    parts = refs[:count]
    (gain, wq, wk, wv, wo, cos, sin, seg_row, seg_column) = refs[count : count + 9]
    refs = refs[count + 9 :]
    if full:
        places, gathered = refs[0], refs[1:9]
        refs = refs[9:]
    (x_out, a_out, q_out, kk_out, vv_out, mix_out, part_out) = refs[:7]
    x = parts[0][...].astype(F32)
    if count == 3:
        x = x + (parts[1][...] + parts[2][...])
    x_out[...] = x
    a = (x * row_factor(x) * gain[...].astype(F32)).astype(BF16)
    a_out[...] = a
    common = (cos[...], sin[...], allowed_pairs(seg_row[...], seg_column[...]))
    attend(a, wq[...], wk[...], wv[...], q_out, kk_out, vv_out, mix_out, *common)
    part_out[...] = mm(mix_out[...], wo[...])
    if full:
        q_other, kk_other, vv_other, part_other, weights, mix_other = refs[7:]
        unpack_gathered(places, gathered, weights)
        wq, wk, wv, wo = halves_of(weights)
        attend(a, wq[...], wk[...], wv[...], q_other, kk_other, vv_other, mix_other, *common)
        part_other[...] = mm(mix_other[...], wo[...])


ONCE = pl.Buffered(1)
SMEM = pl.BlockSpec(memory_space=pltpu.SMEM)
ANYWHERE = pl.BlockSpec(memory_space=pl.ANY)


def whole(shape):
    return pl.BlockSpec(shape, lambda i: (0,) * len(shape), pipeline_mode=ONCE)


def of_layer(layer, shape):
    return pl.BlockSpec(
        (None, *shape), lambda i: (layer,) + (0,) * len(shape), pipeline_mode=ONCE
    )


def params(mib):
    return pltpu.CompilerParams(
        vmem_limit_bytes=mib * MIB, dimension_semantics=("arbitrary",)
    )


def cost(flops, nbytes):
    return pl.CostEstimate(flops=flops, bytes_accessed=nbytes, transcendentals=0)


def attention_forward(layer, parts, weights, tables, segment, gathered=()):
    gain, wq, wk, wv, wo = weights
    length, features = parts[0].shape
    q_width, k_width = wq.shape[2], wk.shape[2]
    heads = 2 * k_width // LANES
    ins = [*parts, gain, wq, wk, wv, wo, *tables, *segment]
    in_specs = [whole(part.shape) for part in parts]
    in_specs += [of_layer(layer, w.shape[1:]) for w in (gain, wq, wk, wv, wo)]
    in_specs += [whole(t.shape) for t in (*tables, *segment)]
    outs = [
        ((length, features), F32),
        ((length, features), BF16),
        ((length, q_width), BF16),
        ((heads, length, LANES), BF16),
        ((heads, length, LANES), BF16),
        ((length, q_width), BF16),
        ((length, features), F32),
    ]
    scratch = []
    if gathered:
        ins += gathered
        in_specs += [SMEM, *(whole(array.shape) for array in gathered[1:])]
        outs += [outs[2], outs[3], outs[4], outs[6], ((4 * gathered[1].shape[0], features), BF16)]
        scratch = [pltpu.VMEM((length, q_width), BF16)]
    return pl.pallas_call(
        functools.partial(attention_forward_kernel, len(parts), bool(gathered)),
        grid=(1,),
        scratch_shapes=scratch,
        in_specs=in_specs,
        out_specs=[whole(shape) for shape, _ in outs],
        out_shape=[jax.ShapeDtypeStruct(*out) for out in outs],
        compiler_params=params(60),
        cost_estimate=cost(6 << 30, 8 * MIB),
        name="attention_forward",
    )(*ins)


def column_of(table, lane, index):
    return jnp.sum(jnp.where(lane == index, table, 0.0), axis=1, keepdims=True)


def expert_prologue(x, own, other, gain, router, mask, middle_out, xi_out, share_out):
    middle = x[...] + (own[...] + other[...])
    middle_out[...] = middle
    xi = (middle * row_factor(middle) * gain[...].astype(F32)).astype(BF16)
    xi_out[...] = xi
    logits = mm(xi, router[...])
    chosen = mask[...] > 0.5
    logits = jnp.where(chosen, logits, EXCLUDED)
    shifted = jnp.exp(logits - jnp.max(logits, axis=-1, keepdims=True))
    shifted = jnp.where(chosen, shifted, 0.0)
    share_out[...] = shifted / jnp.sum(shifted, axis=-1, keepdims=True)


def expert_step(gate_in, linear, wd, share):
    squashed = 1.0 / (1.0 + jnp.exp(-gate_in))
    silu = gate_in * squashed
    activation = (silu * linear).astype(BF16)
    return squashed, silu, activation, mm(activation, wd)


def expert_backward_step(places, g, xi, share, gate_in, linear, wg, wu, wd, keep, send):
    where_to = block_places(EXPERT_ORDERS, places, pl.program_id(0) >= STREAMS // 2)
    squashed, silu, activation, expert_out = expert_step(gate_in, linear, wd, share)
    gate_grad = jnp.sum(g * expert_out, axis=1, keepdims=True)
    expert_grad = (share * g).astype(BF16)
    activation_grad = mm_nt(expert_grad, wd)
    gate_in_grad = (
        activation_grad * linear * squashed * (1.0 + gate_in * (1.0 - squashed))
    ).astype(BF16)
    linear_grad = (activation_grad * silu).astype(BF16)
    width = activation.shape[1]
    store_blocks(keep, send, mm_tn(xi, gate_in_grad), 0, where_to)
    store_blocks(keep, send, mm_tn(xi, linear_grad), width, where_to)
    store_blocks(keep, send, mm_tn(expert_grad, activation), 2 * width, where_to)
    return gate_grad, mm_nt(gate_in_grad, wg) + mm_nt(linear_grad, wu), expert_out


def expert_forward_kernel(
    x, own, other, gain, router, mask, wg, wu, wd,
    middle_out, xi_out, share_out, gate_out, linear_out, part_out,
):
    expert = pl.program_id(0)

    @pl.when(expert == 0)
    def _():
        expert_prologue(x, own, other, gain, router, mask, middle_out, xi_out, share_out)
        part_out[...] = jnp.zeros_like(part_out)

    share = column_of(share_out[...], lane_of(share_out.shape[0]), expert)
    xi = xi_out[...]
    gate_in = mm(xi, wg[...])
    linear = mm(xi, wu[...])
    gate_out[...] = gate_in
    linear_out[...] = linear
    part_out[...] += share * expert_step(gate_in, linear, wd[...], share)[3]


def expert_both_kernel(
    places, x, own, other, gain, router, mask, wg, wu, wd, cotangent,
    middle_out, xi_out, share_out, part_out, back_out, gate_grad_out, keep, send,
):
    expert = pl.program_id(0)
    lane = lane_of(share_out.shape[0])

    @pl.when(expert == 0)
    def _():
        expert_prologue(x, own, other, gain, router, mask, middle_out, xi_out, share_out)
        part_out[...] = jnp.zeros_like(part_out)
        back_out[...] = jnp.zeros_like(back_out)
        gate_grad_out[...] = jnp.zeros_like(gate_grad_out)

    share = column_of(share_out[...], lane, expert)
    xi = xi_out[...]
    gate_in = mm(xi, wg[...])
    linear = mm(xi, wu[...])
    gate_grad, back, expert_out = expert_backward_step(
        places, cotangent[...].astype(F32), xi, share, gate_in, linear, wg[...], wu[...],
        wd[...], keep, send,
    )
    part_out[...] += share * expert_out
    back_out[...] += back
    gate_grad_out[...] += jnp.where(lane == expert, gate_grad, 0.0)


def expert_backward_kernel(
    places, g_in, x, gain, own, other, xi_ref, share_ref, gate_ref, linear_ref, wg, wu, wd,
    *rest,
):
    g_out, gain_out, back_out, keep, send = rest[-5:]
    expert = pl.program_id(0)
    lane = lane_of(share_ref.shape[0])

    @pl.when(expert == 0)
    def _():
        stream = x[...]
        change, gain_row = norm_back(
            stream, row_factor(stream), gain[...].astype(F32), own[...] + other[...]
        )
        g_out[...] = g_in[...] + change
        gain_out[...] = jnp.broadcast_to(gain_row, gain_out.shape)
        back_out[...] = jnp.zeros_like(back_out)

    share = column_of(share_ref[...], lane, expert)
    gate_grad, back, _ = expert_backward_step(
        places, g_out[...], xi_ref[...], share, gate_ref[...], linear_ref[...], wg[...],
        wu[...], wd[...], keep, send,
    )
    back_out[:, : back.shape[1]] += back
    back_out[:, back.shape[1] :] += jnp.where(lane == expert, gate_grad, 0.0)


def of_expert(layer, shape):
    return pl.BlockSpec((None, None, *shape), lambda e: (layer, e, 0, 0))


def each_expert(shape):
    return pl.BlockSpec((None, *shape), lambda e: (e, 0, 0))


def gradient_outs(rows, width):
    spec = pl.BlockSpec((rows, 3 * width), lambda e: (0, e))
    shape = ((rows, 3 * width * STREAMS), F32)
    return [(spec, shape)] * 2


def run_experts(kernel, name, ins, in_specs, outs, flops, nbytes, mib):
    return pl.pallas_call(
        kernel,
        grid=(STREAMS,),
        in_specs=in_specs,
        out_specs=[spec for spec, _ in outs],
        out_shape=[jax.ShapeDtypeStruct(*out) for _, out in outs],
        compiler_params=params(mib),
        cost_estimate=cost(flops, nbytes),
        name=name,
    )(*ins)


def expert_forward(layer, x, own, other, gain, router, mask, wg, wu, wd):
    length, features = x.shape
    width = wg.shape[3]
    big, low = ((length, features), F32), ((length, features), BF16)
    hidden = (each_expert((length, width)), ((STREAMS, length, width), F32))
    ins = [x, own, other, gain, router, mask, wg, wu, wd]
    in_specs = [whole(x.shape)] * 3 + [
        of_layer(layer, gain.shape[1:]),
        of_layer(layer, router.shape[1:]),
        of_layer(layer, mask.shape[1:]),
        *(of_expert(layer, w.shape[2:]) for w in (wg, wu, wd)),
    ]
    outs = [
        (whole(big[0]), big),
        (whole(low[0]), low),
        (whole((length, LANES)), ((length, LANES), F32)),
        hidden,
        hidden,
        (whole(big[0]), big),
    ]
    return run_experts(
        expert_forward_kernel, "experts_forward", ins, in_specs, outs, 8 << 30, 12 * MIB, 60
    )


def expert_both(layer, places, x, own, other, gain, router, mask, wg, wu, wd, cotangent):
    length, features = x.shape
    width = wg.shape[3]
    big, low = ((length, features), F32), ((length, features), BF16)
    table = (whole((length, LANES)), ((length, LANES), F32))
    ins = [places, x, own, other, gain, router, mask, wg, wu, wd, cotangent]
    in_specs = [SMEM] + [whole(x.shape)] * 3 + [
        of_layer(layer, gain.shape[1:]),
        of_layer(layer, router.shape[1:]),
        of_layer(layer, mask.shape[1:]),
        *(of_expert(layer, w.shape[2:]) for w in (wg, wu, wd)),
        whole(cotangent.shape),
    ]
    outs = [
        (whole(big[0]), big),
        (whole(low[0]), low),
        table,
        (whole(big[0]), big),
        (whole(big[0]), big),
        table,
        *gradient_outs(features // 2, width),
    ]
    return run_experts(
        expert_both_kernel, "experts_both", ins, in_specs, outs, 16 << 30, 30 * MIB, 60
    )


def expert_backward(
    layer, places, g, x, gain, own, other, xi, share, gate_in, linear, wg, wu, wd, after
):
    length, features = x.shape
    width = wg.shape[3]
    big = ((length, features), F32)
    hidden = each_expert((length, width))
    ins = [places, g, x, gain, own, other, xi, share, gate_in, linear, wg, wu, wd, *after]
    in_specs = [SMEM, whole(x.shape), whole(x.shape)] + [
        of_layer(layer + 1, gain.shape[1:]),
        whole(x.shape),
        whole(x.shape),
        whole(x.shape),
        whole(share.shape),
        hidden,
        hidden,
        *(of_expert(layer, w.shape[2:]) for w in (wg, wu, wd)),
        *([ANYWHERE] * len(after)),
    ]
    outs = [
        (whole(big[0]), big),
        (whole((8, features)), ((8, features), F32)),
        (whole((length, features + LANES)), ((length, features + LANES), F32)),
        *gradient_outs(features // 2, width),
    ]
    return run_experts(
        expert_backward_kernel, "experts_backward", ins, in_specs, outs, 4 << 30, 30 * MIB, 60
    )


def attend_backward(mixture_grad, q, kk, vv, cosine, sine, allowed):
    length = mixture_grad.shape[0]
    lane = lane_of(length)
    low = lane < HEAD_SIZE
    scale = HEAD_SIZE**-0.5
    query_grads, key_grads, value_grads = [], [], []
    for pair in range(q.shape[1] // LANES // 2):
        key_sides, value_sides = [], []
        for side in range(2):
            head = 2 * pair + side
            columns = slice(head * LANES, (head + 1) * LANES)
            stacked = stacked_pair(q[:, columns], lane)
            scores = jnp.where(allowed, mm_nt(stacked, kk[head]) * scale, EXCLUDED)
            shifted = jnp.exp(scores - jnp.max(scores, axis=-1, keepdims=True))
            probs = shifted / jnp.sum(shifted, axis=-1, keepdims=True)
            mix_grad = stacked_pair(mixture_grad[:, columns], lane)
            prob_grad = mm_nt(mix_grad, vv[head])
            inner = jnp.sum(probs * prob_grad, axis=-1, keepdims=True)
            score_grad = (probs * (prob_grad - inner)).astype(BF16)
            query = mm(score_grad, kk[head])
            query = jnp.where(low, query[:length], query[length:]) * scale
            query = query * cosine - partner(query, lane) * sine
            query_grads.append(query.astype(BF16))
            key = mm_tn(score_grad, stacked) * scale
            key_sides.append(key + pltpu.roll(key, HEAD_SIZE, 1))
            value = mm_tn(probs.astype(BF16), mix_grad)
            value_sides.append(value + pltpu.roll(value, HEAD_SIZE, 1))
        key = jnp.where(low, key_sides[0], key_sides[1])
        key_grads.append((key * cosine - partner(key, lane) * sine).astype(BF16))
        value_grads.append(jnp.where(low, value_sides[0], value_sides[1]).astype(BF16))
    return tuple(
        jnp.concatenate(grads, axis=1) for grads in (query_grads, key_grads, value_grads)
    )


def attention_backward_kernel(
    count, full, orders, places, g, own, other, gate_own, gate_other, middle, xi, share, gain, router_rows,
    wo, mix, q, kk, vv, a, wq, wk, wv, cos, sin, seg_row, seg_column, x, late_gain, *rest,
):
    if full:
        q_other, kk_other, vv_other, weights = rest[:4]
        part_other = rest[-2]
        rest = rest[4:]
    g_out, part_out, keep, send = rest[count : count + 4]
    rows_scratch = rest[-1]
    where_to = block_places(orders, places)
    length = middle.shape[0]
    lane = lane_of(length)
    shares = share[...]
    gate_grad = gate_own[...] + gate_other[...]
    pick = shares * (gate_grad - jnp.sum(shares * gate_grad, axis=1, keepdims=True))
    input_grad = own[...] + other[...]
    xi_full = xi[...].astype(F32)
    rows_scratch[...] = jnp.zeros_like(rows_scratch)
    for expert in range(STREAMS):
        logit_grad = column_of(pick, lane, expert)
        input_grad = input_grad + logit_grad * router_rows[expert : expert + 1, :]
        rows_scratch[expert : expert + 1, :] = jnp.sum(
            xi_full * logit_grad, axis=0, keepdims=True
        )
    mid = middle[...]
    change, gain_row = norm_back(mid, row_factor(mid), gain[...].astype(F32), input_grad)
    rows_scratch[4:5, :] = gain_row
    rows_scratch[6:7, :] = late_gain[0:1, :]
    gradient = g[...].astype(F32) + change
    g_out[...] = gradient
    output_grad = gradient.astype(BF16)
    common = (cos[...], sin[...], allowed_pairs(seg_row[...], seg_column[...]))

    def half(output_weight, weights, *saved):
        mixture_grad = mm_nt(output_grad, output_weight[...]).astype(BF16)
        grads = attend_backward(mixture_grad, *saved, *common)
        part = sum(mm_nt(grad, weight[...]) for grad, weight in zip(grads, weights))
        return grads, part

    if full:
        wq_other, wk_other, wv_other, wo_other = halves_of(weights)
        part_other[...] = half(
            wo_other, (wq_other, wk_other, wv_other), q_other, kk_other, vv_other
        )[1]
    grads, attention_part = half(wo, (wq, wk, wv), q, kk, vv)
    part_out[...] = attention_part
    stream = x[...]
    rows_scratch[5:6, :] = jnp.sum(
        attention_part * stream * row_factor(stream), axis=0, keepdims=True
    )
    a_full = a[...]
    column = 0
    for total in (
        jnp.transpose(rows_scratch[...]),
        *(mm_tn(a_full, grad) for grad in grads),
        mm_tn(output_grad, mix[...]),
    ):
        store_blocks(keep, send, total, column, where_to)
        column += total.shape[1]


def attention_backward(
    layer, orders, places, g, own, other, gate_own, gate_other, saved_experts, weights, saved,
    tables, segment, late_gain, after, others=(),
):
    middle, xi, share = saved_experts
    gain, router_rows, wo, wq, wk, wv = weights
    x, a, q, kk, vv, mix = saved
    length, features = middle.shape
    columns = SMALL + wq.shape[2] + wk.shape[2] + wv.shape[2] + wo.shape[1]
    ins = [
        places, g, own, other, gate_own, gate_other, middle, xi, share, gain, router_rows,
        wo, mix, q, kk, vv, a, wq, wk, wv, *tables, *segment, x, late_gain,
    ]
    layered = {9, 10, 11, 17, 18, 19}
    in_specs = [SMEM]
    for at, array in enumerate(ins[1:], 1):
        if at in layered:
            in_specs.append(of_layer(layer, array.shape[1:]))
        elif at in (2, 3):
            in_specs.append(whole((length, features)))
        elif at in (4, 5):
            block = array.shape[1] // LANES - 1
            in_specs.append(
                pl.BlockSpec((length, LANES), lambda i, b=block: (0, b), pipeline_mode=ONCE)
            )
        else:
            in_specs.append(whole(array.shape))
    ins += [*others, *after]
    in_specs += [whole(array.shape) for array in others]
    in_specs += [ANYWHERE] * len(after)
    outs = [
        ((length, features), F32),
        ((length, features), F32),
        ((features // 2, columns), F32),
        ((features // 2, columns), F32),
    ]
    if others:
        outs.append(((length, features), F32))
    return pl.pallas_call(
        functools.partial(
            attention_backward_kernel, len(after), bool(others), orders
        ),
        grid=(1,),
        in_specs=in_specs,
        out_specs=[whole(shape) for shape, _ in outs],
        out_shape=[jax.ShapeDtypeStruct(*out) for out in outs],
        scratch_shapes=[pltpu.VMEM((LANES, features), F32)],
        compiler_params=params(60),
        cost_estimate=cost(16 << 30, 18 * MIB),
        name="attention_backward",
    )(*ins)


SWAP = ((0, 1), (1, 0))
RING = {"u": tuple((i, i ^ 1) for i in range(4)), "v": tuple((i, 3 - i) for i in range(4))}


def exchange(array):
    return lax.ppermute(array, "tensor", SWAP)


RING_AXES = ("dp_0", "dp_2", "dp_3")


def ring_pairs(orders, step):
    pairs = []
    for x in range(4):
        for z in range(4):
            for core in range(2):
                ring, kind = orders[core][step]
                at = x if ring == "x" else z
                to = at ^ 1 if kind == "u" else 3 - at
                there = (to, z) if ring == "x" else (x, to)
                pairs.append(((x * 4 + z) * 2 + core, (there[0] * 4 + there[1]) * 2 + core))
    return pairs


class Scatter:
    def __init__(self, keep, send, *orders):
        received = lax.ppermute(send, "dp_3", SWAP)
        width = keep.shape[1] // len(orders)
        self.orders = orders
        self.parts = [
            [array[:, at * width : (at + 1) * width] for array in (keep, received)]
            for at in range(len(orders))
        ]
        self.step = 0

    def halve(self):
        half = self.parts[0][0].shape[0] // 2
        self.kept = [first[:half] + second[:half] for first, second in self.parts]
        return [first[half:] + second[half:] for first, second in self.parts]

    def move(self, sends):
        moved = [
            lax.ppermute(send, RING_AXES, ring_pairs(orders, self.step))
            for send, orders in zip(sends, self.orders)
        ]
        self.parts = [list(pair) for pair in zip(self.kept, moved)]
        self.step += 1

    def received(self):
        return [second for _, second in self.parts]

    def hold(self, *after):
        for pair, second in zip(self.parts, behind(self.received(), *after)):
            pair[1] = second

    def advance(self, count=1):
        for _ in range(count):
            self.move(self.halve())

    def join(self, other):
        self.parts = [
            [jnp.concatenate(pair, axis=1) for pair in zip(*both)]
            for both in zip(self.parts, other.parts)
        ]

    def finish(self):
        sends = jnp.concatenate(self.halve(), axis=-1)
        return jnp.concatenate(self.kept, axis=-1) + lax.ppermute(sends, "dp_1", SWAP)


class Gather:
    def __init__(self, weights, layer):
        x, z, core = (lax.axis_index(name) for name in RING_AXES)
        piece = (x * 4 + z) * 2 + core

        def rows_of(weight):
            rows = weight.shape[1] // 32
            return lax.dynamic_slice_in_dim(weight[layer], piece * rows, rows, 0).astype(F32)

        *inputs, output = (rows_of(weight) for weight in weights)
        self.piece = jnp.concatenate([jnp.concatenate(inputs, axis=1), output], axis=0)
        orders = [*EXPERT_ORDERS, *(swapped(order) for order in EXPERT_ORDERS)]
        places = [ring_place(order, x, z) for order in orders]
        self.places = jnp.stack([*places, core]).astype(jnp.int32)

        self.crossed = exchange(self.piece)

    def begin(self, after, received):
        held, *_ = behind([self.crossed], after)
        for step in (3, 2):
            moved = lax.ppermute(held, RING_AXES, ring_pairs(EXPERT_ORDERS, step))
            held = jnp.concatenate([held, moved], axis=0)
        half = held.shape[1] // 2
        self.held = behind([held[:, :half], held[:, half:]], received)
        self.moved = self.moves(self.held, 1)

    def moves(self, held, step):
        return [
            lax.ppermute(half, RING_AXES, ring_pairs(EXPERT_ORDERS, at))
            for half, at in zip(held, (step, 1 - step))
        ]

    def finish(self, after):
        held = behind(self.held, after)
        held = [jnp.concatenate(pair, axis=0) for pair in zip(held, self.moved)]
        near = [*held, *self.moves(held, 0)]
        return [self.places, *near, *(lax.ppermute(half, "dp_3", SWAP) for half in near)]


def behind(arrays, *after):
    return pl.pallas_call(
        lambda *refs: None,
        in_specs=[ANYWHERE] * (len(arrays) + len(after)),
        out_specs=[ANYWHERE] * len(arrays),
        out_shape=[jax.ShapeDtypeStruct(array.shape, array.dtype) for array in arrays],
        input_output_aliases={at: at for at in range(len(arrays))},
        name="behind",
    )(*arrays, *after)


def rope_tables(length):
    half = HEAD_SIZE // 2
    frequency = np.float32(THETA) ** (-2.0 * np.arange(half, dtype=np.float32) / HEAD_SIZE)
    angles = np.arange(length, dtype=np.float32)[:, None] * frequency[None].astype(np.float32)
    angles = angles.astype(np.float32)
    cosine = np.tile(np.cos(angles), (1, LANES // half)).astype(np.float32)
    sine = np.sin(angles)
    sine = np.tile(np.concatenate([-sine, sine], axis=1), (1, LANES // HEAD_SIZE))
    return jnp.asarray(cosine), jnp.asarray(sine.astype(np.float32))


def shards(
    tokens, segments, routes, norm_attention, query_weight, key_matrix, value_matrix,
    output_weight, norm_experts, router_weight, gate_weight, up_weight, down_weight, cotangent,
):
    length, features = tokens.shape
    experts = gate_weight.shape[1]
    hidden = gate_weight.shape[3]
    tables = rope_tables(length)
    segment = (segments.reshape(1, length), segments.reshape(length, 1))
    gain_attention = norm_attention[:, None, :]
    gain_experts = norm_experts[:, None, :]
    router = jnp.pad(router_weight, ((0, 0), (0, 0), (0, LANES - experts)))
    router_rows = jnp.pad(
        jnp.swapaxes(router_weight, 1, 2).astype(F32), ((0, 0), (0, 8 - experts), (0, 0))
    )
    mask = jnp.any(
        routes[..., None] == jnp.arange(LANES, dtype=jnp.int32), axis=2
    ).astype(F32)
    x_at, y_at, z_at = (lax.axis_index(name) for name in DP[:3])
    core = lax.axis_index("dp_3")

    def places_in(orders):
        found = []
        for which in (orders, [crossed(order) for order in orders]):
            one, two = (place(order, x_at, y_at, z_at) for order in which)
            found += [jnp.where(core == 0, one, two), jnp.where(core == 0, two, one)]
        return jnp.stack([*found, core]).astype(jnp.int32)

    expert_places = places_in(EXPERT_ORDERS)
    late_orders = tuple(swapped(order) for order in ATTENTION_ORDERS)

    attention_weights = (gain_attention, query_weight, key_matrix, value_matrix, output_weight)
    expert_weights = (gate_weight, up_weight, down_weight)
    back_weights = (
        gain_experts, router_rows, output_weight, query_weight, key_matrix, value_matrix,
    )

    others = Gather(attention_weights[1:], 1)
    x1, *saved1, part = attention_forward(0, [tokens], attention_weights, tables, segment)
    other = exchange(part)
    others.begin(part, other)
    middle1, xi1, share1, gate1, linear1, part = expert_forward(
        0, x1, part, other, gain_experts, router, mask, *expert_weights
    )
    x2, *saved2, part, q_other, kk_other, vv_other, part_other, weights_other = attention_forward(
        1, [middle1, part, exchange(part)], attention_weights, tables, segment,
        others.finish(part),
    )
    middle2, xi2, share2, last, back, gate_grad, keep, send = expert_both(
        1, expert_places, x2, part, part_other, gain_experts, router, mask, *expert_weights,
        cotangent,
    )
    both_orders = (EXPERT_ORDERS, tuple(crossed(order) for order in EXPERT_ORDERS))
    sum_e2 = Scatter(keep, send, *both_orders)
    other, gate_other = exchange(back), exchange(gate_grad)
    *sends, last = behind([*sum_e2.halve(), last], other)
    sum_e2.move(sends)
    last_other = exchange(last)
    no_gain = jnp.zeros((8, features), F32)
    g2, part, keep, send, part_other = attention_backward(
        1, late_orders, places_in(late_orders), cotangent, back, other, gate_grad, gate_other,
        (middle2, xi2, share2), back_weights, (x2, *saved2), tables, segment, no_gain, sends,
        (q_other, kk_other, vv_other, weights_other),
    )
    sum_a2 = Scatter(keep, send, late_orders)
    sends = sum_e2.halve()
    g1, late_gain, back, keep, send = expert_backward(
        0, expert_places, g2, x2, gain_attention, part, part_other, xi1, share1, gate1,
        linear1, *expert_weights, [*sends, last_other],
    )
    sum_e2.move(sends)
    sum_e1 = Scatter(keep, send, *both_orders)
    other = exchange(back)
    sends_a, sends_e = sum_a2.halve(), sum_e1.halve()
    sum_a2.move(sends_a)
    sum_e1.move(sends_e)
    sends = sends_a + sends_e + sum_e2.received()
    g0, part, keep, send = attention_backward(
        0, late_orders, places_in(late_orders), g1, back, other, back, other,
        (middle1, xi1, share1), back_weights, (x1, *saved1), tables, segment, late_gain,
        sends,
    )
    (send,) = behind([send], *sum_a2.received(), *sum_e1.received())
    sum_a1 = Scatter(keep, send, late_orders)
    sum_e1.advance()
    sum_a1.advance()
    sum_a2.advance()
    sends = sum_a1.halve()
    sum_a1.move(sends)
    sum_e1.hold(*sends)
    sum_a1.join(sum_a2)
    sends = sum_a1.halve()
    sum_a1.move(sends)
    sum_e1.join(sum_e2)
    sum_e1.advance()
    sum_e1.hold(*sends)
    sum_e1.advance()
    (other,) = behind([exchange(part)], *sum_e1.received())
    sum_a1.advance()
    gain = norm_attention[0].astype(F32)
    change, _ = norm_back(x1, row_factor(x1), gain, part + other)
    gradient = g0 + change
    output = (middle2 + (last + last_other)).astype(BF16)
    blocks = [one.finish() for one in (sum_a1, sum_e1)]

    attention_sums, expert_sums = blocks
    rows = attention_sums.shape[0]
    layers = query_weight.shape[0]
    attention_sums = jnp.swapaxes(attention_sums.reshape(rows, layers, -1), 0, 1)
    bounds = np.cumsum(
        [0, SMALL, query_weight.shape[2], key_matrix.shape[2], value_matrix.shape[2],
         output_weight.shape[1]]
    )
    attention_sums = [attention_sums[..., a:b] for a, b in zip(bounds[:-1], bounds[1:])]
    expert_sums = expert_sums.reshape(rows, 2, layers, experts // 2, 3, hidden)
    expert_sums = [
        expert_sums[..., kind, :].transpose(2, 1, 3, 0, 4).reshape(layers, experts, rows, hidden)
        for kind in range(3)
    ]
    small = attention_sums[0]
    attention_gain = small[:, :, 5]
    attention_gain = attention_gain + exchange(attention_gain)
    return (
        output,
        gradient,
        attention_gain,
        *attention_sums[1:4],
        jnp.swapaxes(attention_sums[4], 1, 2),
        small[:, :, 4],
        small[:, :, :experts],
        expert_sums[0],
        expert_sums[1],
        jnp.swapaxes(expert_sums[2], 2, 3),
    )


def solution(mesh):
    torus = Mesh(
        mesh.devices.reshape(*DP_SIZES, mesh.shape["tensor"]), (*DP, "tensor")
    )
    rows, copied, last = P(DP, None), P(), P(None, None, "tensor")
    in_specs = (
        rows, rows, P(None, DP, None), copied, last, last, last, P(None, "tensor", None),
        copied, copied, P(None, None, None, "tensor"), P(None, None, None, "tensor"),
        P(None, None, "tensor", None), rows,
    )
    out_specs = (
        rows, rows, P(None, DP), P(None, DP, "tensor"), P(None, DP, "tensor"),
        P(None, DP, "tensor"), P(None, "tensor", DP), P(None, DP), P(None, DP, None),
        P(None, None, DP, "tensor"), P(None, None, DP, "tensor"), P(None, None, "tensor", DP),
    )
    return jax.shard_map(
        shards, mesh=torus, in_specs=in_specs, out_specs=out_specs, check_vma=False
    )
```
